32 devices in a mesh: rows: 8 (over z, x), band: 4 (over y, core).
Axes of the slice: x: 2, y: 2, z: 4, core: 2. Of those that a mesh axis runs over, the one named last changes fastest.
Arguments:
- latents: float32 [32, 1024, 16], P('rows', 'band'), may hold values from -6 to 6
- gauss_noise: float32 [32, 1024, 16], P('rows', 'band'), may hold values from -6 to 6
- image_counts: int32 [32], P('rows'), may hold values from 1 to 4, as said below
- timesteps: int32 [32, 4], P('rows'), may hold values from 1 to 999
- labels: int32 [32, 4], P('rows'), may hold values from 0 to 1000
- wide_weights: float32 [1152, 17280], P(('rows', 'band')), may hold values from -0.1875 to 0.1875
- square_weights: float32 [1152, 2304], P(('rows', 'band')), may hold values from -0.25 to 0.25
- down_weights: float32 [4608, 1152], P(('rows', 'band')), may hold values from -0.09375 to 0.09375
- embed_tables: float32 [1273, 1152], P(None, ('rows', 'band')), may hold values from -2 to 2
- all_biases: float32 [19, 1152], P(None, ('rows', 'band')), may hold values from -1.75 to 1.75
- head_weights: float32 [1153, 32], replicated, may hold values from -0.1875 to 0.1875
- first_wide: float32 [1152, 17280], P(('rows', 'band')), may hold values from -1.335144e-05 to 1.335144e-05
- first_square: float32 [1152, 2304], P(('rows', 'band')), may hold values from -1.335144e-05 to 1.335144e-05
- first_down: float32 [4608, 1152], P(('rows', 'band')), may hold values from -1.335144e-05 to 1.335144e-05
- first_tables: float32 [1273, 1152], P(None, ('rows', 'band')), may hold values from -1.335144e-05 to 1.335144e-05
- first_biases: float32 [19, 1152], P(None, ('rows', 'band')), may hold values from -6.1035156e-05 to 6.1035156e-05
- first_head: float32 [1153, 32], replicated, may hold values from -6.1035156e-05 to 6.1035156e-05
- second_wide: float32 [1152, 17280], P(('rows', 'band')), may hold values from 3.7676023e-13 to 1.5070409e-12
- second_square: float32 [1152, 2304], P(('rows', 'band')), may hold values from 3.7676023e-13 to 1.5070409e-12
- second_down: float32 [4608, 1152], P(('rows', 'band')), may hold values from 3.7676023e-13 to 1.5070409e-12
- second_tables: float32 [1273, 1152], P(None, ('rows', 'band')), may hold values from 3.7676023e-13 to 1.5070409e-12
- second_biases: float32 [19, 1152], P(None, ('rows', 'band')), may hold values from 9.4190055e-12 to 3.7676022e-11
- second_head: float32 [1153, 32], replicated, may hold values from 9.4190055e-12 to 3.7676022e-11
Outputs:
- new_wide: float32 [1152, 17280], P(('rows', 'band'))
- new_square: float32 [1152, 2304], P(('rows', 'band'))
- new_down: float32 [4608, 1152], P(('rows', 'band'))
- new_tables: float32 [1273, 1152], P(None, ('rows', 'band'))
- new_biases: float32 [19, 1152], P(None, ('rows', 'band'))
- new_head: float32 [1153, 32], replicated
- next_first_wide: float32 [1152, 17280], P(('rows', 'band'))
- next_first_square: float32 [1152, 2304], P(('rows', 'band'))
- next_first_down: float32 [4608, 1152], P(('rows', 'band'))
- next_first_tables: float32 [1273, 1152], P(None, ('rows', 'band'))
- next_first_biases: float32 [19, 1152], P(None, ('rows', 'band'))
- next_first_head: float32 [1153, 32], replicated
- next_second_wide: float32 [1152, 17280], P(('rows', 'band'))
- next_second_square: float32 [1152, 2304], P(('rows', 'band'))
- next_second_down: float32 [4608, 1152], P(('rows', 'band'))
- next_second_tables: float32 [1273, 1152], P(None, ('rows', 'band'))
- next_second_biases: float32 [19, 1152], P(None, ('rows', 'band'))
- next_second_head: float32 [1153, 32], replicated
- half_wide: bfloat16 [1152, 17280], P(('rows', 'band'))
- half_square: bfloat16 [1152, 2304], P(('rows', 'band'))
- half_down: bfloat16 [4608, 1152], P(('rows', 'band'))
- half_tables: bfloat16 [1273, 1152], P(None, ('rows', 'band'))
- half_biases: bfloat16 [19, 1152], P(None, ('rows', 'band'))
- half_head: bfloat16 [1153, 32], replicated
- grad_norm: float32 [], replicated
- loss_sum: float32 [], replicated
- image_total: float32 [], replicated
The draws below stay inside these ranges and needn't reach their ends.
Inputs may be any that keep to these rules, and one draw needn't show every extreme that they name: `image_counts`: each row holds 1 or 4 images; among the 4 rows of one index of rows at least one holds 1.
All inputs are finite; a program needn't handle non-finite values.
Results may differ from the reference program's by a relative error of at most 0.0074.
Values may be sent and summed in bfloat16 or wider, within the bound.
A program may use at most 448 MiB of HBM per device.

```python
import math
import jax
import jax.numpy as jnp
from jax import lax

D = 1152
FF = 4608
HEADS = 16
CLASSES = 1001
FREQ = 256
PATCH_IN = 16
OUT = 32
GRID = 32
SLOTS = 4
TIMESTEPS = 1000
STEP = 10
BIAS_ROWS = 19
ROWS_DEV = 4
PATCHES = 1024
ROWS = 32
HEAD_DIM = 72
TABLE_ROWS = 1273


def draw_image_counts(key, part):
    key = jax.random.fold_in(key, 11)
    jitter_key, offset_key = jax.random.split(key, 2)
    blocks = ROWS // ROWS_DEV
    block_index = jnp.arange(blocks, dtype=jnp.int32)
    base_packed = block_index * ROWS_DEV // (blocks - 1)
    jitter = jax.random.randint(jitter_key, (blocks,), 0, 2)
    packed_count = jnp.where(block_index == 0, 0, jnp.clip(base_packed - jitter, 0, ROWS_DEV - 1))
    offset_at = jax.random.randint(offset_key, (blocks,), 0, ROWS_DEV)
    in_block = jnp.arange(ROWS, dtype=jnp.int32) % ROWS_DEV
    rank = (in_block + jnp.repeat(offset_at, ROWS_DEV)) % ROWS_DEV
    flags = (rank < jnp.repeat(packed_count, ROWS_DEV)).astype(jnp.int32)
    return (1 + 3 * flags).astype(jnp.int32)


def draw_embed_tables(key, part):
    key = jax.random.fold_in(key, 12)
    values = jnp.clip(jax.random.normal(key, (TABLE_ROWS, D), jnp.float32), -4.0, 4.0)
    row_index = jnp.arange(TABLE_ROWS)
    row_scale = jnp.where(row_index < FREQ, FREQ ** (-0.5), jnp.where(row_index < FREQ + PATCH_IN, PATCH_IN ** (-0.5), 0.5))
    return values * row_scale[:, None]


def with_ends(entries, stream_key, smallest, largest):
    dims = entries.shape
    spot = [jax.random.randint(jax.random.fold_in(stream_key, axis), (), 0, dims[axis]) for axis in range(len(dims))]
    entries = entries.at[tuple(spot)].set(smallest)
    longest = dims.index(max(dims))
    spot[longest] = (spot[longest] + 1) % dims[longest]
    return entries.at[tuple(spot)].set(largest)


def shard_levels(key, extent, cuts, smallest, largest):
    gain = 1.0
    for dim, blocks in cuts:
        heights = jax.random.uniform(jax.random.fold_in(jax.random.fold_in(key, 6), dim), (blocks,), jnp.float32, smallest / len(cuts), largest / len(cuts))
        gain = gain * jnp.repeat(jnp.exp(heights), extent[dim] // blocks).reshape((-1,) + (1,) * (len(extent) - 1 - dim))
    return gain


def gaussian(own_key, dims, width, most, cuts=(), kind=jnp.bfloat16):
    array = jax.random.normal(own_key, dims, jnp.float32) * width
    if len(cuts) > 0:
        array = shard_levels(own_key, dims, cuts, -0.22, 0.18) * array
    return jnp.clip(array, min=-most, max=most).astype(kind)


def setup_inputs(seed: int = 0) -> dict:
    splits = jax.random.split(jax.random.key(seed), 24)
    return {
        "latents": gaussian(splits[0], (ROWS, PATCHES, PATCH_IN), 1.0, 6.0, ((0, 8), (1, 4)), jnp.float32),
        "gauss_noise": gaussian(splits[1], (ROWS, PATCHES, PATCH_IN), 1.0, 6.0, ((0, 8), (1, 4)), jnp.float32),
        "image_counts": draw_image_counts(jax.random.fold_in(splits[23], 71), 0),
        "timesteps": with_ends(jax.random.randint(splits[3], (ROWS, SLOTS), 1, TIMESTEPS), jax.random.fold_in(splits[3], 1), 1, TIMESTEPS - 1).astype(jnp.int32),
        "labels": with_ends(jax.random.randint(splits[4], (ROWS, SLOTS), 0, CLASSES), jax.random.fold_in(splits[4], 1), 0, CLASSES - 1).astype(jnp.int32),
        "wide_weights": gaussian(splits[5], (D, 11 * D + FF), D ** -0.5, 0.1875, ((0, 32),), jnp.float32),
        "square_weights": gaussian(splits[6], (D, 2 * D), (D // 2) ** -0.5, 0.25, ((0, 32),), jnp.float32),
        "down_weights": gaussian(splits[7], (FF, D), FF ** -0.5, 0.09375, ((0, 32),), jnp.float32),
        "embed_tables": draw_embed_tables(jax.random.fold_in(splits[23], 71), 0),
        "all_biases": gaussian(splits[9], (BIAS_ROWS, D), 0.3, 1.75, ((1, 32),), jnp.float32),
        "head_weights": gaussian(splits[10], (D + 1, OUT), D ** -0.5, 0.1875, (), jnp.float32),
        "first_wide": gaussian(splits[11], (D, 11 * D + FF), (0.011 * (20 * D * D) ** -0.5), 1.33514404296875e-05, ((0, 32),), jnp.float32),
        "first_square": gaussian(splits[12], (D, 2 * D), (0.011 * (20 * D * D) ** -0.5), 1.33514404296875e-05, ((0, 32),), jnp.float32),
        "first_down": gaussian(splits[13], (FF, D), (0.011 * (20 * D * D) ** -0.5), 1.33514404296875e-05, ((0, 32),), jnp.float32),
        "first_tables": gaussian(splits[14], (TABLE_ROWS, D), (0.011 * (20 * D * D) ** -0.5), 1.33514404296875e-05, ((1, 32),), jnp.float32),
        "first_biases": gaussian(splits[15], (BIAS_ROWS, D), (0.055 * (20 * D * D) ** -0.5), 6.103515625e-05, ((1, 32),), jnp.float32),
        "first_head": gaussian(splits[16], (D + 1, OUT), (0.055 * (20 * D * D) ** -0.5), 6.103515625e-05, (), jnp.float32),
        "second_wide": jnp.clip(jnp.exp(math.log(1.507040911334634e-12) - 1.3862944 * jax.random.uniform(splits[17], (D, 11 * D + FF), jnp.float32) ** shard_levels(splits[17], (D, 11 * D + FF), ((0, 32),), -0.2, 0.2)), 3.767602278336585e-13, 1.507040911334634e-12),
        "second_square": jnp.clip(jnp.exp(math.log(1.507040911334634e-12) - 1.3862944 * jax.random.uniform(splits[18], (D, 2 * D), jnp.float32) ** shard_levels(splits[18], (D, 2 * D), ((0, 32),), -0.2, 0.2)), 3.767602278336585e-13, 1.507040911334634e-12),
        "second_down": jnp.clip(jnp.exp(math.log(1.507040911334634e-12) - 1.3862944 * jax.random.uniform(splits[19], (FF, D), jnp.float32) ** shard_levels(splits[19], (FF, D), ((0, 32),), -0.2, 0.2)), 3.767602278336585e-13, 1.507040911334634e-12),
        "second_tables": jnp.clip(jnp.exp(math.log(1.507040911334634e-12) - 1.3862944 * jax.random.uniform(splits[20], (TABLE_ROWS, D), jnp.float32) ** shard_levels(splits[20], (TABLE_ROWS, D), ((1, 32),), -0.2, 0.2)), 3.767602278336585e-13, 1.507040911334634e-12),
        "second_biases": jnp.clip(jnp.exp(math.log(3.767602202442433e-11) - 1.3862944 * jax.random.uniform(splits[21], (BIAS_ROWS, D), jnp.float32) ** shard_levels(splits[21], (BIAS_ROWS, D), ((1, 32),), -0.2, 0.2)), 9.419005506106082e-12, 3.767602202442433e-11),
        "second_head": jnp.clip(jnp.exp(jax.random.uniform(splits[22], (D + 1, OUT), jnp.float32, math.log(9.419005506106082e-12), math.log(3.767602202442433e-11))), 9.419005506106082e-12, 3.767602202442433e-11),
    }


HIGHEST = lax.Precision.HIGHEST
BETA_LOW = 0.0001
BETA_HIGH = 0.02
NORM_EPS = 1e-06
CLIP_NORM = 0.1
DECAY_FIRST = 0.9
DECAY_SECOND = 0.999
ADAM_EPS = 1e-08
LEARN_RATES = (0.1, 0.1, 0.05, 0.2, 0.3, 0.1)

@jax.custom_vjp
def low(v):
    return lax.optimization_barrier(v.astype(jnp.bfloat16)).astype(jnp.float32)

@jax.custom_vjp
def low_back(v):
    return v

def low_keep(v):
    return (low(v), None)

def low_pass(kept, grad):
    return (grad,)

def back_keep(v):
    return (v, None)

def back_low(kept, grad):
    return (low(grad),)
low.defvjp(low_keep, low_pass)
low_back.defvjp(back_keep, back_low)

def matmul(operand, weights):
    return jnp.einsum('...i,ij->...j', operand, weights, precision=HIGHEST)

def spread(slot_hot, per_slot):
    return jnp.einsum('rns,rsk->rnk', slot_hot, per_slot, precision=HIGHEST)

def plan(time_steps):
    steps_all = jnp.arange(TIMESTEPS, dtype=jnp.int32)
    betas = BETA_LOW + (BETA_HIGH - BETA_LOW) * steps_all.astype(jnp.float32) / (TIMESTEPS - 1)
    cumulate = jnp.cumsum(jnp.log1p(-betas))
    pick_now = (time_steps[..., None] == steps_all).astype(jnp.float32)
    pick_prev = (time_steps[..., None] - 1 == steps_all).astype(jnp.float32)
    return jnp.stack([lax.optimization_barrier(jnp.sum(pick_now * betas, axis=-1)), lax.optimization_barrier(jnp.sum(pick_now * cumulate, axis=-1)), lax.optimization_barrier(jnp.sum(pick_prev * cumulate, axis=-1))], axis=-1)

def time_features(time_steps):
    half_width = FREQ // 2
    frequency = jnp.exp(-math.log(10000.0) * jnp.arange(half_width).astype(jnp.float32) / half_width)
    angles = time_steps.astype(jnp.float32)[..., None] * frequency
    return jnp.concatenate([jnp.cos(angles), jnp.sin(angles)], axis=-1)

def positions(place_at, counts):
    four_way = counts == SLOTS
    segment = jnp.where(four_way, place_at // (PATCHES // SLOTS), 0)
    local_index = place_at - segment * (PATCHES // SLOTS)
    grid_side = jnp.where(four_way, GRID // 2, GRID)
    row_coord = (local_index // grid_side).astype(jnp.float32)
    col_coord = (local_index % grid_side).astype(jnp.float32)
    quarter = D // 4
    omegas = jnp.exp(-math.log(10000.0) * jnp.arange(quarter).astype(jnp.float32) / quarter)
    along_row = row_coord[..., None] * omegas
    along_col = col_coord[..., None] * omegas
    return (jnp.concatenate([jnp.sin(along_row), jnp.cos(along_row), jnp.sin(along_col), jnp.cos(along_col)], axis=-1), segment)

def layer_norm(values):
    centered = values - lax.optimization_barrier(jnp.mean(values, axis=-1, keepdims=True))
    return centered * lax.rsqrt(lax.optimization_barrier(jnp.mean(centered * centered, axis=-1, keepdims=True)) + NORM_EPS)

def modulate(values, shift, scaling):
    return layer_norm(values) * (1.0 + scaling) + shift

def patch_loss(output, target_noise, patch_sched):
    beta = patch_sched[..., 0:1]
    log_now = patch_sched[..., 1:2]
    log_prev = patch_sched[..., 2:3]
    error = output[..., :PATCH_IN] - target_noise
    log_beta = jnp.log(beta)
    keep_now = -jnp.expm1(log_now)
    log_post = log_beta + jnp.log(-jnp.expm1(log_prev)) - jnp.log(keep_now)
    coefficient = beta * lax.rsqrt(keep_now * (1.0 - beta))
    fraction = 0.5 * (output[..., PATCH_IN:] + 1.0)
    log_model = fraction * log_beta + (1.0 - fraction) * log_post
    diverge = 0.5 * (-1.0 + log_model - log_post + jnp.exp(log_post - log_model) + (coefficient * error) ** 2 * jnp.exp(-log_model))
    return lax.optimization_barrier(jnp.mean(error * error, axis=-1)) + lax.optimization_barrier(jnp.mean(diverge, axis=-1)) / math.log(2.0)

def unpack(wide_part, square_part, down_part, table_part, bias_part):
    triple, upward, adaptive, final_adaptive = jnp.split(wide_part, [3 * D, 3 * D + FF, 9 * D + FF], axis=1)
    output_proj, time_out = jnp.split(square_part, 2, axis=1)
    return dict(triple=triple, upward=upward, adaptive=adaptive, final_adaptive=final_adaptive, output_proj=output_proj, time_out=time_out, downward=down_part, time_in=table_part[:FREQ], patch_in=table_part[FREQ:FREQ + PATCH_IN], class_rows=table_part[FREQ + PATCH_IN:], bias_patch=bias_part[0], bias_time_in=bias_part[1], bias_time_out=bias_part[2], bias_adaptive=bias_part[3:9].reshape(-1), bias_query=bias_part[9], bias_value=bias_part[10], bias_output=bias_part[11], bias_upward=bias_part[12:16].reshape(-1), bias_downward=bias_part[16], bias_final=bias_part[17:19].reshape(-1))

def attend_row(pieces):
    query_row, key_row, value_row, segment = pieces
    query_heads = query_row.reshape(PATCHES, HEADS, HEAD_DIM)
    key_heads = key_row.reshape(PATCHES, HEADS, HEAD_DIM)
    value_heads = value_row.reshape(PATCHES, HEADS, HEAD_DIM)
    scores = low_back(jnp.einsum('qhd,khd->hqk', query_heads, key_heads, precision=HIGHEST) * HEAD_DIM ** (-0.5))
    same_image = (segment[:, None] == segment[None, :])[None]
    attention_weights = jax.nn.softmax(jnp.where(same_image, scores, -1e+30), axis=-1)
    mixture = jnp.einsum('hqk,khd->qhd', low(attention_weights), value_heads, precision=HIGHEST)
    return low(low_back(mixture.reshape(PATCHES, D)))

def row_block_loss(pieces_map, head_low, row_block):
    block_latents, block_noise, block_counts, block_mods, block_final, block_sched = row_block
    place_at = jnp.arange(PATCHES, dtype=jnp.int32)[None, :]
    position, segment = positions(place_at, block_counts[:, None])
    slot_hot = (segment[..., None] == jnp.arange(SLOTS, dtype=jnp.int32)).astype(jnp.float32)
    patch_mods = spread(slot_hot, block_mods)
    patch_final = spread(slot_hot, block_final)
    patch_sched = spread(slot_hot, block_sched)
    shift_one, scale_one, gate_one, shift_two, scale_two, gate_two = jnp.split(patch_mods, 6, axis=-1)
    final_shift, final_scale = jnp.split(patch_final, 2, axis=-1)
    log_now = patch_sched[..., 1:2]
    noisy = low(jnp.exp(0.5 * log_now) * block_latents + jnp.sqrt(-jnp.expm1(log_now)) * block_noise)
    hidden_zero = low_back(matmul(noisy, pieces_map['patch_in']) + pieces_map['bias_patch'] + position)
    normed_one = low(modulate(hidden_zero, shift_one, scale_one))
    query_bias = pieces_map['bias_query']
    triple_bias = jnp.concatenate([query_bias, jnp.zeros_like(query_bias), pieces_map['bias_value']])
    projected = low(low_back(matmul(normed_one, pieces_map['triple']) + triple_bias))
    queries, key_rows, value_rows = jnp.split(projected, 3, axis=-1)
    attended = lax.map(jax.checkpoint(attend_row), (queries, key_rows, value_rows, segment))
    hidden_one = hidden_zero + gate_one * low_back(matmul(attended, pieces_map['output_proj']) + pieces_map['bias_output'])
    normed_two = low(modulate(hidden_one, shift_two, scale_two))
    upward = low_back(matmul(normed_two, pieces_map['upward']) + pieces_map['bias_upward'])
    active = low(jax.nn.gelu(upward, approximate=True))
    hidden_two = hidden_one + gate_two * low_back(matmul(active, pieces_map['downward']) + pieces_map['bias_downward'])
    normed_out = low(modulate(hidden_two, final_shift, final_scale))
    output = low_back(matmul(normed_out, head_low[:D]) + head_low[D])
    patch_share = jnp.where(block_counts[:, None] == SLOTS, 1.0 / (PATCHES // SLOTS), 1.0 / PATCHES)
    return jnp.sum(patch_share * patch_loss(output, block_noise, patch_sched))

def total_loss(params, latents, gauss_noise, image_counts, timesteps, labels):
    wide_low, square_low, down_low, table_low, bias_low, head_low = [low(weight_array) for weight_array in params]
    pieces_map = unpack(wide_low, square_low, down_low, table_low, bias_low)
    sched_slots = plan(timesteps)
    frequency = low(time_features(timesteps))
    time_act = low(jax.nn.silu(low_back(matmul(frequency, pieces_map['time_in']) + pieces_map['bias_time_in'])))
    label_hot = (labels[..., None] == jnp.arange(CLASSES, dtype=jnp.int32)).astype(jnp.float32)
    condition = low_back(matmul(time_act, pieces_map['time_out']) + pieces_map['bias_time_out'] + matmul(label_hot, pieces_map['class_rows']))
    cond_act = low(jax.nn.silu(condition))
    modulation = low_back(matmul(cond_act, pieces_map['adaptive']) + pieces_map['bias_adaptive'])
    final_mods = low_back(matmul(cond_act, pieces_map['final_adaptive']) + pieces_map['bias_final'])
    row_blocks = tuple((stacked.reshape((ROWS // 4, 4) + stacked.shape[1:]) for stacked in (latents, gauss_noise, image_counts, modulation, final_mods, sched_slots)))

    def step_block(running, row_block):
        return (running + jax.checkpoint(row_block_loss)(pieces_map, head_low, row_block), None)
    loss_sum, _ = lax.scan(step_block, jnp.zeros((), jnp.float32), row_blocks)
    return loss_sum

def adamw_step(weight, first_old, second_old, gradient, step_rate):
    first_new = DECAY_FIRST * first_old + (1.0 - DECAY_FIRST) * gradient
    second_new = DECAY_SECOND * second_old + (1.0 - DECAY_SECOND) * gradient * gradient
    first_hat = first_new / (1.0 - DECAY_FIRST ** STEP)
    second_hat = second_new / (1.0 - DECAY_SECOND ** STEP)
    return (weight - step_rate * first_hat / (jnp.sqrt(second_hat) + ADAM_EPS), first_new, second_new)

def reference(latents, gauss_noise, image_counts, timesteps, labels, wide_weights, square_weights, down_weights, embed_tables, all_biases, head_weights, first_wide, first_square, first_down, first_tables, first_biases, first_head, second_wide, second_square, second_down, second_tables, second_biases, second_head):
    params = (wide_weights, square_weights, down_weights, embed_tables, all_biases, head_weights)
    firsts = (first_wide, first_square, first_down, first_tables, first_biases, first_head)
    seconds = (second_wide, second_square, second_down, second_tables, second_biases, second_head)
    image_total = jnp.sum(image_counts).astype(jnp.float32)

    def objective(weights_all):
        summed = total_loss(weights_all, latents, gauss_noise, image_counts, timesteps, labels)
        return (summed / image_total, summed)
    scaled, pull_back, loss_sum = jax.vjp(objective, params, has_aux=True)
    gradients = pull_back(jnp.ones_like(scaled))[0]
    grad_norm = jnp.sqrt(sum((jnp.sum(grad_part * grad_part) for grad_part in gradients)))
    clip_factor = jnp.minimum(1.0, CLIP_NORM / (grad_norm + 1e-06))
    results = [adamw_step(params[which], firsts[which], seconds[which], gradients[which] * clip_factor, LEARN_RATES[which]) for which in range(6)]
    return (results[0][0], results[1][0], results[2][0], results[3][0], results[4][0], results[5][0], results[0][1], results[1][1], results[2][1], results[3][1], results[4][1], results[5][1], results[0][2], results[1][2], results[2][2], results[3][2], results[4][2], results[5][2], results[0][0].astype(jnp.bfloat16), results[1][0].astype(jnp.bfloat16), results[2][0].astype(jnp.bfloat16), results[3][0].astype(jnp.bfloat16), results[4][0].astype(jnp.bfloat16), results[5][0].astype(jnp.bfloat16), grad_norm, loss_sum, image_total)
```

```python
import functools
import math

import jax
import jax.numpy as jnp
from jax import lax
from jax.experimental import pallas as pl
from jax.experimental.pallas import tpu as pltpu
from jax.sharding import PartitionSpec as P

D = 1152
FF = 4608
HEADS = 16
HEAD_DIM = D // HEADS
CLASSES = 1001
FREQ = 256
PATCH_IN = 16
GRID = 32
PATCHES = GRID * GRID
SLOTS = 4
SEGMENT = PATCHES // SLOTS
TIMESTEPS = 1000
STEP = 10

BETA_LOW = 0.0001
BETA_HIGH = 0.02
NORM_EPS = 1e-06
CLIP_NORM = 0.1
DECAY_FIRST = 0.9
DECAY_SECOND = 0.999
ADAM_EPS = 1e-08
LEARN_RATES = (0.1, 0.1, 0.05, 0.2, 0.3, 0.1)

AXES = ("rows", "band")
WINDOW = 256
SCALE = HEAD_DIM ** (-0.5)
NT = (((1,), (1,)), ((), ()))
TN = (((0,), (0,)), ((), ()))
NN = (((1,), (0,)), ((), ()))
BF16 = jnp.bfloat16
F32 = jnp.float32


def dot(left, right, dims):
    return lax.dot_general(left, right, dims, preferred_element_type=F32)


def head_window(head):
    start = jnp.minimum(head * HEAD_DIM // 128, (D - WINDOW) // 128) * 128
    return pl.multiple_of(start, 128), head * HEAD_DIM - start


def head_mask(rows, offset):
    lane = lax.broadcasted_iota(jnp.int32, (rows, WINDOW), 1)
    return (lane >= offset) & (lane < offset + HEAD_DIM)


def attend_head(head, apart, q_ref, k_ref, v_ref, out_ref, log_ref, q_block):
    q_len, k_len = q_ref.shape[0], k_ref.shape[0]
    start, offset = head_window(head)
    window = pl.ds(start, WINDOW)
    for at in range(0, q_len, q_block):
        rows = pl.ds(at, q_block)
        mask = head_mask(q_block, offset)
        query = jnp.where(mask, q_ref[rows, window], 0).astype(BF16)
        scores = jnp.concatenate(
            [
                dot(k_ref[pl.ds(k_at, SEGMENT), window], query, NT)
                + apart[pl.ds(k_at // SEGMENT, 1), rows]
                for k_at in range(0, k_len, SEGMENT)
            ],
            axis=0,
        )
        top = jnp.max(scores, axis=0, keepdims=True)
        weights = jnp.exp((scores - top) * SCALE)
        total = jnp.sum(weights, axis=0, keepdims=True)
        weights = (weights * (1.0 / total)).astype(BF16)
        mixed = dot(weights, v_ref[:, window], TN).astype(BF16)
        out_ref[rows, window] = jnp.where(mask, mixed, out_ref[rows, window])
        log_ref[pl.ds(head, 1), rows] = top * SCALE + jnp.log(total)


def attend_back_head(
    head, apart, q_ref, k_ref, v_ref, grad_ref, log_ref, dq_ref, dk_ref, dv_ref
):
    q_len, k_len = q_ref.shape[0], k_ref.shape[0]
    start, offset = head_window(head)
    window = pl.ds(start, WINDOW)
    mask = head_mask(q_len, offset)
    query = jnp.where(mask, q_ref[:, window], 0).astype(BF16)
    grad = jnp.where(mask, grad_ref[:, window], 0).astype(BF16)
    key = k_ref[:, window]
    log_total = log_ref[pl.ds(head, 1), :]
    probs = jnp.concatenate(
        [
            jnp.exp(
                dot(k_ref[pl.ds(k_at, SEGMENT), window], query, NT) * SCALE
                + (apart[pl.ds(k_at // SEGMENT, 1), :] - log_total)
            )
            for k_at in range(0, k_len, SEGMENT)
        ],
        axis=0,
    )
    both = probs * dot(v_ref[:, window], grad, NT)
    inner = jnp.sum(both, axis=0, keepdims=True)
    grad_scores = (both - probs * inner).astype(BF16)
    grad_value = dot(probs.astype(BF16), grad, NN)
    grad_key = dot(grad_scores, query, NN) * SCALE
    grad_query = (dot(grad_scores, key, TN) * SCALE).astype(BF16)
    dq_ref[:, window] = jnp.where(mask, grad_query, dq_ref[:, window])
    mask = head_mask(k_len, offset)
    dk_ref[:, window] = jnp.where(mask, grad_key.astype(BF16), dk_ref[:, window])
    dv_ref[:, window] = jnp.where(mask, grad_value.astype(BF16), dv_ref[:, window])


def whole_block(shape):
    return pl.BlockSpec(shape, lambda step: (0,) * len(shape))


def at_step(head, step, do):
    pl.when(head == step)(do)


MESH_ID = pl.DeviceIdType.MESH
BLOCK = 144
LINE = 4
SPLIT = (80, 64, 80)
ROWS_AXIS = 8
DEVICES = 32
OWN = D // DEVICES
PADDED = 48
PART = 384
OWNERS = 24
OWNER_OF = 7


class Place:
    def __init__(self):
        self.r, self.b = lax.axis_index("rows"), lax.axis_index("band")
        self.me = 4 * self.r + self.b
        self.z, self.x = self.r // 2, self.r % 2
        self.y, self.c = self.b // 2, self.b % 2
        self.other_x, self.other_b = 1 - self.x, self.b + 2 - 4 * self.y
        self.across_x = (self.r + 1 - 2 * self.x, self.b)
        self.across_y = (self.r, self.other_b)
        self.sibling = (self.r, self.b + 1 - 2 * self.c)
        self.right = (self.r + 2, self.b)
        self.left = (self.r - 2, self.b)

    def others(self, do):
        def step(i, carry):
            device = (self.me + i) % DEVICES
            do(device, (device // 4, device % 4))
            return carry

        lax.fori_loop(1, DEVICES, step, 0)

    def greet(self):
        barrier = pltpu.get_barrier_semaphore()
        self.others(
            lambda _, device: pl.semaphore_signal(
                barrier, inc=1, device_id=device, device_id_type=MESH_ID
            )
        )
        pl.semaphore_wait(barrier, DEVICES - 1)

    def each_source(self, do):
        do(self.z)
        for step in range(1, LINE):
            pl.when(self.z - step >= 0)(functools.partial(do, self.z - step))
            pl.when(self.z + step < LINE)(functools.partial(do, self.z + step))


def remote(source, target, send, receive, device):
    return pltpu.make_async_remote_copy(
        source, target, send, receive, device_id=device, device_id_type=MESH_ID
    )


class Spread:
    def __init__(self, at, place, own, rows, width, cut, dummy, sems):
        self.at, self.place, self.own = at, place, own
        self.rows, self.width, self.cut, self.dummy = rows, width, cut, dummy
        self.line_send, self.line_recv, self.sem = sems


    def block(self, r, b, start=0, size=None):
        return self.place(r, b, start, self.rows if size is None else size)

    def to_sibling(self, source, target):
        return remote(source, target, self.sem.at[3], self.sem.at[4], self.at.sibling)

    def to_x(self, source, target, slot):
        return remote(source, target, self.sem.at[1], self.sem.at[slot], self.at.across_x)

    def to_y(self, source, target, slot):
        return remote(source, target, self.sem.at[2], self.sem.at[slot], self.at.across_y)

    def line_copy(self, way, z, source=None):
        target = self.block(2 * z + self.at.x, self.at.b)
        return remote(
            target if source is None else source,
            target,
            self.line_send.at[way, z],
            self.line_recv.at[way, z],
            self.at.right if way == 0 else self.at.left,
        )

    def fan(self, z, source=None):
        target = self.block(2 * z + self.at.x, self.at.b)
        source = target if source is None else source
        self.to_x(source, target, 5 + z).start()
        self.to_y(source, target, 9 + z).start()
        self.to_sibling(source, target).start()

    def local(self):
        return pltpu.make_async_copy(self.own, self.block(self.at.r, self.at.b), self.sem.at[0])

    def open(self):
        at = self.at
        self.local().start()
        pl.when(at.z < LINE - 1)(lambda: self.line_copy(0, at.z, self.own).start())
        pl.when(at.z > 0)(lambda: self.line_copy(1, at.z, self.own).start())
        self.fan(at.z, self.own)

    def along_line(self, steps=(1, 2, 3)):
        at = self.at
        for step in steps:
            for way in (0, 1):
                z = at.z - step if way == 0 else at.z + step

                @pl.when(z >= 0 if way == 0 else z < LINE)
                def _(way=way, z=z):
                    copy = self.line_copy(way, z)
                    copy.wait_recv()
                    onward = at.z < LINE - 1 if way == 0 else at.z > 0
                    pl.when(onward)(lambda: copy.start())
                    self.fan(z)

    def around_square(self):
        at, cut = self.at, self.cut

        def do(z):
            ref = self.block(2 * z + at.other_x, at.b)
            self.to_x(ref, ref, 5 + z).wait_recv()
            part = self.block(2 * z + at.other_x, at.b, 0, cut)
            self.to_y(part, part, 17 + z).start()
            self.to_sibling(ref, ref).start()
            ref = self.block(2 * z + at.x, at.other_b)
            self.to_y(ref, ref, 9 + z).wait_recv()
            part = self.block(2 * z + at.x, at.other_b, cut, self.rows - cut)
            self.to_x(part, part, 13 + z).start()
            self.to_sibling(ref, ref).start()

        at.each_source(do)

    def close_square(self):
        at, cut = self.at, self.cut

        def do(z):
            part = self.block(2 * z + at.other_x, at.other_b, 0, cut)
            self.to_y(part, part, 17 + z).wait_recv()
            part = self.block(2 * z + at.other_x, at.other_b, cut, self.rows - cut)
            self.to_x(part, part, 13 + z).wait_recv()
            ref = self.block(2 * z + at.other_x, at.other_b)
            self.to_sibling(ref, ref).start()

        at.each_source(do)

    def counted(self, rows):
        if self.width >= 128:
            return self.dummy(rows, self.width)
        return self.dummy(rows * self.width // D, D)

    def arrive(self):
        self.local().wait()
        rows = self.counted(4 * LINE * self.rows)
        self.to_sibling(rows, rows).wait_recv()

    def finish(self):
        at, cut = self.at, self.cut
        pl.when(at.z < LINE - 1)(lambda: self.line_copy(0, at.z).wait_send())
        pl.when(at.z > 0)(lambda: self.line_copy(1, at.z).wait_send())
        for step in range(1, LINE):
            go = jnp.logical_and(at.z - step >= 0, at.z < LINE - 1)
            pl.when(go)(lambda: self.line_copy(0, at.z - step).wait_send())
            go = jnp.logical_and(at.z + step < LINE, at.z > 0)
            pl.when(go)(lambda: self.line_copy(1, at.z + step).wait_send())
        rows = self.counted(LINE * (2 * self.rows - cut))
        self.to_x(rows, rows, 5).wait_send()
        rows = self.counted(LINE * (self.rows + cut))
        self.to_y(rows, rows, 9).wait_send()
        rows = self.counted(4 * LINE * self.rows)
        self.to_sibling(rows, rows).wait_send()


def spread_sems(count):
    dma = pltpu.SemaphoreType.DMA
    return [dma((count, 2, LINE)), dma((count, 2, LINE)), dma((count, 21))]


def compact(target, pieces, first_row):
    for device in range(DEVICES):
        rows = pieces[device, first_row : first_row + PADDED, :].astype(F32)
        target[OWN * device : OWN * (device + 1), :] = rows[:OWN]


def loosen(target, rows):
    for device in range(DEVICES):
        own = rows[OWN * device : OWN * (device + 1), :]
        target[PADDED * device : PADDED * device + OWN, :] = own
        target[PADDED * device + OWN : PADDED * (device + 1), :] = jnp.zeros(
            (PADDED - OWN, rows.shape[1]), F32
        )


def gather_kernel(
    own,
    time_own,
    mods_own,
    features_own,
    labels_own,
    time_in,
    time_bias,
    classes,
    small_own,
    given_own,
    first,
    mods,
    condition_out,
    small_out,
    time_act_out,
    time_pre_out,
    features,
    labels,
    given,
    piece,
    pieces,
    time_weights,
    mods_weights,
    tall,
    loose,
    mods_part,
    given_send,
    given_recv,
    code_sems,
    mods_send,
    mods_recv,
    part_sems,
    line_send,
    line_recv,
    spread_sem,
):
    at = Place()
    at.greet()

    def rows_at(r, start, size):
        return pl.ds(pl.multiple_of(r * BLOCK + start, 16), size)

    def in_first(r, b, start, size):
        return first.at[b, rows_at(r, start, size)]

    def in_time(r, b, start, size):
        return time_weights.at[pl.ds(pl.multiple_of((4 * r + b) * PADDED + start, 16), size)]

    def in_pieces(r, b, start, size):
        return pieces.at[4 * r + b, pl.ds(start, size)]

    def spread(index, place, source, rows, width, cut):
        sems = line_send.at[index], line_recv.at[index], spread_sem.at[index]
        return Spread(at, place, source, rows, width, cut, bytes_of, sems)

    def bytes_of(rows, width):
        if rows <= D:
            return first.at[0, pl.ds(0, rows), pl.ds(0, width)]
        return first.at[:, pl.ds(0, rows // 4), pl.ds(0, width)]

    of_first = spread(0, in_first, own, BLOCK, D, SPLIT[0])
    of_time = spread(1, in_time, time_own, PADDED, D, 16)
    of_piece = spread(2, in_pieces, piece, BLOCK, 128, SPLIT[0])

    def code_copies(i):
        r = (at.r + i) % ROWS_AXIS
        mine = pl.ds(pl.multiple_of(at.r * 16, 16), 16)
        device = (r, at.b)
        return (
            remote(features_own, features.at[mine], code_sems.at[0, i], code_sems.at[1, i], device),
            remote(labels_own, labels.at[mine], code_sems.at[2, i], code_sems.at[3, i], device),
        )

    for i in range(1, ROWS_AXIS):
        for copy in code_copies(i):
            copy.start()
    mine = pl.ds(pl.multiple_of(at.r * 16, 16), 16)
    features[mine, :] = features_own[...]
    labels[mine, :] = labels_own[...]
    of_time.open()

    patches = given_own.shape[2]

    def given_copy(i):
        b = (at.b + i) % 4
        columns = pl.ds(pl.multiple_of(at.b * patches, 128), patches)
        return remote(
            given_own.at[b], given.at[:, columns], given_send.at[i], given_recv.at[i], (at.r, b)
        )

    for i in range(1, 4):
        given_copy(i).start()
    mine = pl.ds(pl.multiple_of(at.b * patches, 128), patches)
    given[:, mine] = given_own[at.b]

    padded_rows = pl.ds(pl.multiple_of(at.me * PADDED, 16), PADDED)

    def mods_copy(owner):
        columns = pl.ds(pl.multiple_of(owner * PART, 128), PART)
        return remote(
            mods_own.at[:, columns],
            mods_weights.at[padded_rows],
            mods_send.at[0],
            mods_recv.at[0],
            (owner % ROWS_AXIS, owner // ROWS_AXIS),
        )

    def to_owner(i, carry):
        owner = (OWNER_OF * at.me + i) % OWNERS
        own_it = jnp.logical_and(owner % ROWS_AXIS == at.r, owner // ROWS_AXIS == at.b)

        @pl.when(own_it)
        def _():
            columns = pl.ds(pl.multiple_of(owner * PART, 128), PART)
            pltpu.make_async_copy(
                mods_own.at[:, columns], mods_weights.at[padded_rows], mods_recv.at[0]
            ).start()

        pl.when(jnp.logical_not(own_it))(lambda: mods_copy(owner).start())
        return carry

    lax.fori_loop(0, OWNERS, to_owner, 0)
    owner = at.b * ROWS_AXIS + at.r
    owns = at.b < OWNERS // ROWS_AXIS

    for i in range(1, ROWS_AXIS):
        for copy in code_copies(i):
            copy.wait_recv()

    time_pre = dot(time_in[...], features[...], NT) + time_bias[...]
    time_pre_out[...] = time_pre
    piece[0:PADDED, :] = jax.nn.silu(time_pre).astype(BF16)
    lane = lax.broadcasted_iota(jnp.int32, (128, 128), 1)
    class_rows = jnp.zeros((PADDED, 128), F32)
    for k in range(classes.shape[1] // 128):
        hot = ((labels[...] & 1023) == lane + 128 * k).astype(F32).astype(BF16)
        class_rows = class_rows + dot(classes[:, 128 * k : 128 * (k + 1)], hot, NT)
    piece[PADDED : 2 * PADDED, :] = class_rows.astype(BF16)
    piece[2 * PADDED : 3 * PADDED, :] = small_own[...]
    of_piece.open()
    of_first.open()
    of_time.along_line()
    of_piece.along_line()
    of_time.around_square()
    of_piece.around_square()
    of_time.close_square()
    of_piece.close_square()
    of_first.along_line()
    of_time.arrive()
    of_piece.arrive()

    for device in range(DEVICES):
        rows = pl.ds(PADDED * device, PADDED)
        loose[rows, :] = pieces[device, 0:PADDED, :].astype(F32)
    time_act = jnp.transpose(loose[...]).astype(BF16)
    compact(tall, pieces, 0)
    time_act_out[...] = jnp.transpose(tall[...]).astype(BF16)
    compact(tall, pieces, 2 * PADDED)
    small = jnp.transpose(tall[...])
    small_out[...] = small
    compact(tall, pieces, PADDED)
    condition = dot(time_act, time_weights[...], NN) + small[2:3, :] + jnp.transpose(tall[...])
    condition_out[...] = condition

    def part_copy(device, place):
        chip = pl.ds(pl.multiple_of(device // 2 * 8, 8), 8)
        columns = pl.ds(pl.multiple_of(owner * PART, 128), PART)
        return remote(
            mods_part.at[chip], mods.at[:, columns], part_sems.at[0], part_sems.at[1], place
        )

    @pl.when(owns)
    def _():
        tall[...] = jnp.transpose(jax.nn.silu(condition))
        loosen(loose, tall)
        pltpu.make_async_copy(mods_weights, mods_weights, mods_recv.at[0]).wait()
        mods_part[...] = dot(loose[...].astype(BF16), mods_weights[...], TN)
        at.others(lambda device, place: part_copy(device, place).start())
        chip = pl.ds(pl.multiple_of(at.me // 2 * 8, 8), 8)
        columns = pl.ds(pl.multiple_of(owner * PART, 128), PART)
        pltpu.make_async_copy(mods_part.at[chip], mods.at[:, columns], part_sems.at[1]).start()

    of_first.around_square()
    of_first.close_square()
    of_first.arrive()
    pltpu.make_async_copy(mods, mods, part_sems.at[1]).wait()
    for i in range(1, ROWS_AXIS):
        for copy in code_copies(i):
            copy.wait_send()
    for i in range(1, 4):
        given_copy(i).wait()

    @pl.when(owns)
    def _():
        sent = time_weights.at[pl.ds(0, (OWNERS - 1) * PADDED // 3)]
        remote(sent, sent, mods_send.at[0], mods_recv.at[0], at.sibling).wait_send()

    @pl.when(jnp.logical_not(owns))
    def _():
        sent = time_weights.at[pl.ds(0, OWNERS * PADDED // 3)]
        remote(sent, sent, mods_send.at[0], mods_recv.at[0], at.sibling).wait_send()

    @pl.when(owns)
    def _():
        sent = first.at[0, pl.ds(0, (DEVICES - 1) * 16), pl.ds(0, PART)]
        remote(sent, sent, part_sems.at[0], part_sems.at[1], at.sibling).wait_send()

    for group in (of_piece, of_time, of_first):
        group.finish()


def gather_weights(*operands):
    dma = pltpu.SemaphoreType.DMA
    anywhere, inside = (
        pl.BlockSpec(memory_space=pl.ANY),
        pl.BlockSpec(memory_space=pltpu.VMEM),
    )
    return pl.pallas_call(
        gather_kernel,
        in_specs=[anywhere] * 3 + [inside] * 7,
        out_specs=[anywhere] + [inside] * 8,
        out_shape=[
            jax.ShapeDtypeStruct((4, D, D), BF16),
            jax.ShapeDtypeStruct((8, 8 * D), F32),
            jax.ShapeDtypeStruct((128, D), F32),
            jax.ShapeDtypeStruct((128, D), F32),
            jax.ShapeDtypeStruct((128, D), BF16),
            jax.ShapeDtypeStruct((PADDED, 128), F32),
            jax.ShapeDtypeStruct((128, FREQ), BF16),
            jax.ShapeDtypeStruct((128, 128), jnp.int32),
            jax.ShapeDtypeStruct((2 * PATCH_IN, PATCHES), F32),
        ],
        scratch_shapes=[
            pltpu.VMEM((BLOCK, 128), BF16),
            pltpu.VMEM((DEVICES, BLOCK, 128), BF16),
            pltpu.VMEM((DEVICES * PADDED, D), BF16),
            pltpu.VMEM((DEVICES * PADDED, PART), BF16),
            pltpu.VMEM((D, 128), F32),
            pltpu.VMEM((DEVICES * PADDED, 128), F32),
            pltpu.VMEM((128, PART), F32),
            dma((4,)),
            dma((4,)),
            dma((4, ROWS_AXIS)),
            dma((1,)),
            dma((1,)),
            dma((2,)),
            *spread_sems(3),
        ],
        compiler_params=pltpu.CompilerParams(
            collective_id=0, has_side_effects=True, vmem_limit_bytes=32 << 20
        ),
        name="gather_weights",
    )(*operands)


class Collect:
    def __init__(self, at, part, out, buffers, sems, cut):
        self.at, self.part, self.out, self.cut = at, part, out, cut
        self.own, self.got, self.near, self.far, self.line = buffers
        (
            self.own_sem,
            self.core_send,
            self.core_recv,
            self.near_send,
            self.near_recv,
            self.far_send,
            self.far_recv,
            self.line_send,
            self.line_recv,
        ) = sems
        self.other_y = 1 - at.y

    def start(self):
        at = self.at
        for y in (0, 1):
            for core in (0, 1):

                def begin(keep, y=y, b=2 * y + core):
                    for source, first, rows in self.part(b):
                        self.move(y, pl.ds(first, rows), source, keep).start()

                pl.when(at.c == core)(functools.partial(begin, True))
                pl.when(at.c != core)(functools.partial(begin, False))

    def move(self, y, rows, source, keep):
        if keep:
            return pltpu.make_async_copy(source, self.own.at[y, rows], self.own_sem.at[y])
        return remote(
            source,
            self.got.at[y, rows],
            self.core_send.at[y],
            self.core_recv.at[y],
            self.at.sibling,
        )

    def arrive(self):
        for y in (0, 1):
            self.move(y, pl.ds(0, D), self.got.at[y], True).wait()
            self.move(y, pl.ds(0, D), self.got.at[y], False).wait_recv()

    @staticmethod
    def rows_of(r, start, size):
        return pl.ds(pl.multiple_of(r * BLOCK + start, 16), size)

    @staticmethod
    def add(target, sources, size):
        def step(i, carry):
            total = None
            for ref, index, start in sources:
                tile = ref[index + (pl.ds(pl.multiple_of(start + 16 * i, 16), 16),)].astype(F32)
                total = tile if total is None else total + tile
            ref, index, start = target
            ref[index + (pl.ds(pl.multiple_of(start + 16 * i, 16), 16),)] = total.astype(ref.dtype)
            return carry

        lax.fori_loop(0, size // 16, step, 0)

    def near_copy(self, route, i):
        at, cut = self.at, self.cut
        if route == 0:
            source = self.own.at[self.other_y, self.rows_of(i, 0, cut)]
            target = self.near.at[i, pl.ds(0, cut)]
            device = at.across_y
        else:
            rows = self.rows_of(2 * (i // 2) + at.other_x, cut, BLOCK - cut)
            source = self.own.at[i % 2, rows]
            target = self.near.at[i, pl.ds(cut, BLOCK - cut)]
            device = at.across_x
        return remote(
            source, target, self.near_send.at[route], self.near_recv.at[route, i], device
        )

    def far_copy(self, route, z):
        at, cut = self.at, self.cut
        if route == 0:
            source = self.own.at[at.y, self.rows_of(2 * z + at.other_x, 0, cut)]
            target = self.far.at[z, pl.ds(0, cut)]
            device = at.across_x
        else:
            source = self.own.at[self.other_y, self.rows_of(2 * z + at.x, cut, BLOCK - cut)]
            target = self.far.at[z, pl.ds(cut, BLOCK - cut)]
            device = at.across_y
        return remote(source, target, self.far_send.at[route], self.far_recv.at[route, z], device)

    def near_stage(self, begin, end):
        at, cut, own, got = self.at, self.cut, self.own, self.got

        def step(i, carry):
            for y, start, size, route in (
                (self.other_y, i * BLOCK, cut, 0),
                (i % 2, (2 * (i // 2) + at.other_x) * BLOCK + cut, BLOCK - cut, 1),
            ):
                self.add((own, (y,), start), [(own, (y,), start), (got, (y,), start)], size)
                self.near_copy(route, i).start()
            return carry

        lax.fori_loop(begin, end, step, 0)

    def far_stage(self, begin, end):
        at, cut, own, got = self.at, self.cut, self.own, self.got

        def step(z, carry):
            r, i = 2 * z + at.other_x, 2 * z + self.other_y
            for y, start, size, route, index, first in (
                (at.y, r * BLOCK, cut, 0, r, 0),
                (self.other_y, (2 * z + at.x) * BLOCK + cut, BLOCK - cut, 1, i, cut),
            ):
                self.near_copy(route, index).wait_recv()
                sources = [(own, (y,), start), (got, (y,), start), (self.near, (index,), first)]
                self.add((own, (y,), start), sources, size)
                self.far_copy(route, z).start()
            return carry

        lax.fori_loop(begin, end, step, 0)

    def line_copy(self, way, z):
        source = self.own.at[self.at.y, self.rows_of(2 * z + self.at.x, 0, BLOCK)]
        slot = z - 1 if way == 0 else z
        return remote(
            source,
            self.line.at[way, slot],
            self.line_send.at[way, slot],
            self.line_recv.at[way, slot],
            self.at.right if way == 0 else self.at.left,
        )

    def arrivals(self, z):
        self.near_copy(0, 2 * z + self.at.x).wait_recv()
        self.near_copy(1, 2 * z + self.at.y).wait_recv()
        self.far_copy(0, z).wait_recv()
        self.far_copy(1, z).wait_recv()

    def total(self, z, target, ways):
        at, cut = self.at, self.cut
        start = (2 * z + at.x) * BLOCK
        for route, begin, size in ((0, 0, cut), (1, cut, BLOCK - cut)):
            index = 2 * z + (at.x if route == 0 else at.y)
            sources = [
                (self.own, (at.y,), start + begin),
                (self.got, (at.y,), start + begin),
                (self.near, (index,), begin),
                (self.far, (z,), begin),
            ]
            for way in ways:
                sources.append((self.line, (way, z - 1 if way == 0 else z), begin))
            ref, place, base = target
            self.add((ref, place, base + begin), sources, size)

    def pass_on(self, way, z):
        at = self.at
        ahead = at.z > 0 if way == 0 else at.z < LINE - 1
        target = (self.own, (at.y,), (2 * z + at.x) * BLOCK)
        self.arrivals(z)

        @pl.when(ahead)
        def _():
            self.line_copy(way, z).wait_recv()
            self.total(z, target, (way,))

        pl.when(jnp.logical_not(ahead))(lambda: self.total(z, target, ()))
        self.line_copy(way, z).start()

    def line_stage(self, step):
        z = LINE - 1 - step
        pl.when(self.at.z < z)(functools.partial(self.pass_on, 0, z))
        pl.when(self.at.z > step)(functools.partial(self.pass_on, 1, step))

    def last(self):
        at = self.at
        self.arrivals(at.z)
        for z in range(LINE):
            ways = ((0,) if z > 0 else ()) + ((1,) if z < LINE - 1 else ())

            @pl.when(at.z == z)
            def _(z=z, ways=ways):
                for way in ways:
                    self.line_copy(way, z).wait_recv()
                self.total(z, (self.out, (), 0), ways)

    def finish(self):
        at, cut = self.at, self.cut
        for y in (0, 1):
            self.move(y, pl.ds(0, D), self.got.at[y], False).wait_send()
        for route, size in ((0, cut), (1, BLOCK - cut)):
            rows = self.own.at[0, pl.ds(0, 2 * LINE * size)]
            sems = self.near_send.at[route], self.near_recv.at[route, 0]
            remote(rows, rows, *sems, at.sibling).wait_send()
            rows = self.own.at[0, pl.ds(0, LINE * size)]
            sems = self.far_send.at[route], self.far_recv.at[route, 0]
            remote(rows, rows, *sems, at.sibling).wait_send()
        for step in range(LINE - 1):
            z = LINE - 1 - step
            pl.when(at.z < z)(lambda: self.line_copy(0, z).wait_send())
            pl.when(at.z > step)(lambda: self.line_copy(1, step).wait_send())


def collect_scratch():
    dma = pltpu.SemaphoreType.DMA
    return [
        pltpu.VMEM((2, D, D), BF16),
        pltpu.VMEM((2, D, D), BF16),
        pltpu.VMEM((2 * LINE, BLOCK, D), BF16),
        pltpu.VMEM((LINE, BLOCK, D), BF16),
        pltpu.VMEM((2, LINE - 1, BLOCK, D), BF16),
        dma((2,)),
        dma((2,)),
        dma((2,)),
        dma((2,)),
        dma((2, 2 * LINE)),
        dma((2,)),
        dma((2, LINE)),
        dma((2, LINE - 1)),
        dma((2, LINE - 1)),
    ]


def scatter_kernel(
    query,
    key,
    value,
    output,
    slots_own,
    mods_weights,
    condition,
    totals_own,
    out,
    slots,
    grad_condition,
    totals,
    quarters,
    slots_block,
    piece,
    pieces,
    tall,
    totals_got,
    band_send,
    band_recv,
    totals_send,
    totals_recv,
    slot_line_send,
    slot_line_recv,
    slot_sem,
    *rest,
):
    at = Place()
    at.greet()
    own = rest[0]
    of_first = Collect(
        at, lambda b: [((query, key, value, output)[b], 0, D)], out, rest[:5], rest[5:], SPLIT[0]
    )
    of_first.start()

    def band_copy(i):
        b = (at.b + i) % 4
        columns = pl.ds(pl.multiple_of(b * 2 * D, 128), 2 * D)
        return remote(
            slots_own.at[:, columns],
            quarters.at[at.b],
            band_send.at[i],
            band_recv.at[i],
            (at.r, b),
        )

    def band_arrival(i):
        source = quarters.at[(at.b + 4 - i) % 4]
        return remote(source, source, band_send.at[i], band_recv.at[i], at.sibling)

    def in_slots(r, b, start, size):
        columns = pl.ds(pl.multiple_of(b * 2 * D + start, 128), size)
        return slots.at[pl.ds(pl.multiple_of(r * 16, 16), 16), columns]

    def in_pieces(r, b, start, size):
        return pieces.at[4 * r + b, pl.ds(start, size)]

    def sems(index):
        return slot_line_send.at[index], slot_line_recv.at[index], slot_sem.at[index]

    def bytes_of(rows, width):
        return own.at[0, pl.ds(0, rows), pl.ds(0, width)]

    of_slots = Spread(at, in_slots, slots_block, 2 * D, 16, D, bytes_of, sems(0))
    of_piece = Spread(at, in_pieces, piece, PADDED, 128, 16, bytes_of, sems(1))

    def share_slots():
        mine = pl.ds(pl.multiple_of(at.b * 2 * D, 128), 2 * D)
        total = slots_own[:, mine].astype(F32)
        for i in range(1, 4):
            band_arrival(i).wait_recv()
        for i in range(1, 4):
            total = total + quarters[(at.b + 4 - i) % 4].astype(F32)
        slots_block[...] = total.astype(BF16)
        of_slots.open()

    def condition_back():
        of_slots.arrive()
        grad = dot(mods_weights[...], slots[...], NT)
        sigmoid = 1.0 / (1.0 + jnp.exp(-condition[...]))
        grad = grad * (sigmoid * (1.0 + condition[...] * (1.0 - sigmoid)))
        piece[...] = grad.astype(BF16)
        of_piece.open()

    def condition_arrives():
        of_piece.arrive()
        compact(tall, pieces, 0)
        grad_condition[...] = jnp.transpose(tall[...]).astype(BF16)

    def near_line():
        return (at.r + 2 - 4 * (at.z % 2), at.b)

    def far_line():
        return (at.r + 4 - 8 * (at.z // 2), at.b)

    partners = (at.sibling, at.across_x, at.across_y, near_line(), far_line())

    def totals_copy(step):
        return remote(
            totals_own if step == 0 else totals.at[step - 1],
            totals_got.at[step],
            totals_send.at[step],
            totals_recv.at[step],
            partners[step],
        )

    def totals_step(step):
        totals_copy(step).wait_recv()
        before = totals_own[...] if step == 0 else totals[step - 1]
        totals[step] = before + totals_got[step]
        if step + 1 < len(partners):
            totals_copy(step + 1).start()

    for i in range(1, 4):
        band_copy(i).start()
    totals_copy(0).start()
    share_slots()
    of_first.arrive()
    of_first.near_stage(0, 4)
    totals_step(0)
    of_slots.along_line()
    of_first.near_stage(4, 8)
    of_slots.around_square()
    totals_step(1)
    of_slots.close_square()
    of_first.far_stage(0, 2)
    condition_back()
    of_first.far_stage(2, 4)
    totals_step(2)
    of_piece.along_line()
    of_first.line_stage(0)
    of_piece.around_square()
    totals_step(3)
    of_first.line_stage(1)
    of_piece.close_square()
    of_first.line_stage(2)
    totals_step(4)
    condition_arrives()
    of_first.last()
    of_first.finish()
    for i in range(1, 4):
        band_copy(i).wait_send()
    for step in range(len(partners)):
        totals_copy(step).wait_send()
    of_slots.finish()
    of_piece.finish()


def scatter_sums(matrices, slots_own, mods_weights, condition, totals_own):
    dma = pltpu.SemaphoreType.DMA
    anywhere, inside = (
        pl.BlockSpec(memory_space=pl.ANY),
        pl.BlockSpec(memory_space=pltpu.VMEM),
    )
    steps = 5
    return pl.pallas_call(
        scatter_kernel,
        in_specs=[anywhere] * 4 + [inside] * 4,
        out_specs=[inside] * 4,
        out_shape=[
            jax.ShapeDtypeStruct((BLOCK, D), F32),
            jax.ShapeDtypeStruct((128, 8 * D), BF16),
            jax.ShapeDtypeStruct((128, D), BF16),
            jax.ShapeDtypeStruct((steps, *totals_own.shape), F32),
        ],
        scratch_shapes=[
            pltpu.VMEM((4, 16, 2 * D), BF16),
            pltpu.VMEM((16, 2 * D), BF16),
            pltpu.VMEM((PADDED, 128), BF16),
            pltpu.VMEM((DEVICES, PADDED, 128), BF16),
            pltpu.VMEM((D, 128), F32),
            pltpu.VMEM((steps, *totals_own.shape), F32),
            dma((4,)),
            dma((4,)),
            dma((steps,)),
            dma((steps,)),
            *spread_sems(2),
            *collect_scratch(),
        ],
        compiler_params=pltpu.CompilerParams(
            collective_id=1, has_side_effects=True, vmem_limit_bytes=61 << 20
        ),
        name="scatter_sums",
    )(*matrices, slots_own, mods_weights, condition, totals_own)


def attend_kernel(apart, q_ref, k_ref, v_ref, *rest, travels):
    head = pl.program_id(0)
    if travels:
        up_own, out_ref, log_ref, up, line_send, line_recv, spread_sem = rest
        at = Place()

        def in_up(r, b, start, size):
            rows = pl.ds(pl.multiple_of(r * BLOCK + start, 16), size)
            return up.at[rows, pl.ds(pl.multiple_of(b * D, 128), D)]

        def bytes_of(rows, width):
            return up.at[pl.ds(0, rows // 4), :]

        sems = line_send.at[0], line_recv.at[0], spread_sem.at[0]
        of_up = Spread(at, in_up, up_own, BLOCK, D, SPLIT[1], bytes_of, sems)

        def begin():
            at.greet()
            of_up.open()

        at_step(head, 0, begin)
        at_step(head, 3, lambda: of_up.along_line((1,)))
        at_step(head, 5, lambda: of_up.along_line((2,)))
        at_step(head, 7, lambda: of_up.along_line((3,)))
        at_step(head, 10, of_up.around_square)
        at_step(head, 14, of_up.close_square)
    else:
        out_ref, log_ref = rest
    attend_head(head, apart, q_ref, k_ref, v_ref, out_ref, log_ref, min(512, q_ref.shape[0]))
    if travels:

        def end():
            of_up.arrive()
            of_up.finish()

        at_step(head, HEADS - 1, end)


def attend_back_kernel(apart, q_ref, k_ref, v_ref, grad_ref, log_ref, *rest, travels):
    head = pl.program_id(0)
    if travels:
        up_grad, dq_ref, dk_ref, dv_ref, up_sum, *rest = rest
        at = Place()

        def part(b):
            return [(up_grad.at[:, pl.ds(b * D, D)], 0, D)]

        of_up = Collect(at, part, up_sum, rest[:5], rest[5:], SPLIT[1])

        def begin():
            at.greet()
            of_up.start()

        at_step(head, 0, begin)
        at_step(head, 1, of_up.arrive)
        for step in range(4):
            at_step(head, 1 + step, lambda: of_up.near_stage(2 * step, 2 * step + 2))
            at_step(head, 6 + step, lambda: of_up.far_stage(step, step + 1))
        for step in range(3):
            at_step(head, 11 + step, lambda: of_up.line_stage(step))
    else:
        dq_ref, dk_ref, dv_ref = rest
    attend_back_head(
        head, apart, q_ref, k_ref, v_ref, grad_ref, log_ref, dq_ref, dk_ref, dv_ref
    )
    if travels:

        def end():
            of_up.last()
            of_up.finish()

        at_step(head, HEADS - 1, end)


def attend(apart, queries, keys, values, up_own):
    q_len, k_len = queries.shape[0], keys.shape[0]
    travels = up_own is not None
    anywhere = pl.BlockSpec(memory_space=pl.ANY)
    return pl.pallas_call(
        functools.partial(attend_kernel, travels=travels),
        grid=(HEADS,),
        in_specs=[
            whole_block(apart.shape),
            whole_block((q_len, D)),
            whole_block((k_len, D)),
            whole_block((k_len, D)),
        ]
        + [anywhere] * travels,
        out_specs=[whole_block((q_len, D)), whole_block((HEADS, q_len))] + [anywhere] * travels,
        out_shape=[
            jax.ShapeDtypeStruct((q_len, D), BF16),
            jax.ShapeDtypeStruct((HEADS, q_len), F32),
        ]
        + [jax.ShapeDtypeStruct((D, FF), BF16)] * travels,
        scratch_shapes=spread_sems(1) if travels else [],
        compiler_params=pltpu.CompilerParams(
            vmem_limit_bytes=56 << 20,
            **(dict(collective_id=2, has_side_effects=True) if travels else {}),
        ),
        name="attend_rows",
    )(apart, queries, keys, values, *((up_own,) if travels else ()))


def attend_back(apart, queries, keys, values, grads, log_total, up_grad):
    q_len, k_len = queries.shape[0], keys.shape[0]
    travels = up_grad is not None
    anywhere = pl.BlockSpec(memory_space=pl.ANY)
    return pl.pallas_call(
        functools.partial(attend_back_kernel, travels=travels),
        grid=(HEADS,),
        in_specs=[
            whole_block(apart.shape),
            whole_block((q_len, D)),
            whole_block((k_len, D)),
            whole_block((k_len, D)),
            whole_block((q_len, D)),
            whole_block((HEADS, q_len)),
        ]
        + [anywhere] * travels,
        out_specs=[whole_block((q_len, D)), whole_block((k_len, D)), whole_block((k_len, D))]
        + [whole_block((BLOCK, D))] * travels,
        out_shape=[
            jax.ShapeDtypeStruct((q_len, D), BF16),
            jax.ShapeDtypeStruct((k_len, D), BF16),
            jax.ShapeDtypeStruct((k_len, D), BF16),
        ]
        + [jax.ShapeDtypeStruct((BLOCK, D), F32)] * travels,
        scratch_shapes=collect_scratch() if travels else [],
        compiler_params=pltpu.CompilerParams(
            vmem_limit_bytes=61 << 20,
            **(dict(collective_id=3, has_side_effects=True) if travels else {}),
        ),
        name="attend_rows_back",
    )(apart, queries, keys, values, grads, log_total, *((up_grad,) if travels else ()))


def matmul(operand, weights):
    return jnp.einsum("...i,ij->...j", operand, weights, preferred_element_type=F32)


def matmul_back(gradient, weights):
    return jnp.einsum("...j,ij->...i", gradient, weights, preferred_element_type=F32)


def outer_sum(operand, gradient):
    return jnp.einsum(
        "ni,nj->ij",
        operand.reshape(-1, operand.shape[-1]),
        gradient.reshape(-1, gradient.shape[-1]),
        preferred_element_type=F32,
    )


def column_sum(gradient):
    return jnp.sum(gradient.reshape(-1, gradient.shape[-1]), axis=0, dtype=F32)


def silu_back(values, gradient):
    return jax.vjp(jax.nn.silu, values)[1](gradient)[0]


def plan(time_steps):
    steps_all = jnp.arange(TIMESTEPS, dtype=jnp.int32)
    betas = BETA_LOW + (BETA_HIGH - BETA_LOW) * steps_all.astype(F32) / (TIMESTEPS - 1)
    cumulate = jnp.cumsum(jnp.log1p(-betas))
    pick_now = (time_steps[..., None] == steps_all).astype(F32)
    pick_prev = (time_steps[..., None] - 1 == steps_all).astype(F32)
    return jnp.stack(
        [
            jnp.sum(pick_now * betas, axis=-1),
            jnp.sum(pick_now * cumulate, axis=-1),
            jnp.sum(pick_prev * cumulate, axis=-1),
        ],
        axis=-1,
    )


def time_features(time_steps):
    half_width = FREQ // 2
    frequency = jnp.exp(-math.log(10000.0) * jnp.arange(half_width).astype(F32) / half_width)
    angles = time_steps.astype(F32)[..., None] * frequency
    return jnp.concatenate([jnp.cos(angles), jnp.sin(angles)], axis=-1)


def positions(four_way):
    quarter = D // 4
    omegas = jnp.exp(-math.log(10000.0) * jnp.arange(quarter).astype(F32) / quarter)
    angles = jnp.arange(GRID).astype(F32)[:, None] * omegas
    table = jnp.concatenate([jnp.sin(angles), jnp.cos(angles)], axis=-1)

    def grid(side):
        shape = (PATCHES // side**2, side, side, D // 2)
        down = jnp.broadcast_to(table[None, :side, None], shape)
        across = jnp.broadcast_to(table[None, None, :side], shape)
        return jnp.concatenate([down, across], axis=-1).reshape(SLOTS, SEGMENT, D)

    return jnp.where(four_way, grid(GRID // 2), grid(GRID))


def layer_norm(values):
    centered = values - jnp.mean(values, axis=-1, keepdims=True)
    return centered * lax.rsqrt(jnp.mean(centered * centered, axis=-1, keepdims=True) + NORM_EPS)


def modulate(values, shift, scaling):
    return layer_norm(values) * (1.0 + scaling) + shift


def patch_loss(output, target_noise, patch_sched):
    beta = patch_sched[..., 0:1]
    log_now = patch_sched[..., 1:2]
    log_prev = patch_sched[..., 2:3]
    error = output[..., :PATCH_IN] - target_noise
    log_beta = jnp.log(beta)
    keep_now = -jnp.expm1(log_now)
    log_post = log_beta + jnp.log(-jnp.expm1(log_prev)) - jnp.log(keep_now)
    coefficient = beta * lax.rsqrt(keep_now * (1.0 - beta))
    fraction = 0.5 * (output[..., PATCH_IN:] + 1.0)
    log_model = fraction * log_beta + (1.0 - fraction) * log_post
    diverge = 0.5 * (
        -1.0
        + log_model
        - log_post
        + jnp.exp(log_post - log_model)
        + (coefficient * error) ** 2 * jnp.exp(-log_model)
    )
    return jnp.mean(error * error, axis=-1) + jnp.mean(diverge, axis=-1) / math.log(2.0)


def adamw_step(weight, first_old, second_old, gradient, step_rate):
    first_new = DECAY_FIRST * first_old + (1.0 - DECAY_FIRST) * gradient
    second_new = DECAY_SECOND * second_old + (1.0 - DECAY_SECOND) * gradient * gradient
    first_hat = first_new / (1.0 - DECAY_FIRST**STEP)
    second_hat = second_new / (1.0 - DECAY_SECOND**STEP)
    return (
        weight - step_rate * first_hat / (jnp.sqrt(second_hat) + ADAM_EPS),
        first_new,
        second_new,
    )


def body(
    sizes,
    latents,
    gauss_noise,
    image_counts,
    timesteps,
    labels,
    wide_weights,
    square_weights,
    down_weights,
    embed_tables,
    all_biases,
    head_weights,
    first_wide,
    first_square,
    first_down,
    first_tables,
    first_biases,
    first_head,
    second_wide,
    second_square,
    second_down,
    second_tables,
    second_biases,
    second_head,
):
    n_rows, n_band = sizes
    n_all = n_rows * n_band
    rows_here, band_len, _ = latents.shape
    share = n_band // rows_here
    part_len = PATCHES // share
    at_row, at_band = lax.axis_index("rows"), lax.axis_index("band")
    own_row = at_band // share
    part_start = (at_band % share) * part_len
    n_slots = n_rows * rows_here * SLOTS
    groups = [[row * share + i for i in range(share)] for row in range(rows_here)]

    def in_row_gather(array):
        if share == 1:
            return array
        return lax.all_gather(array, "band", axis=0, tiled=True, axis_index_groups=groups)

    def in_row_scatter(array):
        if share == 1:
            return array
        return lax.psum_scatter(
            array, "band", scatter_dimension=0, tiled=True, axis_index_groups=groups
        )

    def in_row_sum(array):
        if share == 1:
            return array
        return lax.psum(array, "band", axis_index_groups=groups)

    tuned = sizes == (ROWS_AXIS, DEVICES // ROWS_AXIS)
    n_seg = part_len // SEGMENT
    given = jnp.concatenate([latents, gauss_noise], axis=-1)
    count = lax.dynamic_slice_in_dim(image_counts, own_row, 1)[0]
    four_way = count == SLOTS
    seg_first = part_start // SEGMENT + jnp.arange(n_seg)
    seg_slot = jnp.where(four_way, seg_first, 0)
    seg_hot = (seg_slot[:, None] == jnp.arange(SLOTS)).astype(F32)

    def by_segment(per_slot):
        return jnp.sum(seg_hot[:, :, None] * per_slot[None], axis=1)[:, None]

    wide_low = wide_weights.astype(BF16)
    square_low = square_weights.astype(BF16)
    down_low = down_weights.astype(BF16)
    tables_low = embed_tables.astype(BF16)
    biases_low = all_biases.astype(BF16)
    mods_low = wide_low[:, 3 * D + FF :]
    time_out_low = square_low[:, D:]
    first_group = jnp.concatenate([wide_low[:, : 3 * D], square_low[:, :D]], axis=1)
    up_group = wide_low[:, 3 * D : 3 * D + FF]
    head_low = head_weights.astype(BF16)
    head_matrix = head_low[:D]
    small_rows = jnp.concatenate([biases_low, tables_low[FREQ : FREQ + PATCH_IN]], axis=0)
    device = at_row * n_band + at_band
    if tuned:
        padded = lambda array: jnp.pad(array, ((0, PADDED - OWN), (0, 0)))
        regroup = functools.partial(
            lax.all_to_all, axis_name="band", split_axis=1, concat_axis=0, tiled=True
        )
        own_times = timesteps.reshape(-1)
        codes = (labels + 1024 * image_counts[:, None]).reshape(-1, 1)
        own_codes = jnp.broadcast_to(codes, (rows_here * SLOTS, 128))
        class_columns = jnp.pad(tables_low[FREQ + PATCH_IN :].T, ((0, 0), (0, 1024 - CLASSES)))
        (
            first_all,
            mods,
            condition_all,
            small_all,
            time_act_all,
            time_pre,
            frequency,
            codes,
            given,
        ) = gather_weights(
            regroup(first_group.reshape(-1, 4, D))[:, 0],
            padded(time_out_low),
            padded(mods_low),
            time_features(own_times).astype(BF16),
            own_codes,
            padded(tables_low[:FREQ].T),
            jnp.broadcast_to(padded(biases_low[1][:, None].astype(F32)), (PADDED, 128)),
            padded(class_columns),
            jnp.pad(small_rows.T, ((0, PADDED - OWN), (0, 128 - small_rows.shape[0]))),
            given.transpose(0, 2, 1),
        )
        given = given.T
        up_own = regroup(up_group.reshape(-1, 4, D))[:, 0]
        down_own, first_all = lax.optimization_barrier((down_low, first_all))
        down_all = lax.all_gather(down_own, AXES, axis=0, tiled=True)
        weight_q, weight_k, weight_v, weight_o = first_all
        biases = small_all[: all_biases.shape[0]]
        patch_in = small_all[all_biases.shape[0] :][:PATCH_IN].astype(BF16)
        mods = lax.dynamic_slice_in_dim(mods, (at_band % 2) * SLOTS, SLOTS, 0)
        own_columns = lambda array: lax.dynamic_slice_in_dim(array, device * OWN, OWN, 1)
        condition = own_columns(condition_all)
        time_act = own_columns(time_act_all)
        time_pre = time_pre[:OWN].T
        labels_all = codes[:, 0] & 1023
        images = (jnp.sum(codes[:, 0] >> 10) // SLOTS).astype(F32)
        cond_act = jax.nn.silu(condition).astype(BF16)
    else:
        given = lax.all_gather(given, "band", axis=1, tiled=True)
        given = lax.dynamic_slice_in_dim(given, own_row, 1, 0)[0]
        given = lax.dynamic_slice_in_dim(given, part_start, part_len, 0)
        codes = jnp.concatenate([timesteps, labels, image_counts[:, None]], axis=1)
        codes = lax.all_gather(codes, "rows", axis=0, tiled=True)
        labels_all = codes[:, SLOTS : 2 * SLOTS].reshape(n_slots)
        images = jnp.sum(codes[:, 2 * SLOTS]).astype(F32)
        frequency = time_features(codes[:, :SLOTS].reshape(n_slots)).astype(BF16)
        first_all = lax.all_gather(first_group, AXES, axis=0, tiled=True)
        up_all = lax.all_gather(up_group, AXES, axis=0, tiled=True)
        down_all = lax.all_gather(down_low, AXES, axis=0, tiled=True)
        weight_q, weight_k, weight_v, weight_o = jnp.split(first_all, 4, axis=1)
        small_all = lax.all_gather(small_rows, AXES, axis=1, tiled=True)
        biases = small_all[: all_biases.shape[0]].astype(F32)
        patch_in = small_all[all_biases.shape[0] :]
        own_biases = biases_low.astype(F32)
        time_pre = matmul(frequency, tables_low[:FREQ]) + own_biases[1]
        time_act = jax.nn.silu(time_pre).astype(BF16)
        class_rows = tables_low[FREQ + PATCH_IN :]
        class_part = class_rows[labels_all].astype(F32)
        time_out_columns = lax.all_to_all(
            time_out_low, AXES, split_axis=1, concat_axis=0, tiled=True
        )
        time_act_all = lax.all_gather(time_act, AXES, axis=1, tiled=True)
        condition = matmul(time_act_all, time_out_columns) + own_biases[2] + class_part
        cond_act = jax.nn.silu(condition).astype(BF16)
        mods_columns = lax.all_to_all(mods_low, AXES, split_axis=1, concat_axis=0, tiled=True)
        cond_act_all = lax.all_gather(cond_act, AXES, axis=1, tiled=True)
        mods_part = matmul(cond_act_all, mods_columns)
        mods_part = mods_part.reshape(n_rows * rows_here, SLOTS, -1)
        if share > 1:
            mods_part = jnp.repeat(mods_part, share, axis=0)
        mods = lax.all_to_all(mods_part, AXES, split_axis=0, concat_axis=2, tiled=True)[0]
    label_hot = (labels_all[:, None] == jnp.arange(CLASSES, dtype=jnp.int32)).astype(BF16)
    mods_bias = jnp.concatenate([biases[3:9].reshape(-1), biases[17:19].reshape(-1)])
    seg_mods = by_segment(mods + mods_bias)
    (
        shift_one,
        scale_one,
        gate_one,
        shift_two,
        scale_two,
        gate_two,
        final_shift,
        final_scale,
    ) = jnp.split(seg_mods, 8, axis=-1)

    given = given.reshape(n_seg, SEGMENT, 2 * PATCH_IN)
    row_latents, row_noise = given[..., :PATCH_IN], given[..., PATCH_IN:]
    own_times = lax.dynamic_slice_in_dim(timesteps, own_row, 1, 0)[0]
    patch_sched = by_segment(plan(own_times))
    log_now = patch_sched[..., 1:2]
    noisy = (
        jnp.exp(0.5 * log_now) * row_latents + jnp.sqrt(-jnp.expm1(log_now)) * row_noise
    ).astype(BF16)
    position = lax.dynamic_slice_in_dim(positions(four_way), part_start // SEGMENT, n_seg, 0)
    hidden_zero = matmul(noisy, patch_in) + biases[0] + position
    normed_one = modulate(hidden_zero, shift_one, scale_one).astype(BF16)
    flat = lambda array: array.reshape(part_len, array.shape[-1])
    deep = lambda array: array.reshape(n_seg, SEGMENT, array.shape[-1])
    queries = flat(matmul(normed_one, weight_q) + biases[9]).astype(BF16)
    keys = flat(matmul(normed_one, weight_k)).astype(BF16)
    values = flat(matmul(normed_one, weight_v) + biases[10]).astype(BF16)
    keys, values = in_row_gather(keys), in_row_gather(values)
    key_seg = jnp.where(four_way, jnp.arange(SLOTS), 0)
    apart = jnp.where(key_seg[:, None] == jnp.repeat(seg_slot, SEGMENT), 0.0, -1e30).astype(F32)
    if tuned:
        attended, log_total, up_all = attend(apart, queries, keys, values, up_own)
    else:
        attended, log_total = attend(apart, queries, keys, values, None)
    attended = deep(attended)
    branch_one = matmul(attended, weight_o) + biases[11]
    hidden_one = hidden_zero + gate_one * branch_one
    normed_two = modulate(hidden_one, shift_two, scale_two).astype(BF16)
    upward = matmul(normed_two, up_all) + biases[12:16].reshape(-1)
    active = jax.nn.gelu(upward, approximate=True).astype(BF16)
    branch_two = matmul(active, down_all) + biases[16]
    hidden_two = hidden_one + gate_two * branch_two
    normed_out = modulate(hidden_two, final_shift, final_scale).astype(BF16)
    output = matmul(normed_out, head_matrix) + head_low[D].astype(F32)
    patch_share = jnp.where(four_way, 1.0 / SEGMENT, 1.0 / PATCHES)
    losses, loss_back = jax.vjp(lambda at: patch_loss(at, row_noise, patch_sched), output)
    loss_local = jnp.sum(patch_share * losses)

    grad_out = loss_back(jnp.broadcast_to(patch_share / images, losses.shape))[0].astype(BF16)
    grad_two, grad_fshift, grad_fscale = jax.vjp(modulate, hidden_two, final_shift, final_scale)[1](
        matmul_back(grad_out, head_matrix)
    )
    seg_sum = lambda array: jnp.sum(array, axis=1, keepdims=True)
    grad_gate_two = seg_sum(grad_two * branch_two)
    grad_branch_two = (gate_two * grad_two).astype(BF16)
    down_grad = outer_sum(active, grad_branch_two)
    grad_active = matmul_back(grad_branch_two, down_all)
    grad_upward = jax.vjp(lambda at: jax.nn.gelu(at, approximate=True), upward)[1](grad_active)[
        0
    ].astype(BF16)
    up_grad = outer_sum(normed_two, grad_upward)
    grad_one_part, grad_shift_two, grad_scale_two = jax.vjp(
        modulate, hidden_one, shift_two, scale_two
    )[1](matmul_back(grad_upward, up_all))
    grad_one = grad_two + grad_one_part
    grad_gate_one = seg_sum(grad_one * branch_one)
    grad_branch_one = (gate_one * grad_one).astype(BF16)
    output_grad = outer_sum(attended, grad_branch_one)
    grad_attended = flat(matmul_back(grad_branch_one, weight_o).astype(BF16))
    if tuned:
        grad_query, grad_key, grad_value, up_sum = attend_back(
            apart, queries, keys, values, grad_attended, log_total, up_grad.astype(BF16)
        )
    else:
        grad_query, grad_key, grad_value = attend_back(
            apart, queries, keys, values, grad_attended, log_total, None
        )
    grad_key, grad_value = in_row_scatter(grad_key), in_row_scatter(grad_value)
    q_grad = outer_sum(normed_one, grad_query)
    k_grad = outer_sum(normed_one, grad_key)
    v_grad = outer_sum(normed_one, grad_value)
    grad_normed = deep(
        matmul_back(grad_query, weight_q)
        + matmul_back(grad_key, weight_k)
        + matmul_back(grad_value, weight_v)
    )
    grad_zero_part, grad_shift_one, grad_scale_one = jax.vjp(
        modulate, hidden_zero, shift_one, scale_one
    )[1](grad_normed)
    grad_zero = (grad_one + grad_zero_part).astype(BF16)
    patch_grad = outer_sum(noisy, grad_zero)

    seg_grads = jnp.concatenate(
        [
            grad_shift_one,
            grad_scale_one,
            grad_gate_one,
            grad_shift_two,
            grad_scale_two,
            grad_gate_two,
            grad_fshift,
            grad_fscale,
        ],
        axis=-1,
    )
    slot_grads = in_row_sum(jnp.sum(seg_hot[:, :, None] * seg_grads, axis=0)).astype(BF16)
    last_row = jnp.concatenate([column_sum(grad_out), loss_local[None]])
    totals = jnp.concatenate(
        [
            column_sum(grad_zero)[None],
            column_sum(grad_query)[None],
            column_sum(grad_value)[None],
            column_sum(grad_branch_one)[None],
            column_sum(grad_upward).reshape(FF // D, D),
            column_sum(grad_branch_two)[None],
            patch_grad,
            outer_sum(grad_out, normed_out),
            jnp.pad(last_row, (0, D - last_row.shape[0]))[None],
        ],
        axis=0,
    )
    if tuned:
        slots_own = jnp.where(
            (jnp.arange(4 * SLOTS) // SLOTS == at_band)[:, None], jnp.tile(slot_grads, (4, 1)), 0
        ).astype(BF16)
        regroup_back = functools.partial(
            lax.all_to_all, axis_name="band", split_axis=0, concat_axis=1, tiled=True
        )
        up_squares = jnp.sum(up_sum * up_sum)
        up_grad = regroup_back(up_sum[:, None]).reshape(-1, FF)
        matrices = (q_grad, k_grad, v_grad, output_grad)
        down_grad = lax.psum_scatter(
            down_grad.astype(BF16), AXES, scatter_dimension=0, tiled=True
        )
        slots_own, down_grad = lax.optimization_barrier((slots_own, down_grad))
        down_grad = down_grad.astype(F32)
        sums, slot_grads, grad_condition_all, totals = scatter_sums(
            [array.astype(BF16) for array in matrices],
            slots_own,
            padded(mods_low),
            padded(condition.T),
            jnp.pad(totals, ((0, -totals.shape[0] % 8), (0, 0))),
        )
        totals = totals[-1]
        first_grad = regroup_back(sums[:, None]).reshape(-1, 4 * D)
        local_squares = jnp.sum(sums * sums) + up_squares + jnp.sum(down_grad * down_grad)
        grad_condition = own_columns(grad_condition_all)
    else:
        slot_grads = lax.all_gather(slot_grads, AXES, axis=0, tiled=True)
        if share > 1:
            slot_grads = slot_grads.reshape(-1, share, SLOTS, 8 * D)[:, 0].reshape(n_slots, 8 * D)
        grad_condition = silu_back(condition, matmul_back(slot_grads, mods_low)).astype(BF16)
        grad_condition_all = lax.all_gather(grad_condition, AXES, axis=1, tiled=True)

        def scatter(array):
            return lax.psum_scatter(array, AXES, scatter_dimension=0, tiled=True)

        first_grad = scatter(jnp.concatenate([q_grad, k_grad, v_grad, output_grad], axis=1))
        up_grad = scatter(up_grad)
        down_grad = scatter(down_grad)
        local_squares = sum(jnp.sum(array * array) for array in (first_grad, up_grad, down_grad))
        totals = lax.psum(totals, AXES)
    mods_grad = outer_sum(cond_act, slot_grads)
    mods_bias_grad = column_sum(slot_grads).reshape(8, n_all, -1)
    time_out_grad = outer_sum(time_act, grad_condition_all)
    class_grad = outer_sum(label_hot, grad_condition)
    grad_time_pre = silu_back(time_pre, matmul_back(grad_condition_all, time_out_low)).astype(BF16)
    time_in_grad = outer_sum(frequency, grad_time_pre)
    n_sums = 9 + PATCH_IN
    own_width = D // n_all
    row_grads = lax.dynamic_slice_in_dim(totals[:n_sums], device * own_width, own_width, 1)
    head_total = jnp.concatenate(
        [totals[n_sums : n_sums + 32].T, totals[n_sums + 32, :32][None]], axis=0
    )
    loss_sum = totals[n_sums + 32, 32]
    own_mods_bias = lax.dynamic_index_in_dim(mods_bias_grad, device, 1, keepdims=False)
    grad_wide = jnp.concatenate([first_grad[:, : 3 * D], up_grad, mods_grad], axis=1)
    grad_square = jnp.concatenate([first_grad[:, 3 * D :], time_out_grad], axis=1)
    grad_tables = jnp.concatenate([time_in_grad, row_grads[9:], class_grad], axis=0)
    grad_biases = jnp.concatenate(
        [
            row_grads[:1],
            column_sum(grad_time_pre)[None],
            column_sum(grad_condition)[None],
            own_mods_bias[:6],
            row_grads[1:9],
            own_mods_bias[6:],
        ],
        axis=0,
    )
    owned_grads = (grad_wide, grad_square, down_grad, grad_tables, grad_biases)
    for array in (mods_grad, time_out_grad, grad_tables, grad_biases):
        local_squares = local_squares + jnp.sum(array * array)
    squares = lax.all_to_all(
        jnp.broadcast_to(local_squares, (n_all, 1, 128)), AXES, split_axis=0, concat_axis=1, tiled=True
    )
    grad_norm = jnp.sqrt(jnp.sum(squares[0, :, 0]) + jnp.sum(head_total * head_total))
    clip_factor = jnp.minimum(1.0, CLIP_NORM / (grad_norm + 1e-06))
    params = (wide_weights, square_weights, down_weights, embed_tables, all_biases, head_weights)
    firsts = (first_wide, first_square, first_down, first_tables, first_biases, first_head)
    seconds = (second_wide, second_square, second_down, second_tables, second_biases, second_head)
    gradients = owned_grads + (head_total,)
    results = [
        adamw_step(
            params[which],
            firsts[which],
            seconds[which],
            gradients[which] * clip_factor,
            LEARN_RATES[which],
        )
        for which in range(6)
    ]
    return (
        tuple(result[0] for result in results)
        + tuple(result[1] for result in results)
        + tuple(result[2] for result in results)
        + tuple(result[0].astype(BF16) for result in results)
        + (grad_norm, loss_sum, images)
    )


def solution(mesh):
    sizes = (mesh.shape["rows"], mesh.shape["band"])
    by_row, by_column, copied = P(AXES, None), P(None, AXES), P()
    params = (by_row, by_row, by_row, by_column, by_column, copied)
    patches = P("rows", "band", None)
    return jax.shard_map(
        functools.partial(body, sizes),
        mesh=mesh,
        in_specs=(patches, patches, P("rows"), P("rows", None), P("rows", None)) + 3 * params,
        out_specs=4 * params + (copied, copied, copied),
        check_vma=False,
    )
```

```python
import functools
import math

import jax
import jax.numpy as jnp
from jax import lax
from jax.experimental import pallas as pl
from jax.experimental.pallas import tpu as pltpu
from jax.sharding import PartitionSpec as P

D = 1152
FF = 4608
HEADS = 16
HEAD_DIM = D // HEADS
CLASSES = 1001
FREQ = 256
PATCH_IN = 16
GRID = 32
PATCHES = GRID * GRID
SLOTS = 4
SEGMENT = PATCHES // SLOTS
TIMESTEPS = 1000
STEP = 10

BETA_LOW = 0.0001
BETA_HIGH = 0.02
NORM_EPS = 1e-06
CLIP_NORM = 0.1
DECAY_FIRST = 0.9
DECAY_SECOND = 0.999
ADAM_EPS = 1e-08
LEARN_RATES = (0.1, 0.1, 0.05, 0.2, 0.3, 0.1)

GELU_ROOT = math.sqrt(2.0 / math.pi)
GELU_CUBE = 0.044715

AXES = ("rows", "band")
WINDOW = 256
SCALE = HEAD_DIM ** (-0.5)
NT = (((1,), (1,)), ((), ()))
TN = (((0,), (0,)), ((), ()))
NN = (((1,), (0,)), ((), ()))
BF16 = jnp.bfloat16
F32 = jnp.float32


def dot(left, right, dims):
    return lax.dot_general(left, right, dims, preferred_element_type=F32)


def head_window(head):
    start = jnp.minimum(head * HEAD_DIM // 128, (D - WINDOW) // 128) * 128
    return pl.multiple_of(start, 128), head * HEAD_DIM - start


def head_mask(rows, offset):
    lane = lax.broadcasted_iota(jnp.int32, (rows, WINDOW), 1)
    return (lane >= offset) & (lane < offset + HEAD_DIM)


def attend_head(head, apart, q_ref, k_ref, v_ref, out_ref, log_ref, q_block):
    q_len, k_len = q_ref.shape[0], k_ref.shape[0]
    start, offset = head_window(head)
    window = pl.ds(start, WINDOW)
    for at in range(0, q_len, q_block):
        rows = pl.ds(at, q_block)
        mask = head_mask(q_block, offset)
        query = jnp.where(mask, q_ref[rows, window], 0).astype(BF16)
        scores = jnp.concatenate(
            [
                dot(k_ref[pl.ds(k_at, SEGMENT), window], query, NT)
                + apart[pl.ds(k_at // SEGMENT, 1), rows]
                for k_at in range(0, k_len, SEGMENT)
            ],
            axis=0,
        )
        top = jnp.max(scores, axis=0, keepdims=True)
        weights = jnp.exp((scores - top) * SCALE)
        total = jnp.sum(weights, axis=0, keepdims=True)
        weights = (weights * (1.0 / total)).astype(BF16)
        mixed = dot(weights, v_ref[:, window], TN).astype(BF16)
        out_ref[rows, window] = jnp.where(mask, mixed, out_ref[rows, window])
        log_ref[pl.ds(head, 1), rows] = top * SCALE + jnp.log(total)


def attend_back_head(
    head, apart, q_ref, k_ref, v_ref, grad_ref, log_ref, dq_ref, dk_ref, dv_ref
):
    q_len, k_len = q_ref.shape[0], k_ref.shape[0]
    start, offset = head_window(head)
    window = pl.ds(start, WINDOW)
    mask = head_mask(q_len, offset)
    query = jnp.where(mask, q_ref[:, window], 0).astype(BF16)
    grad = jnp.where(mask, grad_ref[:, window], 0).astype(BF16)
    key = k_ref[:, window]
    log_total = log_ref[pl.ds(head, 1), :]
    probs = jnp.concatenate(
        [
            jnp.exp(
                dot(k_ref[pl.ds(k_at, SEGMENT), window], query, NT) * SCALE
                + (apart[pl.ds(k_at // SEGMENT, 1), :] - log_total)
            )
            for k_at in range(0, k_len, SEGMENT)
        ],
        axis=0,
    )
    both = probs * dot(v_ref[:, window], grad, NT)
    inner = jnp.sum(both, axis=0, keepdims=True)
    grad_scores = (both - probs * inner).astype(BF16)
    grad_value = dot(probs.astype(BF16), grad, NN)
    grad_key = dot(grad_scores, query, NN) * SCALE
    grad_query = (dot(grad_scores, key, TN) * SCALE).astype(BF16)
    dq_ref[:, window] = jnp.where(mask, grad_query, dq_ref[:, window])
    mask = head_mask(k_len, offset)
    dk_ref[:, window] = jnp.where(mask, grad_key.astype(BF16), dk_ref[:, window])
    dv_ref[:, window] = jnp.where(mask, grad_value.astype(BF16), dv_ref[:, window])


def whole_block(shape):
    return pl.BlockSpec(shape, lambda step: (0,) * len(shape))


def at_step(head, step, do):
    pl.when(head == step)(do)


MESH_ID = pl.DeviceIdType.MESH
BLOCK = 144
LINE = 4
SPLIT = (80, 64, 80)
ROWS_AXIS = 8
DEVICES = 32
OWN = D // DEVICES
PADDED = 48
ROUNDED = 40
PART = 384
OWNERS = 24
OWNER_OF = 7


class Place:
    def __init__(self):
        self.r, self.b = lax.axis_index("rows"), lax.axis_index("band")
        self.me = 4 * self.r + self.b
        self.z, self.x = self.r // 2, self.r % 2
        self.y, self.c = self.b // 2, self.b % 2
        self.other_x, self.other_b = 1 - self.x, self.b + 2 - 4 * self.y
        self.across_x = (self.r + 1 - 2 * self.x, self.b)
        self.across_y = (self.r, self.other_b)
        self.sibling = (self.r, self.b + 1 - 2 * self.c)
        self.right = (self.r + 2, self.b)
        self.left = (self.r - 2, self.b)

    def others(self, do):
        def step(i, carry):
            device = (self.me + i) % DEVICES
            do(device, (device // 4, device % 4))
            return carry

        lax.fori_loop(1, DEVICES, step, 0)

    def greet(self):
        barrier = pltpu.get_barrier_semaphore()
        self.others(
            lambda _, device: pl.semaphore_signal(
                barrier, inc=1, device_id=device, device_id_type=MESH_ID
            )
        )
        pl.semaphore_wait(barrier, DEVICES - 1)

    def each_source(self, do, steps):
        for step in steps:
            if step == 0:
                do(self.z)
            else:
                pl.when(self.z - step >= 0)(functools.partial(do, self.z - step))
                pl.when(self.z + step < LINE)(functools.partial(do, self.z + step))


def remote(source, target, send, receive, device):
    return pltpu.make_async_remote_copy(
        source, target, send, receive, device_id=device, device_id_type=MESH_ID
    )


class Spread:
    def __init__(self, at, place, own, rows, width, cut, dummy, sems):
        self.at, self.place, self.own = at, place, own
        self.rows, self.width, self.cut, self.dummy = rows, width, cut, dummy
        self.line_send, self.line_recv, self.sem = sems


    def block(self, r, b, start=0, size=None):
        return self.place(r, b, start, self.rows if size is None else size)

    def to_sibling(self, source, target):
        return remote(source, target, self.sem.at[3], self.sem.at[4], self.at.sibling)

    def to_x(self, source, target, slot):
        return remote(source, target, self.sem.at[1], self.sem.at[slot], self.at.across_x)

    def to_y(self, source, target, slot):
        return remote(source, target, self.sem.at[2], self.sem.at[slot], self.at.across_y)

    def line_copy(self, way, z, source=None):
        target = self.block(2 * z + self.at.x, self.at.b)
        return remote(
            target if source is None else source,
            target,
            self.line_send.at[way, z],
            self.line_recv.at[way, z],
            self.at.right if way == 0 else self.at.left,
        )

    def fan(self, z, source=None):
        target = self.block(2 * z + self.at.x, self.at.b)
        source = target if source is None else source
        self.to_x(source, target, 5 + z).start()
        self.to_y(source, target, 9 + z).start()
        self.to_sibling(source, target).start()

    def local(self):
        return pltpu.make_async_copy(self.own, self.block(self.at.r, self.at.b), self.sem.at[0])

    def open(self):
        at = self.at
        self.local().start()
        pl.when(at.z < LINE - 1)(lambda: self.line_copy(0, at.z, self.own).start())
        pl.when(at.z > 0)(lambda: self.line_copy(1, at.z, self.own).start())
        self.fan(at.z, self.own)

    def along_line(self, steps=(1, 2, 3)):
        at = self.at
        for step in steps:
            for way in (0, 1):
                z = at.z - step if way == 0 else at.z + step

                @pl.when(z >= 0 if way == 0 else z < LINE)
                def _(way=way, z=z):
                    copy = self.line_copy(way, z)
                    copy.wait_recv()
                    onward = at.z < LINE - 1 if way == 0 else at.z > 0
                    pl.when(onward)(lambda: copy.start())
                    self.fan(z)

    def around_square(self, steps=(0, 1, 2, 3)):
        at, cut = self.at, self.cut

        def do(z):
            ref = self.block(2 * z + at.other_x, at.b)
            self.to_x(ref, ref, 5 + z).wait_recv()
            part = self.block(2 * z + at.other_x, at.b, 0, cut)
            self.to_y(part, part, 17 + z).start()
            self.to_sibling(ref, ref).start()
            ref = self.block(2 * z + at.x, at.other_b)
            self.to_y(ref, ref, 9 + z).wait_recv()
            part = self.block(2 * z + at.x, at.other_b, cut, self.rows - cut)
            self.to_x(part, part, 13 + z).start()
            self.to_sibling(ref, ref).start()

        at.each_source(do, steps)

    def close_square(self, steps=(0, 1, 2, 3)):
        at, cut = self.at, self.cut

        def do(z):
            part = self.block(2 * z + at.other_x, at.other_b, 0, cut)
            self.to_y(part, part, 17 + z).wait_recv()
            part = self.block(2 * z + at.other_x, at.other_b, cut, self.rows - cut)
            self.to_x(part, part, 13 + z).wait_recv()
            ref = self.block(2 * z + at.other_x, at.other_b)
            self.to_sibling(ref, ref).start()

        at.each_source(do, steps)

    def counted(self, rows):
        if self.width >= 128:
            return self.dummy(rows, self.width)
        return self.dummy(rows * self.width // D, D)

    def arrive(self):
        self.local().wait()
        rows = self.counted(4 * LINE * self.rows)
        self.to_sibling(rows, rows).wait_recv()

    def finish(self):
        at, cut = self.at, self.cut
        pl.when(at.z < LINE - 1)(lambda: self.line_copy(0, at.z).wait_send())
        pl.when(at.z > 0)(lambda: self.line_copy(1, at.z).wait_send())
        for step in range(1, LINE):
            go = jnp.logical_and(at.z - step >= 0, at.z < LINE - 1)
            pl.when(go)(lambda: self.line_copy(0, at.z - step).wait_send())
            go = jnp.logical_and(at.z + step < LINE, at.z > 0)
            pl.when(go)(lambda: self.line_copy(1, at.z + step).wait_send())
        rows = self.counted(LINE * (2 * self.rows - cut))
        self.to_x(rows, rows, 5).wait_send()
        rows = self.counted(LINE * (self.rows + cut))
        self.to_y(rows, rows, 9).wait_send()
        rows = self.counted(4 * LINE * self.rows)
        self.to_sibling(rows, rows).wait_send()


def spread_sems(count):
    dma = pltpu.SemaphoreType.DMA
    return [dma((count, 2, LINE)), dma((count, 2, LINE)), dma((count, 21))]


def compact(target, pieces, first_row):
    for device in range(DEVICES):
        rows = pieces[device, first_row : first_row + PADDED, :].astype(F32)
        target[OWN * device : OWN * (device + 1), :] = rows[:OWN]


def loosen(target, rows):
    for device in range(DEVICES):
        own = rows[OWN * device : OWN * (device + 1), :]
        target[PADDED * device : PADDED * device + OWN, :] = own
        target[PADDED * device + OWN : PADDED * (device + 1), :] = jnp.zeros(
            (PADDED - OWN, rows.shape[1]), F32
        )


def gather_kernel(
    own,
    time_own,
    mods_own,
    features_own,
    labels_own,
    time_in,
    time_bias,
    classes,
    small_own,
    given_own,
    first,
    mods,
    condition_out,
    small_out,
    time_act_out,
    time_pre_out,
    features,
    labels,
    given,
    piece,
    pieces,
    time_weights,
    mods_weights,
    tall,
    loose,
    mods_part,
    given_send,
    given_recv,
    code_sems,
    mods_send,
    mods_recv,
    part_sems,
    line_send,
    line_recv,
    spread_sem,
):
    at = Place()
    at.greet()

    def rows_at(r, start, size):
        return pl.ds(pl.multiple_of(r * BLOCK + start, 16), size)

    def in_first(r, b, start, size):
        return first.at[b, rows_at(r, start, size)]

    def in_time(r, b, start, size):
        return time_weights.at[pl.ds(pl.multiple_of((4 * r + b) * PADDED + start, 16), size)]

    def in_pieces(r, b, start, size):
        return pieces.at[4 * r + b, pl.ds(start, size)]

    def spread(index, place, source, rows, width, cut):
        sems = line_send.at[index], line_recv.at[index], spread_sem.at[index]
        return Spread(at, place, source, rows, width, cut, bytes_of, sems)

    def bytes_of(rows, width):
        if rows <= D:
            return first.at[0, pl.ds(0, rows), pl.ds(0, width)]
        return first.at[:, pl.ds(0, rows // 4), pl.ds(0, width)]

    of_first = spread(0, in_first, own, BLOCK, D, SPLIT[0])
    of_time = spread(1, in_time, time_own, PADDED, D, 16)
    of_piece = spread(2, in_pieces, piece, BLOCK, 128, SPLIT[0])

    def code_copies(i):
        r = (at.r + i) % ROWS_AXIS
        mine = pl.ds(pl.multiple_of(at.r * 16, 16), 16)
        device = (r, at.b)
        return (
            remote(features_own, features.at[mine], code_sems.at[0, i], code_sems.at[1, i], device),
            remote(labels_own, labels.at[mine], code_sems.at[2, i], code_sems.at[3, i], device),
        )

    for i in range(1, ROWS_AXIS):
        for copy in code_copies(i):
            copy.start()
    mine = pl.ds(pl.multiple_of(at.r * 16, 16), 16)
    features[mine, :] = features_own[...]
    labels[mine, :] = labels_own[...]
    of_time.open()

    patches = given_own.shape[2]

    def given_copy(i):
        b = (at.b + i) % 4
        columns = pl.ds(pl.multiple_of(at.b * patches, 128), patches)
        return remote(
            given_own.at[b], given.at[:, columns], given_send.at[i], given_recv.at[i], (at.r, b)
        )

    for i in range(1, 4):
        given_copy(i).start()
    mine = pl.ds(pl.multiple_of(at.b * patches, 128), patches)
    given[:, mine] = given_own[at.b]

    padded_rows = pl.ds(pl.multiple_of(at.me * PADDED, 16), PADDED)

    def mods_copy(owner):
        columns = pl.ds(pl.multiple_of(owner * PART, 128), PART)
        return remote(
            mods_own.at[:, columns],
            mods_weights.at[padded_rows],
            mods_send.at[0],
            mods_recv.at[0],
            (owner % ROWS_AXIS, owner // ROWS_AXIS),
        )

    def to_owner(i, carry):
        owner = (OWNER_OF * at.me + i) % OWNERS
        own_it = jnp.logical_and(owner % ROWS_AXIS == at.r, owner // ROWS_AXIS == at.b)

        @pl.when(own_it)
        def _():
            columns = pl.ds(pl.multiple_of(owner * PART, 128), PART)
            pltpu.make_async_copy(
                mods_own.at[:, columns], mods_weights.at[padded_rows], mods_recv.at[0]
            ).start()

        pl.when(jnp.logical_not(own_it))(lambda: mods_copy(owner).start())
        return carry

    lax.fori_loop(0, OWNERS, to_owner, 0)
    owner = at.b * ROWS_AXIS + at.r
    owns = at.b < OWNERS // ROWS_AXIS

    for i in range(1, ROWS_AXIS):
        for copy in code_copies(i):
            copy.wait_recv()

    time_pre = dot(time_in[...], features[...], NT) + time_bias[...]
    time_pre_out[...] = time_pre
    piece[0:PADDED, :] = jax.nn.silu(time_pre).astype(BF16)
    lane = lax.broadcasted_iota(jnp.int32, (128, 128), 1)
    class_rows = jnp.zeros((PADDED, 128), F32)
    for k in range(classes.shape[1] // 128):
        hot = ((labels[...] & 1023) == lane + 128 * k).astype(F32).astype(BF16)
        class_rows = class_rows + dot(classes[:, 128 * k : 128 * (k + 1)], hot, NT)
    piece[PADDED : 2 * PADDED, :] = class_rows.astype(BF16)
    piece[2 * PADDED : 3 * PADDED, :] = small_own[...]
    of_piece.open()
    of_first.open()
    of_time.along_line()
    of_piece.along_line()
    of_time.around_square()
    of_piece.around_square()
    of_time.close_square()
    of_piece.close_square()
    of_first.along_line()
    of_time.arrive()
    of_piece.arrive()

    for device in range(DEVICES):
        rows = pl.ds(PADDED * device, PADDED)
        loose[rows, :] = pieces[device, 0:PADDED, :].astype(F32)
    time_act = jnp.transpose(loose[...]).astype(BF16)
    compact(tall, pieces, 0)
    time_act_out[...] = jnp.transpose(tall[...]).astype(BF16)
    compact(tall, pieces, 2 * PADDED)
    small = jnp.transpose(tall[...])
    small_out[...] = small
    compact(tall, pieces, PADDED)
    condition = dot(time_act, time_weights[...], NN) + small[2:3, :] + jnp.transpose(tall[...])
    condition_out[...] = condition

    def part_copy(device, place):
        chip = pl.ds(pl.multiple_of(device // 2 * 8, 8), 8)
        columns = pl.ds(pl.multiple_of(owner * PART, 128), PART)
        return remote(
            mods_part.at[chip], mods.at[:, columns], part_sems.at[0], part_sems.at[1], place
        )

    @pl.when(owns)
    def _():
        tall[...] = jnp.transpose(jax.nn.silu(condition))
        loosen(loose, tall)
        pltpu.make_async_copy(mods_weights, mods_weights, mods_recv.at[0]).wait()
        mods_part[...] = dot(loose[...].astype(BF16), mods_weights[...], TN)
        at.others(lambda device, place: part_copy(device, place).start())
        chip = pl.ds(pl.multiple_of(at.me // 2 * 8, 8), 8)
        columns = pl.ds(pl.multiple_of(owner * PART, 128), PART)
        pltpu.make_async_copy(mods_part.at[chip], mods.at[:, columns], part_sems.at[1]).start()

    of_first.around_square()
    of_first.close_square()
    of_first.arrive()
    pltpu.make_async_copy(mods, mods, part_sems.at[1]).wait()
    for i in range(1, ROWS_AXIS):
        for copy in code_copies(i):
            copy.wait_send()
    for i in range(1, 4):
        given_copy(i).wait()

    @pl.when(owns)
    def _():
        sent = time_weights.at[pl.ds(0, (OWNERS - 1) * PADDED // 3)]
        remote(sent, sent, mods_send.at[0], mods_recv.at[0], at.sibling).wait_send()

    @pl.when(jnp.logical_not(owns))
    def _():
        sent = time_weights.at[pl.ds(0, OWNERS * PADDED // 3)]
        remote(sent, sent, mods_send.at[0], mods_recv.at[0], at.sibling).wait_send()

    @pl.when(owns)
    def _():
        sent = first.at[0, pl.ds(0, (DEVICES - 1) * 16), pl.ds(0, PART)]
        remote(sent, sent, part_sems.at[0], part_sems.at[1], at.sibling).wait_send()

    for group in (of_piece, of_time, of_first):
        group.finish()


def gather_weights(*operands):
    dma = pltpu.SemaphoreType.DMA
    anywhere, inside = (
        pl.BlockSpec(memory_space=pl.ANY),
        pl.BlockSpec(memory_space=pltpu.VMEM),
    )
    return pl.pallas_call(
        gather_kernel,
        in_specs=[anywhere] * 3 + [inside] * 7,
        out_specs=[anywhere] + [inside] * 8,
        out_shape=[
            jax.ShapeDtypeStruct((4, D, D), BF16),
            jax.ShapeDtypeStruct((8, 8 * D), F32),
            jax.ShapeDtypeStruct((128, D), F32),
            jax.ShapeDtypeStruct((128, D), F32),
            jax.ShapeDtypeStruct((128, D), BF16),
            jax.ShapeDtypeStruct((PADDED, 128), F32),
            jax.ShapeDtypeStruct((128, FREQ), BF16),
            jax.ShapeDtypeStruct((128, 128), jnp.int32),
            jax.ShapeDtypeStruct((2 * PATCH_IN, PATCHES), F32),
        ],
        scratch_shapes=[
            pltpu.VMEM((BLOCK, 128), BF16),
            pltpu.VMEM((DEVICES, BLOCK, 128), BF16),
            pltpu.VMEM((DEVICES * PADDED, D), BF16),
            pltpu.VMEM((DEVICES * PADDED, PART), BF16),
            pltpu.VMEM((D, 128), F32),
            pltpu.VMEM((DEVICES * PADDED, 128), F32),
            pltpu.VMEM((128, PART), F32),
            dma((4,)),
            dma((4,)),
            dma((4, ROWS_AXIS)),
            dma((1,)),
            dma((1,)),
            dma((2,)),
            *spread_sems(3),
        ],
        compiler_params=pltpu.CompilerParams(
            collective_id=0, has_side_effects=True, vmem_limit_bytes=32 << 20
        ),
        name="gather_weights",
    )(*operands)


ORDER = (3, 0, 2, 1)


class Collect:
    def __init__(self, at, part, out, buffers, sems, cut):
        self.at, self.part, self.out, self.cut = at, part, out, cut
        self.own, self.got, self.near, self.far, self.line = buffers
        (
            self.own_sem,
            self.core_send,
            self.core_recv,
            self.near_send,
            self.near_recv,
            self.far_send,
            self.far_recv,
            self.line_send,
            self.line_recv,
        ) = sems
        self.other_y = 1 - at.y

    def start(self):
        at = self.at
        for z in ORDER:
            for y in (0, 1):
                for core in (0, 1):

                    def begin(keep, y=y, z=z, b=2 * y + core):
                        for source, first, rows in self.part(b, z):
                            self.move(y, z, pl.ds(first, rows), source, keep).start()

                    pl.when(at.c == core)(functools.partial(begin, True))
                    pl.when(at.c != core)(functools.partial(begin, False))

    def move(self, y, z, rows, source, keep):
        if keep:
            return pltpu.make_async_copy(source, self.own.at[y, rows], self.own_sem.at[y, z])
        return remote(
            source,
            self.got.at[y, rows],
            self.core_send.at[y, z],
            self.core_recv.at[y, z],
            self.at.sibling,
        )

    def whole_move(self, y, z, keep):
        rows = pl.ds(2 * z * BLOCK, 2 * BLOCK)
        return self.move(y, z, rows, self.got.at[y, rows], keep)

    def arrive(self, z):
        for y in (0, 1):
            self.whole_move(y, z, True).wait()
            self.whole_move(y, z, False).wait_recv()

    @staticmethod
    def rows_of(r, start, size):
        return pl.ds(pl.multiple_of(r * BLOCK + start, 16), size)

    @staticmethod
    def add(target, sources, size):
        def step(i, carry):
            total = None
            for ref, index, start in sources:
                tile = ref[index + (pl.ds(pl.multiple_of(start + 16 * i, 16), 16),)].astype(F32)
                total = tile if total is None else total + tile
            ref, index, start = target
            ref[index + (pl.ds(pl.multiple_of(start + 16 * i, 16), 16),)] = total.astype(ref.dtype)
            return carry

        lax.fori_loop(0, size // 16, step, 0)

    def near_copy(self, route, i):
        at, cut = self.at, self.cut
        if route == 0:
            source = self.own.at[self.other_y, self.rows_of(i, 0, cut)]
            target = self.near.at[i, pl.ds(0, cut)]
            device = at.across_y
        else:
            rows = self.rows_of(2 * (i // 2) + at.other_x, cut, BLOCK - cut)
            source = self.own.at[i % 2, rows]
            target = self.near.at[i, pl.ds(cut, BLOCK - cut)]
            device = at.across_x
        return remote(
            source, target, self.near_send.at[route], self.near_recv.at[route, i], device
        )

    def far_copy(self, route, z):
        at, cut = self.at, self.cut
        if route == 0:
            source = self.own.at[at.y, self.rows_of(2 * z + at.other_x, 0, cut)]
            target = self.far.at[z, pl.ds(0, cut)]
            device = at.across_x
        else:
            source = self.own.at[self.other_y, self.rows_of(2 * z + at.x, cut, BLOCK - cut)]
            target = self.far.at[z, pl.ds(cut, BLOCK - cut)]
            device = at.across_y
        return remote(source, target, self.far_send.at[route], self.far_recv.at[route, z], device)

    def near_stage(self, z):
        at, cut, own, got = self.at, self.cut, self.own, self.got
        self.arrive(z)

        def step(i, carry):
            for y, start, size, route in (
                (self.other_y, i * BLOCK, cut, 0),
                (i % 2, (2 * (i // 2) + at.other_x) * BLOCK + cut, BLOCK - cut, 1),
            ):
                self.add((own, (y,), start), [(own, (y,), start), (got, (y,), start)], size)
                self.near_copy(route, i).start()
            return carry

        lax.fori_loop(2 * z, 2 * z + 2, step, 0)

    def far_stage(self, z):
        at, cut, own, got = self.at, self.cut, self.own, self.got
        r, i = 2 * z + at.other_x, 2 * z + self.other_y
        for y, start, size, route, index, first in (
            (at.y, r * BLOCK, cut, 0, r, 0),
            (self.other_y, (2 * z + at.x) * BLOCK + cut, BLOCK - cut, 1, i, cut),
        ):
            self.near_copy(route, index).wait_recv()
            sources = [(own, (y,), start), (got, (y,), start), (self.near, (index,), first)]
            self.add((own, (y,), start), sources, size)
            self.far_copy(route, z).start()

    def line_copy(self, way, z):
        source = self.own.at[self.at.y, self.rows_of(2 * z + self.at.x, 0, BLOCK)]
        slot = z - 1 if way == 0 else z
        return remote(
            source,
            self.line.at[way, slot],
            self.line_send.at[way, slot],
            self.line_recv.at[way, slot],
            self.at.right if way == 0 else self.at.left,
        )

    def arrivals(self, z):
        self.near_copy(0, 2 * z + self.at.x).wait_recv()
        self.near_copy(1, 2 * z + self.at.y).wait_recv()
        self.far_copy(0, z).wait_recv()
        self.far_copy(1, z).wait_recv()

    def total(self, z, target, ways):
        at, cut = self.at, self.cut
        start = (2 * z + at.x) * BLOCK
        for route, begin, size in ((0, 0, cut), (1, cut, BLOCK - cut)):
            index = 2 * z + (at.x if route == 0 else at.y)
            sources = [
                (self.own, (at.y,), start + begin),
                (self.got, (at.y,), start + begin),
                (self.near, (index,), begin),
                (self.far, (z,), begin),
            ]
            for way in ways:
                sources.append((self.line, (way, z - 1 if way == 0 else z), begin))
            ref, place, base = target
            self.add((ref, place, base + begin), sources, size)

    def pass_on(self, way, z):
        at = self.at
        ahead = at.z > 0 if way == 0 else at.z < LINE - 1
        target = (self.own, (at.y,), (2 * z + at.x) * BLOCK)
        self.arrivals(z)

        @pl.when(ahead)
        def _():
            self.line_copy(way, z).wait_recv()
            self.total(z, target, (way,))

        pl.when(jnp.logical_not(ahead))(lambda: self.total(z, target, ()))
        self.line_copy(way, z).start()

    def line_stage(self, z):
        pl.when(self.at.z < z)(functools.partial(self.pass_on, 0, z))
        pl.when(self.at.z > z)(functools.partial(self.pass_on, 1, z))

    def last(self):
        at = self.at
        self.arrivals(at.z)
        for z in range(LINE):
            ways = ((0,) if z > 0 else ()) + ((1,) if z < LINE - 1 else ())

            @pl.when(at.z == z)
            def _(z=z, ways=ways):
                for way in ways:
                    self.line_copy(way, z).wait_recv()
                self.total(z, (self.out, (), 0), ways)

    def finish(self):
        at, cut = self.at, self.cut
        for y in (0, 1):
            for z in range(LINE):
                self.whole_move(y, z, False).wait_send()
        for route, size in ((0, cut), (1, BLOCK - cut)):
            rows = self.own.at[0, pl.ds(0, 2 * LINE * size)]
            sems = self.near_send.at[route], self.near_recv.at[route, 0]
            remote(rows, rows, *sems, at.sibling).wait_send()
            rows = self.own.at[0, pl.ds(0, LINE * size)]
            sems = self.far_send.at[route], self.far_recv.at[route, 0]
            remote(rows, rows, *sems, at.sibling).wait_send()
        for z in range(LINE):
            pl.when(at.z < z)(lambda: self.line_copy(0, z).wait_send())
            pl.when(at.z > z)(lambda: self.line_copy(1, z).wait_send())


class Share:
    def __init__(self, at, sums, shares, scratch):
        self.at, self.sums, self.shares = at, sums, shares
        self.stage, self.send, self.recv = scratch

    def copy(self, i):
        at = self.at
        b = (at.b + i) % 4
        target = self.shares.at[at.b]
        return remote(self.stage.at[b], target, self.send.at[i], self.recv.at[i], (at.r, b))

    def start(self):
        for j in range(4):
            self.stage[j, :OWN, :] = self.sums[OWN * j : OWN * (j + 1), :]
            self.stage[j, OWN:, :] = jnp.zeros((ROUNDED - OWN, D), F32)
        for i in range(1, 4):
            self.copy(i).start()
        self.shares[self.at.b] = self.stage[self.at.b]

    def finish(self):
        for i in range(1, 4):
            self.copy(i).wait()


def share_scratch():
    dma = pltpu.SemaphoreType.DMA
    return [pltpu.VMEM((4, ROUNDED, D), F32), dma((4,)), dma((4,))]


def collect_scratch():
    dma = pltpu.SemaphoreType.DMA
    return [
        pltpu.VMEM((2, D, D), BF16),
        pltpu.VMEM((2, D, D), BF16),
        pltpu.VMEM((2 * LINE, BLOCK, D), BF16),
        pltpu.VMEM((LINE, BLOCK, D), BF16),
        pltpu.VMEM((2, LINE - 1, BLOCK, D), BF16),
        dma((2, LINE)),
        dma((2, LINE)),
        dma((2, LINE)),
        dma((2,)),
        dma((2, 2 * LINE)),
        dma((2,)),
        dma((2, LINE)),
        dma((2, LINE - 1)),
        dma((2, LINE - 1)),
    ]


def scatter_kernel(
    query,
    key,
    value,
    output,
    slots_own,
    mods_weights,
    condition,
    totals_own,
    out,
    slots,
    grad_condition,
    totals,
    quarters,
    slots_block,
    pieces,
    tall,
    totals_got,
    band_send,
    band_recv,
    totals_send,
    totals_recv,
    slot_line_send,
    slot_line_recv,
    slot_sem,
    piece_sems,
    sums,
    *rest,
):
    at = Place()
    at.greet()
    own = rest[3]
    share = Share(at, sums, out, rest[:3])
    of_first = Collect(
        at,
        lambda b, z: [
            (
                (query, key, value, output)[b].at[pl.ds(2 * z * BLOCK, 2 * BLOCK)],
                2 * z * BLOCK,
                2 * BLOCK,
            )
        ],
        sums,
        rest[3:8],
        rest[8:],
        SPLIT[0],
    )

    def band_copy(i):
        b = (at.b + i) % 4
        columns = pl.ds(pl.multiple_of(b * 2 * D, 128), 2 * D)
        return remote(
            slots_own.at[:, columns],
            quarters.at[at.b],
            band_send.at[i],
            band_recv.at[i],
            (at.r, b),
        )

    def band_arrival(i):
        source = quarters.at[(at.b + 4 - i) % 4]
        return remote(source, source, band_send.at[i], band_recv.at[i], at.sibling)

    def in_slots(r, b, start, size):
        columns = pl.ds(pl.multiple_of(b * 2 * D + start, 128), size)
        return slots.at[pl.ds(pl.multiple_of(r * 16, 16), 16), columns]

    def sems(index):
        return slot_line_send.at[index], slot_line_recv.at[index], slot_sem.at[index]

    def bytes_of(rows, width):
        return own.at[0, pl.ds(0, rows), pl.ds(0, width)]

    of_slots = Spread(at, in_slots, slots_block, 2 * D, 16, D, bytes_of, sems(0))

    def piece_copy(place):
        mine = pieces.at[at.me]
        return remote(mine, mine, piece_sems.at[0], piece_sems.at[1], place)

    def share_slots():
        mine = pl.ds(pl.multiple_of(at.b * 2 * D, 128), 2 * D)
        total = slots_own[:, mine].astype(F32)
        for i in range(1, 4):
            band_arrival(i).wait_recv()
        for i in range(1, 4):
            total = total + quarters[(at.b + 4 - i) % 4].astype(F32)
        slots_block[...] = total.astype(BF16)
        of_slots.open()

    def condition_back():
        of_slots.arrive()
        grad = dot(mods_weights[...], slots[...], NT)
        sigmoid = 1.0 / (1.0 + jnp.exp(-condition[...]))
        grad = grad * (sigmoid * (1.0 + condition[...] * (1.0 - sigmoid)))
        pieces[at.me] = grad.astype(BF16)
        at.others(lambda _, place: piece_copy(place).start())

    def condition_arrives():
        others = pieces.at[pl.ds(0, DEVICES - 1)]
        remote(others, others, piece_sems.at[0], piece_sems.at[1], at.sibling).wait()
        compact(tall, pieces, 0)
        grad_condition[...] = jnp.transpose(tall[...]).astype(BF16)

    def near_line():
        return (at.r + 2 - 4 * (at.z % 2), at.b)

    def far_line():
        return (at.r + 4 - 8 * (at.z // 2), at.b)

    partners = (at.sibling, near_line(), far_line(), at.across_x, at.across_y)

    def totals_copy(step):
        return remote(
            totals_own if step == 0 else totals.at[step - 1],
            totals_got.at[step],
            totals_send.at[step],
            totals_recv.at[step],
            partners[step],
        )

    def totals_step(step):
        totals_copy(step).wait_recv()
        before = totals_own[...] if step == 0 else totals[step - 1]
        totals[step] = before + totals_got[step]
        if step + 1 < len(partners):
            totals_copy(step + 1).start()

    for i in range(1, 4):
        band_copy(i).start()
    totals_copy(0).start()
    of_first.start()
    share_slots()
    of_first.near_stage(3)
    totals_step(0)
    of_slots.along_line((1,))
    of_first.near_stage(0)
    of_slots.along_line((2,))
    of_slots.around_square((0,))
    of_first.far_stage(3)
    of_first.near_stage(2)
    of_slots.along_line((3,))
    of_slots.around_square((1,))
    of_first.far_stage(0)
    totals_step(1)
    of_first.near_stage(1)
    of_slots.around_square((2,))
    of_slots.close_square((0,))
    of_slots.around_square((3,))
    of_first.line_stage(3)
    of_slots.close_square((1,))
    totals_step(2)
    of_first.far_stage(2)
    of_slots.close_square((2, 3))
    of_first.line_stage(0)
    condition_back()
    of_first.far_stage(1)
    totals_step(3)
    of_first.line_stage(2)
    of_first.line_stage(1)
    of_first.last()
    share.start()
    condition_arrives()
    totals_step(4)
    of_first.finish()
    share.finish()
    for i in range(1, 4):
        band_copy(i).wait_send()
    for step in range(len(partners)):
        totals_copy(step).wait_send()
    of_slots.finish()


def scatter_sums(matrices, slots_own, mods_weights, condition, totals_own):
    dma = pltpu.SemaphoreType.DMA
    anywhere, inside = (
        pl.BlockSpec(memory_space=pl.ANY),
        pl.BlockSpec(memory_space=pltpu.VMEM),
    )
    steps = 5
    return pl.pallas_call(
        scatter_kernel,
        in_specs=[anywhere] * 4 + [inside] * 4,
        out_specs=[inside] * 4,
        out_shape=[
            jax.ShapeDtypeStruct((4, ROUNDED, D), F32),
            jax.ShapeDtypeStruct((128, 8 * D), BF16),
            jax.ShapeDtypeStruct((128, D), BF16),
            jax.ShapeDtypeStruct((steps, *totals_own.shape), F32),
        ],
        scratch_shapes=[
            pltpu.VMEM((4, 16, 2 * D), BF16),
            pltpu.VMEM((16, 2 * D), BF16),
            pltpu.VMEM((DEVICES, PADDED, 128), BF16),
            pltpu.VMEM((D, 128), F32),
            pltpu.VMEM((steps, *totals_own.shape), F32),
            dma((4,)),
            dma((4,)),
            dma((steps,)),
            dma((steps,)),
            *spread_sems(1),
            dma((2,)),
            pltpu.VMEM((BLOCK, D), F32),
            *share_scratch(),
            *collect_scratch(),
        ],
        compiler_params=pltpu.CompilerParams(
            collective_id=1, has_side_effects=True, vmem_limit_bytes=61 << 20
        ),
        name="scatter_sums",
    )(*matrices, slots_own, mods_weights, condition, totals_own)


def attend_kernel(apart, q_ref, k_ref, v_ref, *rest, travels):
    head = pl.program_id(0)
    if travels:
        up_own, out_ref, log_ref, up, line_send, line_recv, spread_sem = rest
        at = Place()

        def in_up(r, b, start, size):
            rows = pl.ds(pl.multiple_of(r * BLOCK + start, 16), size)
            return up.at[rows, pl.ds(pl.multiple_of(b * D, 128), D)]

        def bytes_of(rows, width):
            return up.at[pl.ds(0, rows // 4), :]

        sems = line_send.at[0], line_recv.at[0], spread_sem.at[0]
        of_up = Spread(at, in_up, up_own, BLOCK, D, SPLIT[1], bytes_of, sems)

        def begin():
            at.greet()
            of_up.open()

        at_step(head, 0, begin)
        for step in (1, 2, 3):
            at_step(head, 1 + 2 * step, lambda: of_up.along_line((step,)))
        for step in range(4):
            at_step(head, 4 + 2 * step, lambda: of_up.around_square((step,)))
            at_step(head, 8 + 2 * step, lambda: of_up.close_square((step,)))
    else:
        out_ref, log_ref = rest
    attend_head(head, apart, q_ref, k_ref, v_ref, out_ref, log_ref, min(512, q_ref.shape[0]))
    if travels:

        def end():
            of_up.arrive()
            of_up.finish()

        at_step(head, HEADS - 1, end)


def attend_back_kernel(apart, q_ref, k_ref, v_ref, grad_ref, log_ref, *rest, travels):
    head = pl.program_id(0)
    if travels:
        up_grad, dq_ref, dk_ref, dv_ref, shares, sums, *rest = rest
        at = Place()
        share = Share(at, sums, rest[3], rest[:3])

        def part(b, z):
            rows = pl.ds(2 * z * BLOCK, 2 * BLOCK)
            return [(up_grad.at[rows, pl.ds(b * D, D)], 2 * z * BLOCK, 2 * BLOCK)]

        of_up = Collect(at, part, sums, rest[4:9], rest[9:], SPLIT[1])

        def begin():
            at.greet()
            of_up.start()

        at_step(head, 0, begin)
        for step, z in ((2, 3), (3, 0), (6, 2), (8, 1)):
            at_step(head, step, lambda: of_up.near_stage(z))
        for step, z in ((6, 3), (8, 0), (11, 2), (13, 1)):
            at_step(head, step, lambda: of_up.far_stage(z))
        for step, z in ((10, 3), (12, 0), (14, 2)):
            at_step(head, step, lambda: of_up.line_stage(z))
    else:
        dq_ref, dk_ref, dv_ref = rest
    attend_back_head(
        head, apart, q_ref, k_ref, v_ref, grad_ref, log_ref, dq_ref, dk_ref, dv_ref
    )
    if travels:

        def end():
            of_up.line_stage(1)
            of_up.last()
            share.start()
            of_up.finish()
            share.finish()
            shares[...] = rest[3][...]

        at_step(head, HEADS - 1, end)


def attend(apart, queries, keys, values, up_own):
    q_len, k_len = queries.shape[0], keys.shape[0]
    travels = up_own is not None
    anywhere = pl.BlockSpec(memory_space=pl.ANY)
    return pl.pallas_call(
        functools.partial(attend_kernel, travels=travels),
        grid=(HEADS,),
        in_specs=[
            whole_block(apart.shape),
            whole_block((q_len, D)),
            whole_block((k_len, D)),
            whole_block((k_len, D)),
        ]
        + [anywhere] * travels,
        out_specs=[whole_block((q_len, D)), whole_block((HEADS, q_len))] + [anywhere] * travels,
        out_shape=[
            jax.ShapeDtypeStruct((q_len, D), BF16),
            jax.ShapeDtypeStruct((HEADS, q_len), F32),
        ]
        + [jax.ShapeDtypeStruct((D, FF), BF16)] * travels,
        scratch_shapes=spread_sems(1) if travels else [],
        compiler_params=pltpu.CompilerParams(
            vmem_limit_bytes=56 << 20,
            **(dict(collective_id=2, has_side_effects=True) if travels else {}),
        ),
        name="attend_rows",
    )(apart, queries, keys, values, *((up_own,) if travels else ()))


def attend_back(apart, queries, keys, values, grads, log_total, up_grad):
    q_len, k_len = queries.shape[0], keys.shape[0]
    travels = up_grad is not None
    anywhere = pl.BlockSpec(memory_space=pl.ANY)
    return pl.pallas_call(
        functools.partial(attend_back_kernel, travels=travels),
        grid=(HEADS,),
        in_specs=[
            whole_block(apart.shape),
            whole_block((q_len, D)),
            whole_block((k_len, D)),
            whole_block((k_len, D)),
            whole_block((q_len, D)),
            whole_block((HEADS, q_len)),
        ]
        + [anywhere] * travels,
        out_specs=[whole_block((q_len, D)), whole_block((k_len, D)), whole_block((k_len, D))]
        + [whole_block((4, ROUNDED, D))] * travels,
        out_shape=[
            jax.ShapeDtypeStruct((q_len, D), BF16),
            jax.ShapeDtypeStruct((k_len, D), BF16),
            jax.ShapeDtypeStruct((k_len, D), BF16),
        ]
        + [jax.ShapeDtypeStruct((4, ROUNDED, D), F32)] * travels,
        scratch_shapes=[
            pltpu.VMEM((BLOCK, D), F32),
            *share_scratch(),
            pltpu.VMEM((4, ROUNDED, D), F32),
            *collect_scratch(),
        ]
        if travels
        else [],
        compiler_params=pltpu.CompilerParams(
            vmem_limit_bytes=61 << 20,
            **(dict(collective_id=3, has_side_effects=True) if travels else {}),
        ),
        name="attend_rows_back",
    )(apart, queries, keys, values, grads, log_total, *((up_grad,) if travels else ()))


def mlp_kernel(normed, up, bias, down, active, slope, branch):
    tile = pl.program_id(0)
    values = dot(normed[...], up[...], NN) + bias[...]
    square = values * values
    curve = jnp.tanh(GELU_ROOT * values * (1.0 + GELU_CUBE * square))
    half = 0.5 * (1.0 + curve)
    acting = (values * half).astype(BF16)
    active[...] = acting
    steep = values * (GELU_ROOT + 3.0 * GELU_ROOT * GELU_CUBE * square)
    slope[...] = (half + half * (1.0 - curve) * steep).astype(BF16)
    part = dot(acting, down[...], NN)

    @pl.when(tile == 0)
    def _():
        branch[...] = part

    @pl.when(tile > 0)
    def _():
        branch[...] += part


def mlp(normed, up, bias, down):
    rows, tile = normed.shape[0], 768
    by_tile = pl.BlockSpec((rows, tile), lambda i: (0, i))
    return pl.pallas_call(
        mlp_kernel,
        grid=(FF // tile,),
        in_specs=[
            whole_block((rows, D)),
            pl.BlockSpec((D, tile), lambda i: (0, i)),
            pl.BlockSpec((1, tile), lambda i: (0, i)),
            pl.BlockSpec((tile, D), lambda i: (i, 0)),
        ],
        out_specs=[by_tile, by_tile, whole_block((rows, D))],
        out_shape=[
            jax.ShapeDtypeStruct((rows, FF), BF16),
            jax.ShapeDtypeStruct((rows, FF), BF16),
            jax.ShapeDtypeStruct((rows, D), F32),
        ],
        compiler_params=pltpu.CompilerParams(vmem_limit_bytes=56 << 20),
        name="mlp",
    )(normed, up, bias, down)


def mlp_back_kernel(
    grad,
    normed,
    slope,
    down,
    up,
    down_grad,
    grad_normed,
    up_grad,
    bias_grad,
    down_sum,
    turned,
    *rest,
):
    tile = pl.program_id(0)
    at = Place()

    def part(b, z):
        return [
            (down_grad.at[pl.ds((4 * r + b) * BLOCK, BLOCK)], r * BLOCK, BLOCK)
            for r in (2 * z, 2 * z + 1)
        ]

    of_down = Collect(at, part, down_sum, rest[:5], rest[5:], SPLIT[0])

    def begin():
        at.greet()
        of_down.start()
        turned[...] = jnp.transpose(normed[...])
        grad_normed[...] = jnp.zeros_like(grad_normed)

    at_step(tile, 0, begin)
    for step, z in ((1, 3), (1, 0), (3, 2), (4, 1)):
        at_step(tile, step, lambda: of_down.near_stage(z))
    for step, z in ((3, 3), (4, 0), (6, 2), (7, 1)):
        at_step(tile, step, lambda: of_down.far_stage(z))
    for step, z in ((6, 3), (7, 0), (8, 2)):
        at_step(tile, step, lambda: of_down.line_stage(z))

    grad_active = dot(grad[...], down[...], NT)
    grad_up = (grad_active * slope[...].astype(F32)).astype(BF16)
    bias_grad[...] = jnp.sum(grad_up.astype(F32), axis=0, keepdims=True)
    up_grad[...] = dot(turned[...], grad_up, NN).astype(BF16)
    grad_normed[...] += dot(grad_up, up[...], NT)

    def end():
        of_down.line_stage(1)
        of_down.last()
        of_down.finish()

    at_step(tile, pl.num_programs(0) - 1, end)


def mlp_back(grad, normed, slope, down, up, down_grad):
    rows, tile = grad.shape[0], 512
    return pl.pallas_call(
        mlp_back_kernel,
        grid=(FF // tile,),
        in_specs=[
            whole_block((rows, D)),
            whole_block((rows, D)),
            pl.BlockSpec((rows, tile), lambda i: (0, i)),
            pl.BlockSpec((tile, D), lambda i: (i, 0)),
            pl.BlockSpec((D, tile), lambda i: (0, i)),
            pl.BlockSpec(memory_space=pl.ANY),
        ],
        out_specs=[
            whole_block((rows, D)),
            pl.BlockSpec((D, tile), lambda i: (0, i)),
            pl.BlockSpec((1, tile), lambda i: (0, i)),
            whole_block((BLOCK, D)),
        ],
        out_shape=[
            jax.ShapeDtypeStruct((rows, D), F32),
            jax.ShapeDtypeStruct((D, FF), BF16),
            jax.ShapeDtypeStruct((1, FF), F32),
            jax.ShapeDtypeStruct((BLOCK, D), F32),
        ],
        scratch_shapes=[pltpu.VMEM((D, rows), BF16)] + collect_scratch(),
        compiler_params=pltpu.CompilerParams(
            vmem_limit_bytes=61 << 20, collective_id=4, has_side_effects=True
        ),
        name="mlp_back",
    )(grad, normed, slope, down, up, down_grad)


def matmul(operand, weights):
    return jnp.einsum("...i,ij->...j", operand, weights, preferred_element_type=F32)


def matmul_back(gradient, weights):
    return jnp.einsum("...j,ij->...i", gradient, weights, preferred_element_type=F32)


def outer_sum(operand, gradient):
    return jnp.einsum(
        "ni,nj->ij",
        operand.reshape(-1, operand.shape[-1]),
        gradient.reshape(-1, gradient.shape[-1]),
        preferred_element_type=F32,
    )


def column_sum(gradient):
    return jnp.sum(gradient.reshape(-1, gradient.shape[-1]), axis=0, dtype=F32)


def silu_back(values, gradient):
    return jax.vjp(jax.nn.silu, values)[1](gradient)[0]


def plan(time_steps):
    steps_all = jnp.arange(TIMESTEPS, dtype=jnp.int32)
    betas = BETA_LOW + (BETA_HIGH - BETA_LOW) * steps_all.astype(F32) / (TIMESTEPS - 1)
    cumulate = jnp.cumsum(jnp.log1p(-betas))
    pick_now = (time_steps[..., None] == steps_all).astype(F32)
    pick_prev = (time_steps[..., None] - 1 == steps_all).astype(F32)
    return jnp.stack(
        [
            jnp.sum(pick_now * betas, axis=-1),
            jnp.sum(pick_now * cumulate, axis=-1),
            jnp.sum(pick_prev * cumulate, axis=-1),
        ],
        axis=-1,
    )


def time_features(time_steps):
    half_width = FREQ // 2
    frequency = jnp.exp(-math.log(10000.0) * jnp.arange(half_width).astype(F32) / half_width)
    angles = time_steps.astype(F32)[..., None] * frequency
    return jnp.concatenate([jnp.cos(angles), jnp.sin(angles)], axis=-1)


def positions(four_way):
    quarter = D // 4
    omegas = jnp.exp(-math.log(10000.0) * jnp.arange(quarter).astype(F32) / quarter)
    angles = jnp.arange(GRID).astype(F32)[:, None] * omegas
    table = jnp.concatenate([jnp.sin(angles), jnp.cos(angles)], axis=-1)

    def grid(side):
        shape = (PATCHES // side**2, side, side, D // 2)
        down = jnp.broadcast_to(table[None, :side, None], shape)
        across = jnp.broadcast_to(table[None, None, :side], shape)
        return jnp.concatenate([down, across], axis=-1).reshape(SLOTS, SEGMENT, D)

    return jnp.where(four_way, grid(GRID // 2), grid(GRID))


def layer_norm(values):
    centered = values - jnp.mean(values, axis=-1, keepdims=True)
    return centered * lax.rsqrt(jnp.mean(centered * centered, axis=-1, keepdims=True) + NORM_EPS)


def modulate(values, shift, scaling):
    return layer_norm(values) * (1.0 + scaling) + shift


def patch_loss(output, target_noise, patch_sched):
    beta = patch_sched[..., 0:1]
    log_now = patch_sched[..., 1:2]
    log_prev = patch_sched[..., 2:3]
    error = output[..., :PATCH_IN] - target_noise
    log_beta = jnp.log(beta)
    keep_now = -jnp.expm1(log_now)
    log_post = log_beta + jnp.log(-jnp.expm1(log_prev)) - jnp.log(keep_now)
    coefficient = beta * lax.rsqrt(keep_now * (1.0 - beta))
    fraction = 0.5 * (output[..., PATCH_IN:] + 1.0)
    log_model = fraction * log_beta + (1.0 - fraction) * log_post
    diverge = 0.5 * (
        -1.0
        + log_model
        - log_post
        + jnp.exp(log_post - log_model)
        + (coefficient * error) ** 2 * jnp.exp(-log_model)
    )
    return jnp.mean(error * error, axis=-1) + jnp.mean(diverge, axis=-1) / math.log(2.0)


def adamw_step(weight, first_old, second_old, gradient, step_rate):
    first_new = DECAY_FIRST * first_old + (1.0 - DECAY_FIRST) * gradient
    second_new = DECAY_SECOND * second_old + (1.0 - DECAY_SECOND) * gradient * gradient
    first_hat = first_new / (1.0 - DECAY_FIRST**STEP)
    second_hat = second_new / (1.0 - DECAY_SECOND**STEP)
    return (
        weight - step_rate * first_hat / (jnp.sqrt(second_hat) + ADAM_EPS),
        first_new,
        second_new,
    )


def body(
    sizes,
    latents,
    gauss_noise,
    image_counts,
    timesteps,
    labels,
    wide_weights,
    square_weights,
    down_weights,
    embed_tables,
    all_biases,
    head_weights,
    first_wide,
    first_square,
    first_down,
    first_tables,
    first_biases,
    first_head,
    second_wide,
    second_square,
    second_down,
    second_tables,
    second_biases,
    second_head,
):
    n_rows, n_band = sizes
    n_all = n_rows * n_band
    rows_here, band_len, _ = latents.shape
    share = n_band // rows_here
    part_len = PATCHES // share
    at_row, at_band = lax.axis_index("rows"), lax.axis_index("band")
    own_row = at_band // share
    part_start = (at_band % share) * part_len
    n_slots = n_rows * rows_here * SLOTS
    groups = [[row * share + i for i in range(share)] for row in range(rows_here)]

    def in_row_gather(array):
        if share == 1:
            return array
        return lax.all_gather(array, "band", axis=0, tiled=True, axis_index_groups=groups)

    def in_row_scatter(array):
        if share == 1:
            return array
        return lax.psum_scatter(
            array, "band", scatter_dimension=0, tiled=True, axis_index_groups=groups
        )

    def in_row_sum(array):
        if share == 1:
            return array
        return lax.psum(array, "band", axis_index_groups=groups)

    tuned = sizes == (ROWS_AXIS, DEVICES // ROWS_AXIS)
    n_seg = part_len // SEGMENT
    given = jnp.concatenate([latents, gauss_noise], axis=-1)
    count = lax.dynamic_slice_in_dim(image_counts, own_row, 1)[0]
    four_way = count == SLOTS
    seg_first = part_start // SEGMENT + jnp.arange(n_seg)
    seg_slot = jnp.where(four_way, seg_first, 0)
    seg_hot = (seg_slot[:, None] == jnp.arange(SLOTS)).astype(F32)

    def by_segment(per_slot):
        return jnp.sum(seg_hot[:, :, None] * per_slot[None], axis=1)[:, None]

    wide_low = wide_weights.astype(BF16)
    square_low = square_weights.astype(BF16)
    down_low = down_weights.astype(BF16)
    tables_low = embed_tables.astype(BF16)
    biases_low = all_biases.astype(BF16)
    mods_low = wide_low[:, 3 * D + FF :]
    time_out_low = square_low[:, D:]
    first_group = jnp.concatenate([wide_low[:, : 3 * D], square_low[:, :D]], axis=1)
    up_group = wide_low[:, 3 * D : 3 * D + FF]
    head_low = head_weights.astype(BF16)
    head_matrix = head_low[:D]
    small_rows = jnp.concatenate([biases_low, tables_low[FREQ : FREQ + PATCH_IN]], axis=0)
    device = at_row * n_band + at_band
    if tuned:
        padded = lambda array: jnp.pad(array, ((0, PADDED - OWN), (0, 0)))
        quarters = [first_group.reshape(-1, 4, D), up_group.reshape(-1, 4, D)]
        quarters = lax.all_to_all(
            jnp.concatenate(quarters, axis=2), "band", split_axis=1, concat_axis=0, tiled=True
        )[:, 0]
        own_times = timesteps.reshape(-1)
        codes = (labels + 1024 * image_counts[:, None]).reshape(-1, 1)
        own_codes = jnp.broadcast_to(codes, (rows_here * SLOTS, 128))
        class_columns = jnp.pad(tables_low[FREQ + PATCH_IN :].T, ((0, 0), (0, 1024 - CLASSES)))
        (
            first_all,
            mods,
            condition_all,
            small_all,
            time_act_all,
            time_pre,
            frequency,
            codes,
            given,
        ) = gather_weights(
            quarters[:, :D],
            padded(time_out_low),
            padded(mods_low),
            time_features(own_times).astype(BF16),
            own_codes,
            padded(tables_low[:FREQ].T),
            jnp.broadcast_to(padded(biases_low[1][:, None].astype(F32)), (PADDED, 128)),
            padded(class_columns),
            jnp.pad(small_rows.T, ((0, PADDED - OWN), (0, 128 - small_rows.shape[0]))),
            given.transpose(0, 2, 1),
        )
        given = given.T
        up_own = quarters[:, D:]
        down_own, first_all = lax.optimization_barrier((down_low, first_all))
        down_all = lax.all_gather(down_own, AXES, axis=0, tiled=True)
        weight_q, weight_k, weight_v, weight_o = first_all
        biases = small_all[: all_biases.shape[0]]
        patch_in = small_all[all_biases.shape[0] :][:PATCH_IN].astype(BF16)
        mods = lax.dynamic_slice_in_dim(mods, (at_band % 2) * SLOTS, SLOTS, 0)
        own_columns = lambda array: lax.dynamic_slice_in_dim(array, device * OWN, OWN, 1)
        condition = own_columns(condition_all)
        time_act = own_columns(time_act_all)
        time_pre = time_pre[:OWN].T
        labels_all = codes[:, 0] & 1023
        images = (jnp.sum(codes[:, 0] >> 10) // SLOTS).astype(F32)
        cond_act = jax.nn.silu(condition).astype(BF16)
    else:
        given = lax.all_gather(given, "band", axis=1, tiled=True)
        given = lax.dynamic_slice_in_dim(given, own_row, 1, 0)[0]
        given = lax.dynamic_slice_in_dim(given, part_start, part_len, 0)
        codes = jnp.concatenate([timesteps, labels, image_counts[:, None]], axis=1)
        codes = lax.all_gather(codes, "rows", axis=0, tiled=True)
        labels_all = codes[:, SLOTS : 2 * SLOTS].reshape(n_slots)
        images = jnp.sum(codes[:, 2 * SLOTS]).astype(F32)
        frequency = time_features(codes[:, :SLOTS].reshape(n_slots)).astype(BF16)
        first_all = lax.all_gather(first_group, AXES, axis=0, tiled=True)
        up_all = lax.all_gather(up_group, AXES, axis=0, tiled=True)
        down_all = lax.all_gather(down_low, AXES, axis=0, tiled=True)
        weight_q, weight_k, weight_v, weight_o = jnp.split(first_all, 4, axis=1)
        small_all = lax.all_gather(small_rows, AXES, axis=1, tiled=True)
        biases = small_all[: all_biases.shape[0]].astype(F32)
        patch_in = small_all[all_biases.shape[0] :]
        own_biases = biases_low.astype(F32)
        time_pre = matmul(frequency, tables_low[:FREQ]) + own_biases[1]
        time_act = jax.nn.silu(time_pre).astype(BF16)
        class_rows = tables_low[FREQ + PATCH_IN :]
        class_part = class_rows[labels_all].astype(F32)
        time_out_columns = lax.all_to_all(
            time_out_low, AXES, split_axis=1, concat_axis=0, tiled=True
        )
        time_act_all = lax.all_gather(time_act, AXES, axis=1, tiled=True)
        condition = matmul(time_act_all, time_out_columns) + own_biases[2] + class_part
        cond_act = jax.nn.silu(condition).astype(BF16)
        mods_columns = lax.all_to_all(mods_low, AXES, split_axis=1, concat_axis=0, tiled=True)
        cond_act_all = lax.all_gather(cond_act, AXES, axis=1, tiled=True)
        mods_part = matmul(cond_act_all, mods_columns)
        mods_part = mods_part.reshape(n_rows * rows_here, SLOTS, -1)
        if share > 1:
            mods_part = jnp.repeat(mods_part, share, axis=0)
        mods = lax.all_to_all(mods_part, AXES, split_axis=0, concat_axis=2, tiled=True)[0]
    label_hot = (labels_all[:, None] == jnp.arange(CLASSES, dtype=jnp.int32)).astype(BF16)
    mods_bias = jnp.concatenate([biases[3:9].reshape(-1), biases[17:19].reshape(-1)])
    seg_mods = by_segment(mods + mods_bias)
    (
        shift_one,
        scale_one,
        gate_one,
        shift_two,
        scale_two,
        gate_two,
        final_shift,
        final_scale,
    ) = jnp.split(seg_mods, 8, axis=-1)

    given = given.reshape(n_seg, SEGMENT, 2 * PATCH_IN)
    row_latents, row_noise = given[..., :PATCH_IN], given[..., PATCH_IN:]
    own_times = lax.dynamic_slice_in_dim(timesteps, own_row, 1, 0)[0]
    patch_sched = by_segment(plan(own_times))
    log_now = patch_sched[..., 1:2]
    noisy = (
        jnp.exp(0.5 * log_now) * row_latents + jnp.sqrt(-jnp.expm1(log_now)) * row_noise
    ).astype(BF16)
    position = lax.dynamic_slice_in_dim(positions(four_way), part_start // SEGMENT, n_seg, 0)
    hidden_zero = matmul(noisy, patch_in) + biases[0] + position
    normed_one = modulate(hidden_zero, shift_one, scale_one).astype(BF16)
    flat = lambda array: array.reshape(part_len, array.shape[-1])
    deep = lambda array: array.reshape(n_seg, SEGMENT, array.shape[-1])
    queries = flat(matmul(normed_one, weight_q) + biases[9]).astype(BF16)
    keys = flat(matmul(normed_one, weight_k)).astype(BF16)
    values = flat(matmul(normed_one, weight_v) + biases[10]).astype(BF16)
    keys, values = in_row_gather(keys), in_row_gather(values)
    key_seg = jnp.where(four_way, jnp.arange(SLOTS), 0)
    apart = jnp.where(key_seg[:, None] == jnp.repeat(seg_slot, SEGMENT), 0.0, -1e30).astype(F32)
    if tuned:
        attended, log_total, up_all = attend(apart, queries, keys, values, up_own)
    else:
        attended, log_total = attend(apart, queries, keys, values, None)
    attended = deep(attended)
    branch_one = matmul(attended, weight_o) + biases[11]
    hidden_one = hidden_zero + gate_one * branch_one
    normed_two = modulate(hidden_one, shift_two, scale_two).astype(BF16)
    up_bias = biases[12:16].reshape(-1)
    if tuned:
        active, slope, branch_two = mlp(flat(normed_two), up_all, up_bias[None], down_all)
        active, branch_two = deep(active), deep(branch_two) + biases[16]
    else:
        upward = matmul(normed_two, up_all) + up_bias
        active = jax.nn.gelu(upward, approximate=True).astype(BF16)
        branch_two = matmul(active, down_all) + biases[16]
    hidden_two = hidden_one + gate_two * branch_two
    normed_out = modulate(hidden_two, final_shift, final_scale).astype(BF16)
    output = matmul(normed_out, head_matrix) + head_low[D].astype(F32)
    patch_share = jnp.where(four_way, 1.0 / SEGMENT, 1.0 / PATCHES)
    losses, loss_back = jax.vjp(lambda at: patch_loss(at, row_noise, patch_sched), output)
    loss_local = jnp.sum(patch_share * losses)

    grad_out = loss_back(jnp.broadcast_to(patch_share / images, losses.shape))[0].astype(BF16)
    grad_two, grad_fshift, grad_fscale = jax.vjp(modulate, hidden_two, final_shift, final_scale)[1](
        matmul_back(grad_out, head_matrix)
    )
    seg_sum = lambda array: jnp.sum(array, axis=1, keepdims=True)
    grad_gate_two = seg_sum(grad_two * branch_two)
    grad_branch_two = (gate_two * grad_two).astype(BF16)
    down_grad = outer_sum(active, grad_branch_two)
    if tuned:
        grad_normed_two, up_grad, up_bias_grad, down_sum = mlp_back(
            flat(grad_branch_two),
            flat(normed_two),
            slope,
            down_all,
            up_all,
            down_grad.astype(BF16),
        )
        grad_normed_two, up_bias_grad = deep(grad_normed_two), up_bias_grad[0]
    else:
        grad_active = matmul_back(grad_branch_two, down_all)
        grad_upward = jax.vjp(lambda at: jax.nn.gelu(at, approximate=True), upward)[1](
            grad_active
        )[0].astype(BF16)
        up_grad = outer_sum(normed_two, grad_upward)
        up_bias_grad = column_sum(grad_upward)
        grad_normed_two = matmul_back(grad_upward, up_all)
    grad_one_part, grad_shift_two, grad_scale_two = jax.vjp(
        modulate, hidden_one, shift_two, scale_two
    )[1](grad_normed_two)
    grad_one = grad_two + grad_one_part
    grad_gate_one = seg_sum(grad_one * branch_one)
    grad_branch_one = (gate_one * grad_one).astype(BF16)
    output_grad = outer_sum(attended, grad_branch_one)
    grad_attended = flat(matmul_back(grad_branch_one, weight_o).astype(BF16))
    if tuned:
        grad_query, grad_key, grad_value, up_sum = attend_back(
            apart, queries, keys, values, grad_attended, log_total, up_grad
        )
    else:
        grad_query, grad_key, grad_value = attend_back(
            apart, queries, keys, values, grad_attended, log_total, None
        )
    grad_key, grad_value = in_row_scatter(grad_key), in_row_scatter(grad_value)
    q_grad = outer_sum(normed_one, grad_query)
    k_grad = outer_sum(normed_one, grad_key)
    v_grad = outer_sum(normed_one, grad_value)
    grad_normed = deep(
        matmul_back(grad_query, weight_q)
        + matmul_back(grad_key, weight_k)
        + matmul_back(grad_value, weight_v)
    )
    grad_zero_part, grad_shift_one, grad_scale_one = jax.vjp(
        modulate, hidden_zero, shift_one, scale_one
    )[1](grad_normed)
    grad_zero = (grad_one + grad_zero_part).astype(BF16)
    patch_grad = outer_sum(noisy, grad_zero)

    seg_grads = jnp.concatenate(
        [
            grad_shift_one,
            grad_scale_one,
            grad_gate_one,
            grad_shift_two,
            grad_scale_two,
            grad_gate_two,
            grad_fshift,
            grad_fscale,
        ],
        axis=-1,
    )
    slot_grads = in_row_sum(jnp.sum(seg_hot[:, :, None] * seg_grads, axis=0)).astype(BF16)
    last_row = jnp.concatenate([column_sum(grad_out), loss_local[None]])
    totals = jnp.concatenate(
        [
            column_sum(grad_zero)[None],
            column_sum(grad_query)[None],
            column_sum(grad_value)[None],
            column_sum(grad_branch_one)[None],
            up_bias_grad.reshape(FF // D, D),
            column_sum(grad_branch_two)[None],
            patch_grad,
            outer_sum(grad_out, normed_out),
            jnp.pad(last_row, (0, D - last_row.shape[0]))[None],
        ],
        axis=0,
    )
    if tuned:
        slots_own = jnp.where(
            (jnp.arange(4 * SLOTS) // SLOTS == at_band)[:, None], jnp.tile(slot_grads, (4, 1)), 0
        ).astype(BF16)
        matrices = (q_grad, k_grad, v_grad, output_grad)
        down_grad = down_sum
        sums, slot_grads, grad_condition_all, totals = scatter_sums(
            [array.astype(BF16) for array in matrices],
            slots_own,
            padded(mods_low),
            padded(condition.T),
            jnp.pad(totals, ((0, -totals.shape[0] % 8), (0, 0))),
        )
        totals = totals[-1]
        first_grad, up_grad = (
            shares[:, :OWN].transpose(1, 0, 2).reshape(OWN, 4 * D) for shares in (sums, up_sum)
        )
        local_squares = sum(jnp.sum(array * array) for array in (first_grad, up_grad, down_grad))
        grad_condition = own_columns(grad_condition_all)
    else:
        slot_grads = lax.all_gather(slot_grads, AXES, axis=0, tiled=True)
        if share > 1:
            slot_grads = slot_grads.reshape(-1, share, SLOTS, 8 * D)[:, 0].reshape(n_slots, 8 * D)
        grad_condition = silu_back(condition, matmul_back(slot_grads, mods_low)).astype(BF16)
        grad_condition_all = lax.all_gather(grad_condition, AXES, axis=1, tiled=True)

        def scatter(array):
            return lax.psum_scatter(array, AXES, scatter_dimension=0, tiled=True)

        first_grad = scatter(jnp.concatenate([q_grad, k_grad, v_grad, output_grad], axis=1))
        up_grad = scatter(up_grad)
        down_grad = scatter(down_grad)
        local_squares = sum(jnp.sum(array * array) for array in (first_grad, up_grad, down_grad))
        totals = lax.psum(totals, AXES)
    mods_grad = outer_sum(cond_act, slot_grads)
    mods_bias_grad = column_sum(slot_grads).reshape(8, n_all, -1)
    time_out_grad = outer_sum(time_act, grad_condition_all)
    class_grad = outer_sum(label_hot, grad_condition)
    grad_time_pre = silu_back(time_pre, matmul_back(grad_condition_all, time_out_low)).astype(BF16)
    time_in_grad = outer_sum(frequency, grad_time_pre)
    n_sums = 9 + PATCH_IN
    own_width = D // n_all
    row_grads = lax.dynamic_slice_in_dim(totals[:n_sums], device * own_width, own_width, 1)
    head_total = jnp.concatenate(
        [totals[n_sums : n_sums + 32].T, totals[n_sums + 32, :32][None]], axis=0
    )
    loss_sum = totals[n_sums + 32, 32]
    own_mods_bias = lax.dynamic_index_in_dim(mods_bias_grad, device, 1, keepdims=False)
    grad_wide = jnp.concatenate([first_grad[:, : 3 * D], up_grad, mods_grad], axis=1)
    grad_square = jnp.concatenate([first_grad[:, 3 * D :], time_out_grad], axis=1)
    grad_tables = jnp.concatenate([time_in_grad, row_grads[9:], class_grad], axis=0)
    grad_biases = jnp.concatenate(
        [
            row_grads[:1],
            column_sum(grad_time_pre)[None],
            column_sum(grad_condition)[None],
            own_mods_bias[:6],
            row_grads[1:9],
            own_mods_bias[6:],
        ],
        axis=0,
    )
    owned_grads = (grad_wide, grad_square, down_grad, grad_tables, grad_biases)
    for array in (mods_grad, time_out_grad, grad_tables, grad_biases):
        local_squares = local_squares + jnp.sum(array * array)
    squares = lax.all_to_all(
        jnp.broadcast_to(local_squares, (n_all, 1, 128)), AXES, split_axis=0, concat_axis=1, tiled=True
    )
    grad_norm = jnp.sqrt(jnp.sum(squares[0, :, 0]) + jnp.sum(head_total * head_total))
    clip_factor = jnp.minimum(1.0, CLIP_NORM / (grad_norm + 1e-06))
    params = (wide_weights, square_weights, down_weights, embed_tables, all_biases, head_weights)
    firsts = (first_wide, first_square, first_down, first_tables, first_biases, first_head)
    seconds = (second_wide, second_square, second_down, second_tables, second_biases, second_head)
    gradients = owned_grads + (head_total,)
    results = [
        adamw_step(
            params[which],
            firsts[which],
            seconds[which],
            gradients[which] * clip_factor,
            LEARN_RATES[which],
        )
        for which in range(6)
    ]
    return (
        tuple(result[0] for result in results)
        + tuple(result[1] for result in results)
        + tuple(result[2] for result in results)
        + tuple(result[0].astype(BF16) for result in results)
        + (grad_norm, loss_sum, images)
    )


def solution(mesh):
    sizes = (mesh.shape["rows"], mesh.shape["band"])
    by_row, by_column, copied = P(AXES, None), P(None, AXES), P()
    params = (by_row, by_row, by_row, by_column, by_column, copied)
    patches = P("rows", "band", None)
    return jax.shard_map(
        functools.partial(body, sizes),
        mesh=mesh,
        in_specs=(patches, patches, P("rows"), P("rows", None), P("rows", None)) + 3 * params,
        out_specs=4 * params + (copied, copied, copied),
        check_vma=False,
    )
```

```python
import functools
import math

import jax
import jax.numpy as jnp
from jax import lax
from jax.experimental import pallas as pl
from jax.experimental.pallas import tpu as pltpu
from jax.sharding import PartitionSpec as P

D = 1152
FF = 4608
HEADS = 16
HEAD_DIM = D // HEADS
CLASSES = 1001
FREQ = 256
PATCH_IN = 16
GRID = 32
PATCHES = GRID * GRID
SLOTS = 4
SEGMENT = PATCHES // SLOTS
TIMESTEPS = 1000
STEP = 10

BETA_LOW = 0.0001
BETA_HIGH = 0.02
NORM_EPS = 1e-06
CLIP_NORM = 0.1
DECAY_FIRST = 0.9
DECAY_SECOND = 0.999
ADAM_EPS = 1e-08
LEARN_RATES = (0.1, 0.1, 0.05, 0.2, 0.3, 0.1)

GELU_ROOT = math.sqrt(2.0 / math.pi)
GELU_CUBE = 0.044715

AXES = ("rows", "band")
WINDOW = 256
SCALE = HEAD_DIM ** (-0.5)
NT = (((1,), (1,)), ((), ()))
TN = (((0,), (0,)), ((), ()))
NN = (((1,), (0,)), ((), ()))
BF16 = jnp.bfloat16
F32 = jnp.float32


def dot(left, right, dims):
    return lax.dot_general(left, right, dims, preferred_element_type=F32)


def head_window(head):
    start = jnp.minimum(head * HEAD_DIM // 128, (D - WINDOW) // 128) * 128
    return pl.multiple_of(start, 128), head * HEAD_DIM - start


def head_mask(rows, offset):
    lane = lax.broadcasted_iota(jnp.int32, (rows, WINDOW), 1)
    return (lane >= offset) & (lane < offset + HEAD_DIM)


def attend_head(head, apart, q_ref, k_ref, v_ref, out_ref, log_ref, q_block):
    q_len, k_len = q_ref.shape[0], k_ref.shape[0]
    start, offset = head_window(head)
    window = pl.ds(start, WINDOW)
    for at in range(0, q_len, q_block):
        rows = pl.ds(at, q_block)
        mask = head_mask(q_block, offset)
        query = jnp.where(mask, q_ref[rows, window], 0).astype(BF16)
        scores = jnp.concatenate(
            [
                dot(k_ref[pl.ds(k_at, SEGMENT), window], query, NT)
                + apart[pl.ds(k_at // SEGMENT, 1), rows]
                for k_at in range(0, k_len, SEGMENT)
            ],
            axis=0,
        )
        top = jnp.max(scores, axis=0, keepdims=True)
        weights = jnp.exp((scores - top) * SCALE)
        total = jnp.sum(weights, axis=0, keepdims=True)
        weights = (weights * (1.0 / total)).astype(BF16)
        mixed = dot(weights, v_ref[:, window], TN).astype(BF16)
        out_ref[rows, window] = jnp.where(mask, mixed, out_ref[rows, window])
        log_ref[pl.ds(head, 1), rows] = top * SCALE + jnp.log(total)


def attend_back_head(
    head, apart, q_ref, k_ref, v_ref, grad_ref, log_ref, dq_ref, dk_ref, dv_ref
):
    q_len, k_len = q_ref.shape[0], k_ref.shape[0]
    start, offset = head_window(head)
    window = pl.ds(start, WINDOW)
    mask = head_mask(q_len, offset)
    query = jnp.where(mask, q_ref[:, window], 0).astype(BF16)
    grad = jnp.where(mask, grad_ref[:, window], 0).astype(BF16)
    key = k_ref[:, window]
    log_total = log_ref[pl.ds(head, 1), :]
    probs = jnp.concatenate(
        [
            jnp.exp(
                dot(k_ref[pl.ds(k_at, SEGMENT), window], query, NT) * SCALE
                + (apart[pl.ds(k_at // SEGMENT, 1), :] - log_total)
            )
            for k_at in range(0, k_len, SEGMENT)
        ],
        axis=0,
    )
    both = probs * dot(v_ref[:, window], grad, NT)
    inner = jnp.sum(both, axis=0, keepdims=True)
    grad_scores = (both - probs * inner).astype(BF16)
    grad_value = dot(probs.astype(BF16), grad, NN)
    grad_key = dot(grad_scores, query, NN) * SCALE
    grad_query = (dot(grad_scores, key, TN) * SCALE).astype(BF16)
    dq_ref[:, window] = jnp.where(mask, grad_query, dq_ref[:, window])
    mask = head_mask(k_len, offset)
    dk_ref[:, window] = jnp.where(mask, grad_key.astype(BF16), dk_ref[:, window])
    dv_ref[:, window] = jnp.where(mask, grad_value.astype(BF16), dv_ref[:, window])


def whole_block(shape):
    return pl.BlockSpec(shape, lambda step: (0,) * len(shape))


def at_step(head, step, do):
    pl.when(head == step)(do)


MESH_ID = pl.DeviceIdType.MESH
BLOCK = 144
LINE = 4
SPLIT = (80, 64, 80)
ROWS_AXIS = 8
DEVICES = 32
OWN = D // DEVICES
PADDED = 48
ROUNDED = 40
PART = 384
OWNERS = 24
OWNER_OF = 7


class Place:
    def __init__(self):
        self.r, self.b = lax.axis_index("rows"), lax.axis_index("band")
        self.me = 4 * self.r + self.b
        self.z, self.x = self.r // 2, self.r % 2
        self.y, self.c = self.b // 2, self.b % 2
        self.other_x, self.other_b = 1 - self.x, self.b + 2 - 4 * self.y
        self.across_x = (self.r + 1 - 2 * self.x, self.b)
        self.across_y = (self.r, self.other_b)
        self.sibling = (self.r, self.b + 1 - 2 * self.c)
        self.right = (self.r + 2, self.b)
        self.left = (self.r - 2, self.b)

    def others(self, do):
        def step(i, carry):
            device = (self.me + i) % DEVICES
            do(device, (device // 4, device % 4))
            return carry

        lax.fori_loop(1, DEVICES, step, 0)

    def greet(self):
        barrier = pltpu.get_barrier_semaphore()
        self.others(
            lambda _, device: pl.semaphore_signal(
                barrier, inc=1, device_id=device, device_id_type=MESH_ID
            )
        )
        pl.semaphore_wait(barrier, DEVICES - 1)

    def each_source(self, do, steps):
        for step in steps:
            if step == 0:
                do(self.z)
            else:
                pl.when(self.z - step >= 0)(functools.partial(do, self.z - step))
                pl.when(self.z + step < LINE)(functools.partial(do, self.z + step))


def remote(source, target, send, receive, device):
    return pltpu.make_async_remote_copy(
        source, target, send, receive, device_id=device, device_id_type=MESH_ID
    )


class Spread:
    def __init__(self, at, place, own, rows, width, cut, dummy, sems):
        self.at, self.place, self.own = at, place, own
        self.rows, self.width, self.cut, self.dummy = rows, width, cut, dummy
        self.line_send, self.line_recv, self.sem = sems


    def block(self, r, b, start=0, size=None):
        return self.place(r, b, start, self.rows if size is None else size)

    def to_sibling(self, source, target):
        return remote(source, target, self.sem.at[3], self.sem.at[4], self.at.sibling)

    def to_x(self, source, target, slot):
        return remote(source, target, self.sem.at[1], self.sem.at[slot], self.at.across_x)

    def to_y(self, source, target, slot):
        return remote(source, target, self.sem.at[2], self.sem.at[slot], self.at.across_y)

    def line_copy(self, way, z, source=None):
        target = self.block(2 * z + self.at.x, self.at.b)
        return remote(
            target if source is None else source,
            target,
            self.line_send.at[way, z],
            self.line_recv.at[way, z],
            self.at.right if way == 0 else self.at.left,
        )

    def fan(self, z, source=None):
        target = self.block(2 * z + self.at.x, self.at.b)
        source = target if source is None else source
        self.to_x(source, target, 5 + z).start()
        self.to_y(source, target, 9 + z).start()
        self.to_sibling(source, target).start()

    def local(self):
        return pltpu.make_async_copy(self.own, self.block(self.at.r, self.at.b), self.sem.at[0])

    def open(self):
        at = self.at
        self.local().start()
        pl.when(at.z < LINE - 1)(lambda: self.line_copy(0, at.z, self.own).start())
        pl.when(at.z > 0)(lambda: self.line_copy(1, at.z, self.own).start())
        self.fan(at.z, self.own)

    def along_line(self, steps=(1, 2, 3)):
        at = self.at
        for step in steps:
            for way in (0, 1):
                z = at.z - step if way == 0 else at.z + step

                @pl.when(z >= 0 if way == 0 else z < LINE)
                def _(way=way, z=z):
                    copy = self.line_copy(way, z)
                    copy.wait_recv()
                    onward = at.z < LINE - 1 if way == 0 else at.z > 0
                    pl.when(onward)(lambda: copy.start())
                    self.fan(z)

    def around_square(self, steps=(0, 1, 2, 3)):
        at, cut = self.at, self.cut

        def do(z):
            ref = self.block(2 * z + at.other_x, at.b)
            self.to_x(ref, ref, 5 + z).wait_recv()
            part = self.block(2 * z + at.other_x, at.b, 0, cut)
            self.to_y(part, part, 17 + z).start()
            self.to_sibling(ref, ref).start()
            ref = self.block(2 * z + at.x, at.other_b)
            self.to_y(ref, ref, 9 + z).wait_recv()
            part = self.block(2 * z + at.x, at.other_b, cut, self.rows - cut)
            self.to_x(part, part, 13 + z).start()
            self.to_sibling(ref, ref).start()

        at.each_source(do, steps)

    def close_square(self, steps=(0, 1, 2, 3)):
        at, cut = self.at, self.cut

        def do(z):
            part = self.block(2 * z + at.other_x, at.other_b, 0, cut)
            self.to_y(part, part, 17 + z).wait_recv()
            part = self.block(2 * z + at.other_x, at.other_b, cut, self.rows - cut)
            self.to_x(part, part, 13 + z).wait_recv()
            ref = self.block(2 * z + at.other_x, at.other_b)
            self.to_sibling(ref, ref).start()

        at.each_source(do, steps)

    def counted(self, rows):
        if self.width >= 128:
            return self.dummy(rows, self.width)
        return self.dummy(rows * self.width // D, D)

    def arrive(self):
        self.local().wait()
        rows = self.counted(4 * LINE * self.rows)
        self.to_sibling(rows, rows).wait_recv()

    def finish(self):
        at, cut = self.at, self.cut
        pl.when(at.z < LINE - 1)(lambda: self.line_copy(0, at.z).wait_send())
        pl.when(at.z > 0)(lambda: self.line_copy(1, at.z).wait_send())
        for step in range(1, LINE):
            go = jnp.logical_and(at.z - step >= 0, at.z < LINE - 1)
            pl.when(go)(lambda: self.line_copy(0, at.z - step).wait_send())
            go = jnp.logical_and(at.z + step < LINE, at.z > 0)
            pl.when(go)(lambda: self.line_copy(1, at.z + step).wait_send())
        rows = self.counted(LINE * (2 * self.rows - cut))
        self.to_x(rows, rows, 5).wait_send()
        rows = self.counted(LINE * (self.rows + cut))
        self.to_y(rows, rows, 9).wait_send()
        rows = self.counted(4 * LINE * self.rows)
        self.to_sibling(rows, rows).wait_send()


def spread_sems(count):
    dma = pltpu.SemaphoreType.DMA
    return [dma((count, 2, LINE)), dma((count, 2, LINE)), dma((count, 21))]


def compact(target, pieces, first_row):
    for device in range(DEVICES):
        rows = pieces[device, first_row : first_row + PADDED, :].astype(F32)
        target[OWN * device : OWN * (device + 1), :] = rows[:OWN]


def loosen(target, rows):
    for device in range(DEVICES):
        own = rows[OWN * device : OWN * (device + 1), :]
        target[PADDED * device : PADDED * device + OWN, :] = own
        target[PADDED * device + OWN : PADDED * (device + 1), :] = jnp.zeros(
            (PADDED - OWN, rows.shape[1]), F32
        )


def gather_kernel(
    own,
    time_own,
    mods_own,
    features_own,
    labels_own,
    time_in,
    time_bias,
    classes,
    small_own,
    given_own,
    first,
    mods,
    condition_out,
    small_out,
    time_act_out,
    time_pre_out,
    features,
    labels,
    given,
    piece,
    pieces,
    time_weights,
    mods_weights,
    tall,
    loose,
    mods_part,
    given_send,
    given_recv,
    code_sems,
    mods_send,
    mods_recv,
    part_sems,
    line_send,
    line_recv,
    spread_sem,
):
    at = Place()
    at.greet()

    def rows_at(r, start, size):
        return pl.ds(pl.multiple_of(r * BLOCK + start, 16), size)

    def in_first(r, b, start, size):
        return first.at[b, rows_at(r, start, size)]

    def in_time(r, b, start, size):
        return time_weights.at[pl.ds(pl.multiple_of((4 * r + b) * PADDED + start, 16), size)]

    def in_pieces(r, b, start, size):
        return pieces.at[4 * r + b, pl.ds(start, size)]

    def spread(index, place, source, rows, width, cut):
        sems = line_send.at[index], line_recv.at[index], spread_sem.at[index]
        return Spread(at, place, source, rows, width, cut, bytes_of, sems)

    def bytes_of(rows, width):
        if rows <= D:
            return first.at[0, pl.ds(0, rows), pl.ds(0, width)]
        return first.at[:, pl.ds(0, rows // 4), pl.ds(0, width)]

    of_first = spread(0, in_first, own, BLOCK, D, SPLIT[0])
    of_time = spread(1, in_time, time_own, PADDED, D, 16)
    of_piece = spread(2, in_pieces, piece, BLOCK, 128, SPLIT[0])

    def code_copies(i):
        r = (at.r + i) % ROWS_AXIS
        mine = pl.ds(pl.multiple_of(at.r * 16, 16), 16)
        device = (r, at.b)
        return (
            remote(features_own, features.at[mine], code_sems.at[0, i], code_sems.at[1, i], device),
            remote(labels_own, labels.at[mine], code_sems.at[2, i], code_sems.at[3, i], device),
        )

    for i in range(1, ROWS_AXIS):
        for copy in code_copies(i):
            copy.start()
    mine = pl.ds(pl.multiple_of(at.r * 16, 16), 16)
    features[mine, :] = features_own[...]
    labels[mine, :] = labels_own[...]
    of_time.open()

    patches = given_own.shape[2]

    def given_copy(i):
        b = (at.b + i) % 4
        columns = pl.ds(pl.multiple_of(at.b * patches, 128), patches)
        return remote(
            given_own.at[b], given.at[:, columns], given_send.at[i], given_recv.at[i], (at.r, b)
        )

    for i in range(1, 4):
        given_copy(i).start()
    mine = pl.ds(pl.multiple_of(at.b * patches, 128), patches)
    given[:, mine] = given_own[at.b]

    padded_rows = pl.ds(pl.multiple_of(at.me * PADDED, 16), PADDED)

    def mods_copy(owner):
        columns = pl.ds(pl.multiple_of(owner * PART, 128), PART)
        return remote(
            mods_own.at[:, columns],
            mods_weights.at[padded_rows],
            mods_send.at[0],
            mods_recv.at[0],
            (owner % ROWS_AXIS, owner // ROWS_AXIS),
        )

    def to_owner(i, carry):
        owner = (OWNER_OF * at.me + i) % OWNERS
        own_it = jnp.logical_and(owner % ROWS_AXIS == at.r, owner // ROWS_AXIS == at.b)

        @pl.when(own_it)
        def _():
            columns = pl.ds(pl.multiple_of(owner * PART, 128), PART)
            pltpu.make_async_copy(
                mods_own.at[:, columns], mods_weights.at[padded_rows], mods_recv.at[0]
            ).start()

        pl.when(jnp.logical_not(own_it))(lambda: mods_copy(owner).start())
        return carry

    lax.fori_loop(0, OWNERS, to_owner, 0)
    owner = at.b * ROWS_AXIS + at.r
    owns = at.b < OWNERS // ROWS_AXIS

    for i in range(1, ROWS_AXIS):
        for copy in code_copies(i):
            copy.wait_recv()

    time_pre = dot(time_in[...], features[...], NT) + time_bias[...]
    time_pre_out[...] = time_pre
    piece[0:PADDED, :] = jax.nn.silu(time_pre).astype(BF16)
    lane = lax.broadcasted_iota(jnp.int32, (128, 128), 1)
    class_rows = jnp.zeros((PADDED, 128), F32)
    for k in range(classes.shape[1] // 128):
        hot = ((labels[...] & 1023) == lane + 128 * k).astype(F32).astype(BF16)
        class_rows = class_rows + dot(classes[:, 128 * k : 128 * (k + 1)], hot, NT)
    piece[PADDED : 2 * PADDED, :] = class_rows.astype(BF16)
    piece[2 * PADDED : 3 * PADDED, :] = small_own[...]
    of_piece.open()
    of_first.open()
    of_time.along_line()
    of_piece.along_line()
    of_time.around_square()
    of_piece.around_square()
    of_time.close_square()
    of_piece.close_square()
    of_first.along_line()
    of_time.arrive()
    of_piece.arrive()

    for device in range(DEVICES):
        rows = pl.ds(PADDED * device, PADDED)
        loose[rows, :] = pieces[device, 0:PADDED, :].astype(F32)
    time_act = jnp.transpose(loose[...]).astype(BF16)
    compact(tall, pieces, 0)
    time_act_out[...] = jnp.transpose(tall[...]).astype(BF16)
    compact(tall, pieces, 2 * PADDED)
    small = jnp.transpose(tall[...])
    small_out[...] = small
    compact(tall, pieces, PADDED)
    condition = dot(time_act, time_weights[...], NN) + small[2:3, :] + jnp.transpose(tall[...])
    condition_out[...] = condition

    def part_copy(device, place):
        chip = pl.ds(pl.multiple_of(device // 2 * 8, 8), 8)
        columns = pl.ds(pl.multiple_of(owner * PART, 128), PART)
        return remote(
            mods_part.at[chip], mods.at[:, columns], part_sems.at[0], part_sems.at[1], place
        )

    @pl.when(owns)
    def _():
        tall[...] = jnp.transpose(jax.nn.silu(condition))
        loosen(loose, tall)
        pltpu.make_async_copy(mods_weights, mods_weights, mods_recv.at[0]).wait()
        mods_part[...] = dot(loose[...].astype(BF16), mods_weights[...], TN)
        at.others(lambda device, place: part_copy(device, place).start())
        chip = pl.ds(pl.multiple_of(at.me // 2 * 8, 8), 8)
        columns = pl.ds(pl.multiple_of(owner * PART, 128), PART)
        pltpu.make_async_copy(mods_part.at[chip], mods.at[:, columns], part_sems.at[1]).start()

    of_first.around_square()
    of_first.close_square()
    of_first.arrive()
    pltpu.make_async_copy(mods, mods, part_sems.at[1]).wait()
    for i in range(1, ROWS_AXIS):
        for copy in code_copies(i):
            copy.wait_send()
    for i in range(1, 4):
        given_copy(i).wait()

    @pl.when(owns)
    def _():
        sent = time_weights.at[pl.ds(0, (OWNERS - 1) * PADDED // 3)]
        remote(sent, sent, mods_send.at[0], mods_recv.at[0], at.sibling).wait_send()

    @pl.when(jnp.logical_not(owns))
    def _():
        sent = time_weights.at[pl.ds(0, OWNERS * PADDED // 3)]
        remote(sent, sent, mods_send.at[0], mods_recv.at[0], at.sibling).wait_send()

    @pl.when(owns)
    def _():
        sent = first.at[0, pl.ds(0, (DEVICES - 1) * 16), pl.ds(0, PART)]
        remote(sent, sent, part_sems.at[0], part_sems.at[1], at.sibling).wait_send()

    for group in (of_piece, of_time, of_first):
        group.finish()


def gather_weights(*operands):
    dma = pltpu.SemaphoreType.DMA
    anywhere, inside = (
        pl.BlockSpec(memory_space=pl.ANY),
        pl.BlockSpec(memory_space=pltpu.VMEM),
    )
    return pl.pallas_call(
        gather_kernel,
        in_specs=[anywhere] * 3 + [inside] * 7,
        out_specs=[anywhere] + [inside] * 8,
        out_shape=[
            jax.ShapeDtypeStruct((4, D, D), BF16),
            jax.ShapeDtypeStruct((8, 8 * D), F32),
            jax.ShapeDtypeStruct((128, D), F32),
            jax.ShapeDtypeStruct((128, D), F32),
            jax.ShapeDtypeStruct((128, D), BF16),
            jax.ShapeDtypeStruct((PADDED, 128), F32),
            jax.ShapeDtypeStruct((128, FREQ), BF16),
            jax.ShapeDtypeStruct((128, 128), jnp.int32),
            jax.ShapeDtypeStruct((2 * PATCH_IN, PATCHES), F32),
        ],
        scratch_shapes=[
            pltpu.VMEM((BLOCK, 128), BF16),
            pltpu.VMEM((DEVICES, BLOCK, 128), BF16),
            pltpu.VMEM((DEVICES * PADDED, D), BF16),
            pltpu.VMEM((DEVICES * PADDED, PART), BF16),
            pltpu.VMEM((D, 128), F32),
            pltpu.VMEM((DEVICES * PADDED, 128), F32),
            pltpu.VMEM((128, PART), F32),
            dma((4,)),
            dma((4,)),
            dma((4, ROWS_AXIS)),
            dma((1,)),
            dma((1,)),
            dma((2,)),
            *spread_sems(3),
        ],
        compiler_params=pltpu.CompilerParams(
            collective_id=0, has_side_effects=True, vmem_limit_bytes=32 << 20
        ),
        name="gather_weights",
    )(*operands)


ORDER = (3, 0, 2, 1)


class Collect:
    def __init__(self, at, part, out, buffers, sems, cut):
        self.at, self.part, self.out, self.cut = at, part, out, cut
        self.own, self.got, self.near, self.far, self.line = buffers
        (
            self.own_sem,
            self.core_send,
            self.core_recv,
            self.near_send,
            self.near_recv,
            self.far_send,
            self.far_recv,
            self.line_send,
            self.line_recv,
        ) = sems
        self.other_y = 1 - at.y

    def start(self):
        at = self.at
        for z in ORDER:
            for y in (0, 1):
                for core in (0, 1):

                    def begin(keep, y=y, z=z, b=2 * y + core):
                        for source, first, rows in self.part(b, z):
                            self.move(y, z, pl.ds(first, rows), source, keep).start()

                    pl.when(at.c == core)(functools.partial(begin, True))
                    pl.when(at.c != core)(functools.partial(begin, False))

    def move(self, y, z, rows, source, keep):
        if keep:
            return pltpu.make_async_copy(source, self.own.at[y, rows], self.own_sem.at[y, z])
        return remote(
            source,
            self.got.at[y, rows],
            self.core_send.at[y, z],
            self.core_recv.at[y, z],
            self.at.sibling,
        )

    def whole_move(self, y, z, keep):
        rows = pl.ds(2 * z * BLOCK, 2 * BLOCK)
        return self.move(y, z, rows, self.got.at[y, rows], keep)

    def arrive(self, z):
        for y in (0, 1):
            self.whole_move(y, z, True).wait()
            self.whole_move(y, z, False).wait_recv()

    @staticmethod
    def rows_of(r, start, size):
        return pl.ds(pl.multiple_of(r * BLOCK + start, 16), size)

    @staticmethod
    def add(target, sources, size):
        def step(i, carry):
            total = None
            for ref, index, start in sources:
                tile = ref[index + (pl.ds(pl.multiple_of(start + 16 * i, 16), 16),)].astype(F32)
                total = tile if total is None else total + tile
            ref, index, start = target
            ref[index + (pl.ds(pl.multiple_of(start + 16 * i, 16), 16),)] = total.astype(ref.dtype)
            return carry

        lax.fori_loop(0, size // 16, step, 0)

    def near_copy(self, route, i):
        at, cut = self.at, self.cut
        if route == 0:
            source = self.own.at[self.other_y, self.rows_of(i, 0, cut)]
            target = self.near.at[i, pl.ds(0, cut)]
            device = at.across_y
        else:
            rows = self.rows_of(2 * (i // 2) + at.other_x, cut, BLOCK - cut)
            source = self.own.at[i % 2, rows]
            target = self.near.at[i, pl.ds(cut, BLOCK - cut)]
            device = at.across_x
        return remote(
            source, target, self.near_send.at[route], self.near_recv.at[route, i], device
        )

    def far_copy(self, route, z):
        at, cut = self.at, self.cut
        if route == 0:
            source = self.own.at[at.y, self.rows_of(2 * z + at.other_x, 0, cut)]
            target = self.far.at[z, pl.ds(0, cut)]
            device = at.across_x
        else:
            source = self.own.at[self.other_y, self.rows_of(2 * z + at.x, cut, BLOCK - cut)]
            target = self.far.at[z, pl.ds(cut, BLOCK - cut)]
            device = at.across_y
        return remote(source, target, self.far_send.at[route], self.far_recv.at[route, z], device)

    def near_stage(self, z):
        at, cut, own, got = self.at, self.cut, self.own, self.got
        self.arrive(z)

        def step(i, carry):
            for y, start, size, route in (
                (self.other_y, i * BLOCK, cut, 0),
                (i % 2, (2 * (i // 2) + at.other_x) * BLOCK + cut, BLOCK - cut, 1),
            ):
                self.add((own, (y,), start), [(own, (y,), start), (got, (y,), start)], size)
                self.near_copy(route, i).start()
            return carry

        lax.fori_loop(2 * z, 2 * z + 2, step, 0)

    def far_stage(self, z):
        at, cut, own, got = self.at, self.cut, self.own, self.got
        r, i = 2 * z + at.other_x, 2 * z + self.other_y
        for y, start, size, route, index, first in (
            (at.y, r * BLOCK, cut, 0, r, 0),
            (self.other_y, (2 * z + at.x) * BLOCK + cut, BLOCK - cut, 1, i, cut),
        ):
            self.near_copy(route, index).wait_recv()
            sources = [(own, (y,), start), (got, (y,), start), (self.near, (index,), first)]
            self.add((own, (y,), start), sources, size)
            self.far_copy(route, z).start()

    def line_copy(self, way, z):
        source = self.own.at[self.at.y, self.rows_of(2 * z + self.at.x, 0, BLOCK)]
        slot = z - 1 if way == 0 else z
        return remote(
            source,
            self.line.at[way, slot],
            self.line_send.at[way, slot],
            self.line_recv.at[way, slot],
            self.at.right if way == 0 else self.at.left,
        )

    def arrivals(self, z):
        self.near_copy(0, 2 * z + self.at.x).wait_recv()
        self.near_copy(1, 2 * z + self.at.y).wait_recv()
        self.far_copy(0, z).wait_recv()
        self.far_copy(1, z).wait_recv()

    def total(self, z, target, ways):
        at, cut = self.at, self.cut
        start = (2 * z + at.x) * BLOCK
        for route, begin, size in ((0, 0, cut), (1, cut, BLOCK - cut)):
            index = 2 * z + (at.x if route == 0 else at.y)
            sources = [
                (self.own, (at.y,), start + begin),
                (self.got, (at.y,), start + begin),
                (self.near, (index,), begin),
                (self.far, (z,), begin),
            ]
            for way in ways:
                sources.append((self.line, (way, z - 1 if way == 0 else z), begin))
            ref, place, base = target
            self.add((ref, place, base + begin), sources, size)

    def pass_on(self, way, z):
        at = self.at
        ahead = at.z > 0 if way == 0 else at.z < LINE - 1
        target = (self.own, (at.y,), (2 * z + at.x) * BLOCK)
        self.arrivals(z)

        @pl.when(ahead)
        def _():
            self.line_copy(way, z).wait_recv()
            self.total(z, target, (way,))

        pl.when(jnp.logical_not(ahead))(lambda: self.total(z, target, ()))
        self.line_copy(way, z).start()

    def line_stage(self, z):
        pl.when(self.at.z < z)(functools.partial(self.pass_on, 0, z))
        pl.when(self.at.z > z)(functools.partial(self.pass_on, 1, z))

    def last(self):
        at = self.at
        self.arrivals(at.z)
        for z in range(LINE):
            ways = ((0,) if z > 0 else ()) + ((1,) if z < LINE - 1 else ())

            @pl.when(at.z == z)
            def _(z=z, ways=ways):
                for way in ways:
                    self.line_copy(way, z).wait_recv()
                self.total(z, (self.out, (), 0), ways)

    def finish(self):
        at, cut = self.at, self.cut
        for y in (0, 1):
            for z in range(LINE):
                self.whole_move(y, z, False).wait_send()
        for route, size in ((0, cut), (1, BLOCK - cut)):
            rows = self.own.at[0, pl.ds(0, 2 * LINE * size)]
            sems = self.near_send.at[route], self.near_recv.at[route, 0]
            remote(rows, rows, *sems, at.sibling).wait_send()
            rows = self.own.at[0, pl.ds(0, LINE * size)]
            sems = self.far_send.at[route], self.far_recv.at[route, 0]
            remote(rows, rows, *sems, at.sibling).wait_send()
        for z in range(LINE):
            pl.when(at.z < z)(lambda: self.line_copy(0, z).wait_send())
            pl.when(at.z > z)(lambda: self.line_copy(1, z).wait_send())


class Share:
    def __init__(self, at, sums, shares, scratch):
        self.at, self.sums, self.shares = at, sums, shares
        self.stage, self.send, self.recv = scratch

    def copy(self, i):
        at = self.at
        b = (at.b + i) % 4
        target = self.shares.at[at.b]
        return remote(self.stage.at[b], target, self.send.at[i], self.recv.at[i], (at.r, b))

    def start(self):
        for j in range(4):
            self.stage[j, :OWN, :] = self.sums[OWN * j : OWN * (j + 1), :]
            self.stage[j, OWN:, :] = jnp.zeros((ROUNDED - OWN, D), F32)
        for i in range(1, 4):
            self.copy(i).start()
        self.shares[self.at.b] = self.stage[self.at.b]

    def finish(self):
        for i in range(1, 4):
            self.copy(i).wait()


def share_scratch():
    dma = pltpu.SemaphoreType.DMA
    return [pltpu.VMEM((4, ROUNDED, D), F32), dma((4,)), dma((4,))]


def collect_scratch():
    dma = pltpu.SemaphoreType.DMA
    return [
        pltpu.VMEM((2, D, D), BF16),
        pltpu.VMEM((2, D, D), BF16),
        pltpu.VMEM((2 * LINE, BLOCK, D), BF16),
        pltpu.VMEM((LINE, BLOCK, D), BF16),
        pltpu.VMEM((2, LINE - 1, BLOCK, D), BF16),
        dma((2, LINE)),
        dma((2, LINE)),
        dma((2, LINE)),
        dma((2,)),
        dma((2, 2 * LINE)),
        dma((2,)),
        dma((2, LINE)),
        dma((2, LINE - 1)),
        dma((2, LINE - 1)),
    ]


def scatter_kernel(
    triple,
    output,
    slots_own,
    mods_weights,
    condition,
    totals_own,
    out,
    slots,
    grad_condition,
    totals,
    quarters,
    slots_block,
    pieces,
    tall,
    totals_got,
    band_send,
    band_recv,
    totals_send,
    totals_recv,
    slot_line_send,
    slot_line_recv,
    slot_sem,
    piece_sems,
    sums,
    *rest,
):
    at = Place()
    at.greet()
    own = rest[3]
    share = Share(at, sums, out, rest[:3])
    of_first = Collect(
        at,
        lambda b, z: [
            (
                (output if b == 3 else triple.at[b]).at[pl.ds(2 * z * BLOCK, 2 * BLOCK)],
                2 * z * BLOCK,
                2 * BLOCK,
            )
        ],
        sums,
        rest[3:8],
        rest[8:],
        SPLIT[0],
    )

    def band_copy(i):
        b = (at.b + i) % 4
        columns = pl.ds(pl.multiple_of(b * 2 * D, 128), 2 * D)
        return remote(
            slots_own.at[:, columns],
            quarters.at[at.b],
            band_send.at[i],
            band_recv.at[i],
            (at.r, b),
        )

    def band_arrival(i):
        source = quarters.at[(at.b + 4 - i) % 4]
        return remote(source, source, band_send.at[i], band_recv.at[i], at.sibling)

    def in_slots(r, b, start, size):
        columns = pl.ds(pl.multiple_of(b * 2 * D + start, 128), size)
        return slots.at[pl.ds(pl.multiple_of(r * 16, 16), 16), columns]

    def sems(index):
        return slot_line_send.at[index], slot_line_recv.at[index], slot_sem.at[index]

    def bytes_of(rows, width):
        return own.at[0, pl.ds(0, rows), pl.ds(0, width)]

    of_slots = Spread(at, in_slots, slots_block, 2 * D, 16, D, bytes_of, sems(0))

    def piece_copy(place):
        mine = pieces.at[at.me]
        return remote(mine, mine, piece_sems.at[0], piece_sems.at[1], place)

    def share_slots():
        mine = pl.ds(pl.multiple_of(at.b * 2 * D, 128), 2 * D)
        total = slots_own[:, mine].astype(F32)
        for i in range(1, 4):
            band_arrival(i).wait_recv()
        for i in range(1, 4):
            total = total + quarters[(at.b + 4 - i) % 4].astype(F32)
        slots_block[...] = total.astype(BF16)
        of_slots.open()

    def condition_back():
        of_slots.arrive()
        grad = dot(mods_weights[...], slots[...], NT)
        sigmoid = 1.0 / (1.0 + jnp.exp(-condition[...]))
        grad = grad * (sigmoid * (1.0 + condition[...] * (1.0 - sigmoid)))
        pieces[at.me] = grad.astype(BF16)
        at.others(lambda _, place: piece_copy(place).start())

    def condition_arrives():
        others = pieces.at[pl.ds(0, DEVICES - 1)]
        remote(others, others, piece_sems.at[0], piece_sems.at[1], at.sibling).wait()
        compact(tall, pieces, 0)
        grad_condition[...] = jnp.transpose(tall[...]).astype(BF16)

    def near_line():
        return (at.r + 2 - 4 * (at.z % 2), at.b)

    def far_line():
        return (at.r + 4 - 8 * (at.z // 2), at.b)

    partners = (at.sibling, near_line(), far_line(), at.across_x, at.across_y)

    def totals_copy(step):
        return remote(
            totals_own if step == 0 else totals.at[step - 1],
            totals_got.at[step],
            totals_send.at[step],
            totals_recv.at[step],
            partners[step],
        )

    def totals_step(step):
        totals_copy(step).wait_recv()
        before = totals_own[...] if step == 0 else totals[step - 1]
        totals[step] = before + totals_got[step]
        if step + 1 < len(partners):
            totals_copy(step + 1).start()

    for i in range(1, 4):
        band_copy(i).start()
    totals_copy(0).start()
    of_first.start()
    share_slots()
    of_first.near_stage(3)
    totals_step(0)
    of_slots.along_line((1,))
    of_first.near_stage(0)
    of_slots.along_line((2,))
    of_slots.around_square((0,))
    of_first.far_stage(3)
    of_first.near_stage(2)
    of_slots.along_line((3,))
    of_slots.around_square((1,))
    of_first.far_stage(0)
    totals_step(1)
    of_first.near_stage(1)
    of_slots.around_square((2,))
    of_slots.close_square((0,))
    of_slots.around_square((3,))
    of_first.line_stage(3)
    of_slots.close_square((1,))
    totals_step(2)
    of_first.far_stage(2)
    of_slots.close_square((2, 3))
    of_first.line_stage(0)
    condition_back()
    of_first.far_stage(1)
    totals_step(3)
    of_first.line_stage(2)
    of_first.line_stage(1)
    of_first.last()
    share.start()
    condition_arrives()
    totals_step(4)
    of_first.finish()
    share.finish()
    for i in range(1, 4):
        band_copy(i).wait_send()
    for step in range(len(partners)):
        totals_copy(step).wait_send()
    of_slots.finish()


def scatter_sums(matrices, slots_own, mods_weights, condition, totals_own):
    dma = pltpu.SemaphoreType.DMA
    anywhere, inside = (
        pl.BlockSpec(memory_space=pl.ANY),
        pl.BlockSpec(memory_space=pltpu.VMEM),
    )
    steps = 5
    return pl.pallas_call(
        scatter_kernel,
        in_specs=[anywhere] * 2 + [inside] * 4,
        out_specs=[inside] * 4,
        out_shape=[
            jax.ShapeDtypeStruct((4, ROUNDED, D), F32),
            jax.ShapeDtypeStruct((128, 8 * D), BF16),
            jax.ShapeDtypeStruct((128, D), BF16),
            jax.ShapeDtypeStruct((steps, *totals_own.shape), F32),
        ],
        scratch_shapes=[
            pltpu.VMEM((4, 16, 2 * D), BF16),
            pltpu.VMEM((16, 2 * D), BF16),
            pltpu.VMEM((DEVICES, PADDED, 128), BF16),
            pltpu.VMEM((D, 128), F32),
            pltpu.VMEM((steps, *totals_own.shape), F32),
            dma((4,)),
            dma((4,)),
            dma((steps,)),
            dma((steps,)),
            *spread_sems(1),
            dma((2,)),
            pltpu.VMEM((BLOCK, D), F32),
            *share_scratch(),
            *collect_scratch(),
        ],
        compiler_params=pltpu.CompilerParams(
            collective_id=1, has_side_effects=True, vmem_limit_bytes=61 << 20
        ),
        name="scatter_sums",
    )(*matrices, slots_own, mods_weights, condition, totals_own)


def attend_kernel(apart, q_ref, k_ref, v_ref, *rest, travels):
    head = pl.program_id(0)
    if travels:
        up_own, out_ref, log_ref, up, line_send, line_recv, spread_sem = rest
        at = Place()

        def in_up(r, b, start, size):
            rows = pl.ds(pl.multiple_of(r * BLOCK + start, 16), size)
            return up.at[rows, pl.ds(pl.multiple_of(b * D, 128), D)]

        def bytes_of(rows, width):
            return up.at[pl.ds(0, rows // 4), :]

        sems = line_send.at[0], line_recv.at[0], spread_sem.at[0]
        of_up = Spread(at, in_up, up_own, BLOCK, D, SPLIT[1], bytes_of, sems)

        def begin():
            at.greet()
            of_up.open()

        at_step(head, 0, begin)
        for step in (1, 2, 3):
            at_step(head, 1 + 2 * step, lambda: of_up.along_line((step,)))
        for step in range(4):
            at_step(head, 4 + 2 * step, lambda: of_up.around_square((step,)))
            at_step(head, 8 + 2 * step, lambda: of_up.close_square((step,)))
    else:
        out_ref, log_ref = rest
    attend_head(head, apart, q_ref, k_ref, v_ref, out_ref, log_ref, min(512, q_ref.shape[0]))
    if travels:

        def end():
            of_up.arrive()
            of_up.finish()

        at_step(head, HEADS - 1, end)


def attend_back_kernel(apart, q_ref, k_ref, v_ref, grad_ref, log_ref, *rest, travels):
    head = pl.program_id(0)
    if travels:
        up_grad, grads, shares, sums, *rest = rest
        dq_ref, dk_ref, dv_ref = (grads.at[which] for which in range(3))
        at = Place()
        share = Share(at, sums, rest[3], rest[:3])

        def part(b, z):
            rows = pl.ds(2 * z * BLOCK, 2 * BLOCK)
            return [(up_grad.at[rows, pl.ds(b * D, D)], 2 * z * BLOCK, 2 * BLOCK)]

        of_up = Collect(at, part, sums, rest[4:9], rest[9:], SPLIT[1])

        def begin():
            at.greet()
            of_up.start()

        at_step(head, 0, begin)
        for step, z in ((2, 3), (3, 0), (6, 2), (8, 1)):
            at_step(head, step, lambda: of_up.near_stage(z))
        for step, z in ((6, 3), (8, 0), (11, 2), (13, 1)):
            at_step(head, step, lambda: of_up.far_stage(z))
        for step, z in ((10, 3), (12, 0), (14, 2)):
            at_step(head, step, lambda: of_up.line_stage(z))
    else:
        dq_ref, dk_ref, dv_ref = rest
    attend_back_head(
        head, apart, q_ref, k_ref, v_ref, grad_ref, log_ref, dq_ref, dk_ref, dv_ref
    )
    if travels:

        def end():
            of_up.line_stage(1)
            of_up.last()
            share.start()
            of_up.finish()
            share.finish()
            shares[...] = rest[3][...]

        at_step(head, HEADS - 1, end)


def one_of(array, which):
    if array.ndim == 2:
        return whole_block(array.shape)
    return pl.BlockSpec((None, *array.shape[1:]), lambda step: (which, 0, 0))


def attend(apart, queries, keys, values, up_own):
    q_len, k_len = queries.shape[-2], keys.shape[-2]
    travels = up_own is not None
    anywhere = pl.BlockSpec(memory_space=pl.ANY)
    return pl.pallas_call(
        functools.partial(attend_kernel, travels=travels),
        grid=(HEADS,),
        in_specs=[
            whole_block(apart.shape),
            one_of(queries, 0),
            one_of(keys, 1),
            one_of(values, 2),
        ]
        + [anywhere] * travels,
        out_specs=[whole_block((q_len, D)), whole_block((HEADS, q_len))] + [anywhere] * travels,
        out_shape=[
            jax.ShapeDtypeStruct((q_len, D), BF16),
            jax.ShapeDtypeStruct((HEADS, q_len), F32),
        ]
        + [jax.ShapeDtypeStruct((D, FF), BF16)] * travels,
        scratch_shapes=spread_sems(1) if travels else [],
        compiler_params=pltpu.CompilerParams(
            vmem_limit_bytes=56 << 20,
            **(dict(collective_id=2, has_side_effects=True) if travels else {}),
        ),
        name="attend_rows",
    )(apart, queries, keys, values, *((up_own,) if travels else ()))


def attend_back(apart, queries, keys, values, grads, log_total, up_grad):
    q_len, k_len = queries.shape[-2], keys.shape[-2]
    travels = up_grad is not None
    anywhere = pl.BlockSpec(memory_space=pl.ANY)
    return pl.pallas_call(
        functools.partial(attend_back_kernel, travels=travels),
        grid=(HEADS,),
        in_specs=[
            whole_block(apart.shape),
            one_of(queries, 0),
            one_of(keys, 1),
            one_of(values, 2),
            whole_block((q_len, D)),
            whole_block((HEADS, q_len)),
        ]
        + [anywhere] * travels,
        out_specs=[whole_block((3, q_len, D)), whole_block((4, ROUNDED, D))]
        if travels
        else [whole_block((q_len, D)), whole_block((k_len, D)), whole_block((k_len, D))],
        out_shape=[
            jax.ShapeDtypeStruct((3, q_len, D), BF16),
            jax.ShapeDtypeStruct((4, ROUNDED, D), F32),
        ]
        if travels
        else [
            jax.ShapeDtypeStruct((q_len, D), BF16),
            jax.ShapeDtypeStruct((k_len, D), BF16),
            jax.ShapeDtypeStruct((k_len, D), BF16),
        ],
        scratch_shapes=[
            pltpu.VMEM((BLOCK, D), F32),
            *share_scratch(),
            pltpu.VMEM((4, ROUNDED, D), F32),
            *collect_scratch(),
        ]
        if travels
        else [],
        compiler_params=pltpu.CompilerParams(
            vmem_limit_bytes=61 << 20,
            **(dict(collective_id=3, has_side_effects=True) if travels else {}),
        ),
        name="attend_rows_back",
    )(apart, queries, keys, values, grads, log_total, *((up_grad,) if travels else ()))


def project_kernel(normed, weights, bias, out):
    out[...] = (dot(normed[...], weights[...], NN) + bias[...]).astype(BF16)


def project(normed, weights, bias):
    rows, count = normed.shape[0], bias.shape[0]
    return pl.pallas_call(
        project_kernel,
        grid=(count,),
        in_specs=[
            whole_block((rows, D)),
            pl.BlockSpec((None, D, D), lambda i: (i, 0, 0)),
            pl.BlockSpec((None, 1, D), lambda i: (i, 0, 0)),
        ],
        out_specs=pl.BlockSpec((None, rows, D), lambda i: (i, 0, 0)),
        out_shape=jax.ShapeDtypeStruct((count, rows, D), BF16),
        compiler_params=pltpu.CompilerParams(vmem_limit_bytes=40 << 20),
        name="project",
    )(normed, weights, bias[:, None])


def project_back_kernel(normed, weights, grad, grad_normed, weight_grad, turned):
    part = dot(grad[...], weights[...], NT)

    @pl.when(pl.program_id(0) == 0)
    def _():
        turned[...] = jnp.transpose(normed[...])
        grad_normed[...] = part

    @pl.when(pl.program_id(0) > 0)
    def _():
        grad_normed[...] += part

    weight_grad[...] = dot(turned[...], grad[...], NN).astype(BF16)


def project_back(normed, weights, grads):
    count, rows = grads.shape[:2]
    return pl.pallas_call(
        project_back_kernel,
        grid=(count,),
        in_specs=[
            whole_block((rows, D)),
            pl.BlockSpec((None, D, D), lambda i: (i, 0, 0)),
            pl.BlockSpec((None, rows, D), lambda i: (i, 0, 0)),
        ],
        out_specs=[whole_block((rows, D)), pl.BlockSpec((None, D, D), lambda i: (i, 0, 0))],
        out_shape=[
            jax.ShapeDtypeStruct((rows, D), F32),
            jax.ShapeDtypeStruct((count, D, D), BF16),
        ],
        scratch_shapes=[pltpu.VMEM((D, rows), BF16)],
        compiler_params=pltpu.CompilerParams(vmem_limit_bytes=56 << 20),
        name="project_back",
    )(normed, weights, grads)


def outer_kernel(left, right, out):
    out[...] = dot(left[...], right[...], TN).astype(BF16)


def outer(left, right):
    rows, tile = left.shape[0], 768
    return pl.pallas_call(
        outer_kernel,
        grid=(left.shape[1] // tile,),
        in_specs=[pl.BlockSpec((rows, tile), lambda i: (0, i)), whole_block((rows, D))],
        out_specs=pl.BlockSpec((tile, D), lambda i: (i, 0)),
        out_shape=jax.ShapeDtypeStruct((left.shape[1], D), BF16),
        compiler_params=pltpu.CompilerParams(vmem_limit_bytes=40 << 20),
        name="outer",
    )(left, right)


def mlp_kernel(normed, up, bias, down, active, slope, branch):
    tile = pl.program_id(0)
    values = dot(normed[...], up[...], NN) + bias[...]
    square = values * values
    curve = jnp.tanh(GELU_ROOT * values * (1.0 + GELU_CUBE * square))
    half = 0.5 * (1.0 + curve)
    acting = (values * half).astype(BF16)
    active[...] = acting
    steep = values * (GELU_ROOT + 3.0 * GELU_ROOT * GELU_CUBE * square)
    slope[...] = (half + half * (1.0 - curve) * steep).astype(BF16)
    part = dot(acting, down[...], NN)

    @pl.when(tile == 0)
    def _():
        branch[...] = part

    @pl.when(tile > 0)
    def _():
        branch[...] += part


def mlp(normed, up, bias, down):
    rows, tile = normed.shape[0], 768
    by_tile = pl.BlockSpec((rows, tile), lambda i: (0, i))
    return pl.pallas_call(
        mlp_kernel,
        grid=(FF // tile,),
        in_specs=[
            whole_block((rows, D)),
            pl.BlockSpec((D, tile), lambda i: (0, i)),
            pl.BlockSpec((1, tile), lambda i: (0, i)),
            pl.BlockSpec((tile, D), lambda i: (i, 0)),
        ],
        out_specs=[by_tile, by_tile, whole_block((rows, D))],
        out_shape=[
            jax.ShapeDtypeStruct((rows, FF), BF16),
            jax.ShapeDtypeStruct((rows, FF), BF16),
            jax.ShapeDtypeStruct((rows, D), F32),
        ],
        compiler_params=pltpu.CompilerParams(vmem_limit_bytes=56 << 20),
        name="mlp",
    )(normed, up, bias, down)


def mlp_back_kernel(
    grad,
    normed,
    slope,
    down,
    up,
    down_grad,
    grad_normed,
    up_grad,
    bias_grad,
    down_sum,
    turned,
    *rest,
):
    tile = pl.program_id(0)
    at = Place()

    def part(b, z):
        return [
            (down_grad.at[pl.ds((4 * r + b) * BLOCK, BLOCK)], r * BLOCK, BLOCK)
            for r in (2 * z, 2 * z + 1)
        ]

    of_down = Collect(at, part, down_sum, rest[:5], rest[5:], SPLIT[0])

    def begin():
        at.greet()
        of_down.start()
        turned[...] = jnp.transpose(normed[...])
        grad_normed[...] = jnp.zeros_like(grad_normed)

    at_step(tile, 0, begin)
    for step, z in ((1, 3), (1, 0), (3, 2), (4, 1)):
        at_step(tile, step, lambda: of_down.near_stage(z))
    for step, z in ((3, 3), (4, 0), (6, 2), (7, 1)):
        at_step(tile, step, lambda: of_down.far_stage(z))
    for step, z in ((6, 3), (7, 0), (8, 2)):
        at_step(tile, step, lambda: of_down.line_stage(z))

    grad_active = dot(grad[...], down[...], NT)
    grad_up = (grad_active * slope[...].astype(F32)).astype(BF16)
    bias_grad[...] = jnp.sum(grad_up.astype(F32), axis=0, keepdims=True)
    up_grad[...] = dot(turned[...], grad_up, NN).astype(BF16)
    grad_normed[...] += dot(grad_up, up[...], NT)

    def end():
        of_down.line_stage(1)
        of_down.last()
        of_down.finish()

    at_step(tile, pl.num_programs(0) - 1, end)


def mlp_back(grad, normed, slope, down, up, down_grad):
    rows, tile = grad.shape[0], 512
    return pl.pallas_call(
        mlp_back_kernel,
        grid=(FF // tile,),
        in_specs=[
            whole_block((rows, D)),
            whole_block((rows, D)),
            pl.BlockSpec((rows, tile), lambda i: (0, i)),
            pl.BlockSpec((tile, D), lambda i: (i, 0)),
            pl.BlockSpec((D, tile), lambda i: (0, i)),
            pl.BlockSpec(memory_space=pl.ANY),
        ],
        out_specs=[
            whole_block((rows, D)),
            pl.BlockSpec((D, tile), lambda i: (0, i)),
            pl.BlockSpec((1, tile), lambda i: (0, i)),
            whole_block((BLOCK, D)),
        ],
        out_shape=[
            jax.ShapeDtypeStruct((rows, D), F32),
            jax.ShapeDtypeStruct((D, FF), BF16),
            jax.ShapeDtypeStruct((1, FF), F32),
            jax.ShapeDtypeStruct((BLOCK, D), F32),
        ],
        scratch_shapes=[pltpu.VMEM((D, rows), BF16)] + collect_scratch(),
        compiler_params=pltpu.CompilerParams(
            vmem_limit_bytes=61 << 20, collective_id=4, has_side_effects=True
        ),
        name="mlp_back",
    )(grad, normed, slope, down, up, down_grad)


def matmul(operand, weights):
    return jnp.einsum("...i,ij->...j", operand, weights, preferred_element_type=F32)


def matmul_back(gradient, weights):
    return jnp.einsum("...j,ij->...i", gradient, weights, preferred_element_type=F32)


def outer_sum(operand, gradient):
    return jnp.einsum(
        "ni,nj->ij",
        operand.reshape(-1, operand.shape[-1]),
        gradient.reshape(-1, gradient.shape[-1]),
        preferred_element_type=F32,
    )


def column_sum(gradient):
    return jnp.sum(gradient.reshape(-1, gradient.shape[-1]), axis=0, dtype=F32)


def silu_back(values, gradient):
    return jax.vjp(jax.nn.silu, values)[1](gradient)[0]


def plan(time_steps):
    steps_all = jnp.arange(TIMESTEPS, dtype=jnp.int32)
    betas = BETA_LOW + (BETA_HIGH - BETA_LOW) * steps_all.astype(F32) / (TIMESTEPS - 1)
    cumulate = jnp.cumsum(jnp.log1p(-betas))
    pick_now = (time_steps[..., None] == steps_all).astype(F32)
    pick_prev = (time_steps[..., None] - 1 == steps_all).astype(F32)
    return jnp.stack(
        [
            jnp.sum(pick_now * betas, axis=-1),
            jnp.sum(pick_now * cumulate, axis=-1),
            jnp.sum(pick_prev * cumulate, axis=-1),
        ],
        axis=-1,
    )


def time_features(time_steps):
    half_width = FREQ // 2
    frequency = jnp.exp(-math.log(10000.0) * jnp.arange(half_width).astype(F32) / half_width)
    angles = time_steps.astype(F32)[..., None] * frequency
    return jnp.concatenate([jnp.cos(angles), jnp.sin(angles)], axis=-1)


def positions(four_way):
    quarter = D // 4
    omegas = jnp.exp(-math.log(10000.0) * jnp.arange(quarter).astype(F32) / quarter)
    angles = jnp.arange(GRID).astype(F32)[:, None] * omegas
    table = jnp.concatenate([jnp.sin(angles), jnp.cos(angles)], axis=-1)

    def grid(side):
        shape = (PATCHES // side**2, side, side, D // 2)
        down = jnp.broadcast_to(table[None, :side, None], shape)
        across = jnp.broadcast_to(table[None, None, :side], shape)
        return jnp.concatenate([down, across], axis=-1).reshape(SLOTS, SEGMENT, D)

    return jnp.where(four_way, grid(GRID // 2), grid(GRID))


def layer_norm(values):
    centered = values - jnp.mean(values, axis=-1, keepdims=True)
    return centered * lax.rsqrt(jnp.mean(centered * centered, axis=-1, keepdims=True) + NORM_EPS)


def modulate(values, shift, scaling):
    return layer_norm(values) * (1.0 + scaling) + shift


def patch_loss(output, target_noise, patch_sched):
    beta = patch_sched[..., 0:1]
    log_now = patch_sched[..., 1:2]
    log_prev = patch_sched[..., 2:3]
    error = output[..., :PATCH_IN] - target_noise
    log_beta = jnp.log(beta)
    keep_now = -jnp.expm1(log_now)
    log_post = log_beta + jnp.log(-jnp.expm1(log_prev)) - jnp.log(keep_now)
    coefficient = beta * lax.rsqrt(keep_now * (1.0 - beta))
    fraction = 0.5 * (output[..., PATCH_IN:] + 1.0)
    log_model = fraction * log_beta + (1.0 - fraction) * log_post
    diverge = 0.5 * (
        -1.0
        + log_model
        - log_post
        + jnp.exp(log_post - log_model)
        + (coefficient * error) ** 2 * jnp.exp(-log_model)
    )
    return jnp.mean(error * error, axis=-1) + jnp.mean(diverge, axis=-1) / math.log(2.0)


def adamw_step(weight, first_old, second_old, gradient, step_rate):
    first_new = DECAY_FIRST * first_old + (1.0 - DECAY_FIRST) * gradient
    second_new = DECAY_SECOND * second_old + (1.0 - DECAY_SECOND) * gradient * gradient
    first_hat = first_new / (1.0 - DECAY_FIRST**STEP)
    second_hat = second_new / (1.0 - DECAY_SECOND**STEP)
    return (
        weight - step_rate * first_hat / (jnp.sqrt(second_hat) + ADAM_EPS),
        first_new,
        second_new,
    )


def body(
    sizes,
    latents,
    gauss_noise,
    image_counts,
    timesteps,
    labels,
    wide_weights,
    square_weights,
    down_weights,
    embed_tables,
    all_biases,
    head_weights,
    first_wide,
    first_square,
    first_down,
    first_tables,
    first_biases,
    first_head,
    second_wide,
    second_square,
    second_down,
    second_tables,
    second_biases,
    second_head,
):
    n_rows, n_band = sizes
    n_all = n_rows * n_band
    rows_here, band_len, _ = latents.shape
    share = n_band // rows_here
    part_len = PATCHES // share
    at_row, at_band = lax.axis_index("rows"), lax.axis_index("band")
    own_row = at_band // share
    part_start = (at_band % share) * part_len
    n_slots = n_rows * rows_here * SLOTS
    groups = [[row * share + i for i in range(share)] for row in range(rows_here)]

    def in_row_gather(array):
        if share == 1:
            return array
        return lax.all_gather(array, "band", axis=0, tiled=True, axis_index_groups=groups)

    def in_row_scatter(array):
        if share == 1:
            return array
        return lax.psum_scatter(
            array, "band", scatter_dimension=0, tiled=True, axis_index_groups=groups
        )

    def in_row_sum(array):
        if share == 1:
            return array
        return lax.psum(array, "band", axis_index_groups=groups)

    tuned = sizes == (ROWS_AXIS, DEVICES // ROWS_AXIS)
    n_seg = part_len // SEGMENT
    given = jnp.concatenate([latents, gauss_noise], axis=-1)
    count = lax.dynamic_slice_in_dim(image_counts, own_row, 1)[0]
    four_way = count == SLOTS
    seg_first = part_start // SEGMENT + jnp.arange(n_seg)
    seg_slot = jnp.where(four_way, seg_first, 0)
    seg_hot = (seg_slot[:, None] == jnp.arange(SLOTS)).astype(F32)

    def by_segment(per_slot):
        return jnp.sum(seg_hot[:, :, None] * per_slot[None], axis=1)[:, None]

    wide_low = wide_weights.astype(BF16)
    square_low = square_weights.astype(BF16)
    down_low = down_weights.astype(BF16)
    tables_low = embed_tables.astype(BF16)
    biases_low = all_biases.astype(BF16)
    mods_low = wide_low[:, 3 * D + FF :]
    time_out_low = square_low[:, D:]
    first_group = jnp.concatenate([wide_low[:, : 3 * D], square_low[:, :D]], axis=1)
    up_group = wide_low[:, 3 * D : 3 * D + FF]
    head_low = head_weights.astype(BF16)
    head_matrix = head_low[:D]
    small_rows = jnp.concatenate([biases_low, tables_low[FREQ : FREQ + PATCH_IN]], axis=0)
    device = at_row * n_band + at_band
    if tuned:
        padded = lambda array: jnp.pad(array, ((0, PADDED - OWN), (0, 0)))
        quarters = [first_group.reshape(-1, 4, D), up_group.reshape(-1, 4, D)]
        quarters = lax.all_to_all(
            jnp.concatenate(quarters, axis=2), "band", split_axis=1, concat_axis=0, tiled=True
        )[:, 0]
        own_times = timesteps.reshape(-1)
        codes = (labels + 1024 * image_counts[:, None]).reshape(-1, 1)
        own_codes = jnp.broadcast_to(codes, (rows_here * SLOTS, 128))
        class_columns = jnp.pad(tables_low[FREQ + PATCH_IN :].T, ((0, 0), (0, 1024 - CLASSES)))
        (
            first_all,
            mods,
            condition_all,
            small_all,
            time_act_all,
            time_pre,
            frequency,
            codes,
            given,
        ) = gather_weights(
            quarters[:, :D],
            padded(time_out_low),
            padded(mods_low),
            time_features(own_times).astype(BF16),
            own_codes,
            padded(tables_low[:FREQ].T),
            jnp.broadcast_to(padded(biases_low[1][:, None].astype(F32)), (PADDED, 128)),
            padded(class_columns),
            jnp.pad(small_rows.T, ((0, PADDED - OWN), (0, 128 - small_rows.shape[0]))),
            given.transpose(0, 2, 1),
        )
        given = given.T
        up_own = quarters[:, D:]
        down_own, codes = lax.optimization_barrier((down_low, codes))
        down_all = lax.all_gather(down_own, AXES, axis=0, tiled=True)
        weight_o = first_all[3]
        biases = small_all[: all_biases.shape[0]]
        patch_in = small_all[all_biases.shape[0] :][:PATCH_IN].astype(BF16)
        mods = lax.dynamic_slice_in_dim(mods, (at_band % 2) * SLOTS, SLOTS, 0)
        own_columns = lambda array: lax.dynamic_slice_in_dim(array, device * OWN, OWN, 1)
        condition = own_columns(condition_all)
        time_act = own_columns(time_act_all)
        time_pre = time_pre[:OWN].T
        labels_all = codes[:, 0] & 1023
        images = (jnp.sum(codes[:, 0] >> 10) // SLOTS).astype(F32)
        cond_act = jax.nn.silu(condition).astype(BF16)
    else:
        given = lax.all_gather(given, "band", axis=1, tiled=True)
        given = lax.dynamic_slice_in_dim(given, own_row, 1, 0)[0]
        given = lax.dynamic_slice_in_dim(given, part_start, part_len, 0)
        codes = jnp.concatenate([timesteps, labels, image_counts[:, None]], axis=1)
        codes = lax.all_gather(codes, "rows", axis=0, tiled=True)
        labels_all = codes[:, SLOTS : 2 * SLOTS].reshape(n_slots)
        images = jnp.sum(codes[:, 2 * SLOTS]).astype(F32)
        frequency = time_features(codes[:, :SLOTS].reshape(n_slots)).astype(BF16)
        first_all = lax.all_gather(first_group, AXES, axis=0, tiled=True)
        up_all = lax.all_gather(up_group, AXES, axis=0, tiled=True)
        down_all = lax.all_gather(down_low, AXES, axis=0, tiled=True)
        weight_q, weight_k, weight_v, weight_o = jnp.split(first_all, 4, axis=1)
        small_all = lax.all_gather(small_rows, AXES, axis=1, tiled=True)
        biases = small_all[: all_biases.shape[0]].astype(F32)
        patch_in = small_all[all_biases.shape[0] :]
        own_biases = biases_low.astype(F32)
        time_pre = matmul(frequency, tables_low[:FREQ]) + own_biases[1]
        time_act = jax.nn.silu(time_pre).astype(BF16)
        class_rows = tables_low[FREQ + PATCH_IN :]
        class_part = class_rows[labels_all].astype(F32)
        time_out_columns = lax.all_to_all(
            time_out_low, AXES, split_axis=1, concat_axis=0, tiled=True
        )
        time_act_all = lax.all_gather(time_act, AXES, axis=1, tiled=True)
        condition = matmul(time_act_all, time_out_columns) + own_biases[2] + class_part
        cond_act = jax.nn.silu(condition).astype(BF16)
        mods_columns = lax.all_to_all(mods_low, AXES, split_axis=1, concat_axis=0, tiled=True)
        cond_act_all = lax.all_gather(cond_act, AXES, axis=1, tiled=True)
        mods_part = matmul(cond_act_all, mods_columns)
        mods_part = mods_part.reshape(n_rows * rows_here, SLOTS, -1)
        if share > 1:
            mods_part = jnp.repeat(mods_part, share, axis=0)
        mods = lax.all_to_all(mods_part, AXES, split_axis=0, concat_axis=2, tiled=True)[0]
    label_hot = (labels_all[:, None] == jnp.arange(CLASSES, dtype=jnp.int32)).astype(BF16)
    mods_bias = jnp.concatenate([biases[3:9].reshape(-1), biases[17:19].reshape(-1)])
    seg_mods = by_segment(mods + mods_bias)
    (
        shift_one,
        scale_one,
        gate_one,
        shift_two,
        scale_two,
        gate_two,
        final_shift,
        final_scale,
    ) = jnp.split(seg_mods, 8, axis=-1)

    given = given.reshape(n_seg, SEGMENT, 2 * PATCH_IN)
    row_latents, row_noise = given[..., :PATCH_IN], given[..., PATCH_IN:]
    own_times = lax.dynamic_slice_in_dim(timesteps, own_row, 1, 0)[0]
    patch_sched = by_segment(plan(own_times))
    log_now = patch_sched[..., 1:2]
    noisy = (
        jnp.exp(0.5 * log_now) * row_latents + jnp.sqrt(-jnp.expm1(log_now)) * row_noise
    ).astype(BF16)
    position = lax.dynamic_slice_in_dim(positions(four_way), part_start // SEGMENT, n_seg, 0)
    hidden_zero = matmul(noisy, patch_in) + biases[0] + position
    normed_one = modulate(hidden_zero, shift_one, scale_one).astype(BF16)
    flat = lambda array: array.reshape(part_len, array.shape[-1])
    deep = lambda array: array.reshape(n_seg, SEGMENT, array.shape[-1])
    if tuned:
        query_bias = jnp.stack([biases[9], jnp.zeros_like(biases[9]), biases[10]])
        queries = keys = values = project(flat(normed_one), first_all, query_bias)
    else:
        queries = flat(matmul(normed_one, weight_q) + biases[9]).astype(BF16)
        keys = flat(matmul(normed_one, weight_k)).astype(BF16)
        values = flat(matmul(normed_one, weight_v) + biases[10]).astype(BF16)
        keys, values = in_row_gather(keys), in_row_gather(values)
    key_seg = jnp.where(four_way, jnp.arange(SLOTS), 0)
    apart = jnp.where(key_seg[:, None] == jnp.repeat(seg_slot, SEGMENT), 0.0, -1e30).astype(F32)
    if tuned:
        attended, log_total, up_all = attend(apart, queries, keys, values, up_own)
    else:
        attended, log_total = attend(apart, queries, keys, values, None)
    attended = deep(attended)
    branch_one = matmul(attended, weight_o) + biases[11]
    hidden_one = hidden_zero + gate_one * branch_one
    normed_two = modulate(hidden_one, shift_two, scale_two).astype(BF16)
    up_bias = biases[12:16].reshape(-1)
    if tuned:
        active, slope, branch_two = mlp(flat(normed_two), up_all, up_bias[None], down_all)
        active, branch_two = deep(active), deep(branch_two) + biases[16]
    else:
        upward = matmul(normed_two, up_all) + up_bias
        active = jax.nn.gelu(upward, approximate=True).astype(BF16)
        branch_two = matmul(active, down_all) + biases[16]
    hidden_two = hidden_one + gate_two * branch_two
    normed_out = modulate(hidden_two, final_shift, final_scale).astype(BF16)
    output = matmul(normed_out, head_matrix) + head_low[D].astype(F32)
    patch_share = jnp.where(four_way, 1.0 / SEGMENT, 1.0 / PATCHES)
    losses, loss_back = jax.vjp(lambda at: patch_loss(at, row_noise, patch_sched), output)
    loss_local = jnp.sum(patch_share * losses)

    grad_out = loss_back(jnp.broadcast_to(patch_share / images, losses.shape))[0].astype(BF16)
    grad_two, grad_fshift, grad_fscale = jax.vjp(modulate, hidden_two, final_shift, final_scale)[1](
        matmul_back(grad_out, head_matrix)
    )
    seg_sum = lambda array: jnp.sum(array, axis=1, keepdims=True)
    grad_gate_two = seg_sum(grad_two * branch_two)
    grad_branch_two = (gate_two * grad_two).astype(BF16)
    if tuned:
        down_grad = outer(flat(active), flat(grad_branch_two))
    else:
        down_grad = outer_sum(active, grad_branch_two)
    if tuned:
        grad_normed_two, up_grad, up_bias_grad, down_sum = mlp_back(
            flat(grad_branch_two),
            flat(normed_two),
            slope,
            down_all,
            up_all,
            down_grad,
        )
        grad_normed_two, up_bias_grad = deep(grad_normed_two), up_bias_grad[0]
    else:
        grad_active = matmul_back(grad_branch_two, down_all)
        grad_upward = jax.vjp(lambda at: jax.nn.gelu(at, approximate=True), upward)[1](
            grad_active
        )[0].astype(BF16)
        up_grad = outer_sum(normed_two, grad_upward)
        up_bias_grad = column_sum(grad_upward)
        grad_normed_two = matmul_back(grad_upward, up_all)
    grad_one_part, grad_shift_two, grad_scale_two = jax.vjp(
        modulate, hidden_one, shift_two, scale_two
    )[1](grad_normed_two)
    grad_one = grad_two + grad_one_part
    grad_gate_one = seg_sum(grad_one * branch_one)
    grad_branch_one = (gate_one * grad_one).astype(BF16)
    output_grad = outer_sum(attended, grad_branch_one)
    grad_attended = flat(matmul_back(grad_branch_one, weight_o).astype(BF16))
    if tuned:
        triple, up_sum = attend_back(
            apart, queries, keys, values, grad_attended, log_total, up_grad
        )
        grad_normed, triple_grad = project_back(flat(normed_one), first_all, triple)
        grad_query, _, grad_value = triple
        grad_normed = deep(grad_normed)
    else:
        grad_query, grad_key, grad_value = attend_back(
            apart, queries, keys, values, grad_attended, log_total, None
        )
        grad_key, grad_value = in_row_scatter(grad_key), in_row_scatter(grad_value)
        q_grad = outer_sum(normed_one, grad_query)
        k_grad = outer_sum(normed_one, grad_key)
        v_grad = outer_sum(normed_one, grad_value)
        grad_normed = deep(
            matmul_back(grad_query, weight_q)
            + matmul_back(grad_key, weight_k)
            + matmul_back(grad_value, weight_v)
        )
    grad_zero_part, grad_shift_one, grad_scale_one = jax.vjp(
        modulate, hidden_zero, shift_one, scale_one
    )[1](grad_normed)
    grad_zero = (grad_one + grad_zero_part).astype(BF16)
    patch_grad = outer_sum(noisy, grad_zero)

    seg_grads = jnp.concatenate(
        [
            grad_shift_one,
            grad_scale_one,
            grad_gate_one,
            grad_shift_two,
            grad_scale_two,
            grad_gate_two,
            grad_fshift,
            grad_fscale,
        ],
        axis=-1,
    )
    slot_grads = in_row_sum(jnp.sum(seg_hot[:, :, None] * seg_grads, axis=0)).astype(BF16)
    last_row = jnp.concatenate([column_sum(grad_out), loss_local[None]])
    totals = jnp.concatenate(
        [
            column_sum(grad_zero)[None],
            column_sum(grad_query)[None],
            column_sum(grad_value)[None],
            column_sum(grad_branch_one)[None],
            up_bias_grad.reshape(FF // D, D),
            column_sum(grad_branch_two)[None],
            patch_grad,
            outer_sum(grad_out, normed_out),
            jnp.pad(last_row, (0, D - last_row.shape[0]))[None],
        ],
        axis=0,
    )
    if tuned:
        slots_own = jnp.where(
            (jnp.arange(4 * SLOTS) // SLOTS == at_band)[:, None], jnp.tile(slot_grads, (4, 1)), 0
        ).astype(BF16)
        down_grad = down_sum
        sums, slot_grads, grad_condition_all, totals = scatter_sums(
            (triple_grad, output_grad.astype(BF16)),
            slots_own,
            padded(mods_low),
            padded(condition.T),
            jnp.pad(totals, ((0, -totals.shape[0] % 8), (0, 0))),
        )
        totals = totals[-1]
        first_grad, up_grad = (
            shares[:, :OWN].transpose(1, 0, 2).reshape(OWN, 4 * D) for shares in (sums, up_sum)
        )
        local_squares = sum(jnp.sum(array * array) for array in (first_grad, up_grad, down_grad))
        grad_condition = own_columns(grad_condition_all)
    else:
        slot_grads = lax.all_gather(slot_grads, AXES, axis=0, tiled=True)
        if share > 1:
            slot_grads = slot_grads.reshape(-1, share, SLOTS, 8 * D)[:, 0].reshape(n_slots, 8 * D)
        grad_condition = silu_back(condition, matmul_back(slot_grads, mods_low)).astype(BF16)
        grad_condition_all = lax.all_gather(grad_condition, AXES, axis=1, tiled=True)

        def scatter(array):
            return lax.psum_scatter(array, AXES, scatter_dimension=0, tiled=True)

        first_grad = scatter(jnp.concatenate([q_grad, k_grad, v_grad, output_grad], axis=1))
        up_grad = scatter(up_grad)
        down_grad = scatter(down_grad)
        local_squares = sum(jnp.sum(array * array) for array in (first_grad, up_grad, down_grad))
        totals = lax.psum(totals, AXES)
    mods_grad = outer_sum(cond_act, slot_grads)
    mods_bias_grad = column_sum(slot_grads).reshape(8, n_all, -1)
    time_out_grad = outer_sum(time_act, grad_condition_all)
    class_grad = outer_sum(label_hot, grad_condition)
    grad_time_pre = silu_back(time_pre, matmul_back(grad_condition_all, time_out_low)).astype(BF16)
    time_in_grad = outer_sum(frequency, grad_time_pre)
    n_sums = 9 + PATCH_IN
    own_width = D // n_all
    row_grads = lax.dynamic_slice_in_dim(totals[:n_sums], device * own_width, own_width, 1)
    head_total = jnp.concatenate(
        [totals[n_sums : n_sums + 32].T, totals[n_sums + 32, :32][None]], axis=0
    )
    loss_sum = totals[n_sums + 32, 32]
    own_mods_bias = lax.dynamic_index_in_dim(mods_bias_grad, device, 1, keepdims=False)
    grad_wide = jnp.concatenate([first_grad[:, : 3 * D], up_grad, mods_grad], axis=1)
    grad_square = jnp.concatenate([first_grad[:, 3 * D :], time_out_grad], axis=1)
    grad_tables = jnp.concatenate([time_in_grad, row_grads[9:], class_grad], axis=0)
    grad_biases = jnp.concatenate(
        [
            row_grads[:1],
            column_sum(grad_time_pre)[None],
            column_sum(grad_condition)[None],
            own_mods_bias[:6],
            row_grads[1:9],
            own_mods_bias[6:],
        ],
        axis=0,
    )
    owned_grads = (grad_wide, grad_square, down_grad, grad_tables, grad_biases)
    for array in (mods_grad, time_out_grad, grad_tables, grad_biases):
        local_squares = local_squares + jnp.sum(array * array)
    squares = lax.all_to_all(
        jnp.broadcast_to(local_squares, (n_all, 1, 128)), AXES, split_axis=0, concat_axis=1, tiled=True
    )
    grad_norm = jnp.sqrt(jnp.sum(squares[0, :, 0]) + jnp.sum(head_total * head_total))
    clip_factor = jnp.minimum(1.0, CLIP_NORM / (grad_norm + 1e-06))
    params = (wide_weights, square_weights, down_weights, embed_tables, all_biases, head_weights)
    firsts = (first_wide, first_square, first_down, first_tables, first_biases, first_head)
    seconds = (second_wide, second_square, second_down, second_tables, second_biases, second_head)
    gradients = owned_grads + (head_total,)
    results = [
        adamw_step(
            params[which],
            firsts[which],
            seconds[which],
            gradients[which] * clip_factor,
            LEARN_RATES[which],
        )
        for which in range(6)
    ]
    return (
        tuple(result[0] for result in results)
        + tuple(result[1] for result in results)
        + tuple(result[2] for result in results)
        + tuple(result[0].astype(BF16) for result in results)
        + (grad_norm, loss_sum, images)
    )


def solution(mesh):
    sizes = (mesh.shape["rows"], mesh.shape["band"])
    by_row, by_column, copied = P(AXES, None), P(None, AXES), P()
    params = (by_row, by_row, by_row, by_column, by_column, copied)
    patches = P("rows", "band", None)
    return jax.shard_map(
        functools.partial(body, sizes),
        mesh=mesh,
        in_specs=(patches, patches, P("rows"), P("rows", None), P("rows", None)) + 3 * params,
        out_specs=4 * params + (copied, copied, copied),
        check_vma=False,
    )
```
